32 devices in a mesh: dp: 16 (over z, y, core), mp: 2 (over x).
Axes of the slice: x: 2, y: 2, z: 4, core: 2. Of those that a mesh axis runs over, the one named last changes fastest.
Arguments:
- inputs: bfloat16 [65536, 1024], P(('dp', 'mp')), may hold values from -6 to 6
- skip_in: bfloat16 [65536, 1024], P(('dp', 'mp')), may hold values from -6 to 6
- cotangent: bfloat16 [65536, 1024], P(('dp', 'mp')), may hold values from -6 to 6
- lengths: int32 [16, 8], P('dp'), may hold values from 1 to 3840, as said below
- w_concat: bfloat16 [2048, 1024], replicated, may hold values from -0.125 to 0.125
- b_concat: float32 [1024], replicated, may hold values from -2 to 2
- gain_attn: float32 [1024], replicated, may hold values from 0.5 to 1.5
- w_query: bfloat16 [1024, 1024], P(None, 'mp'), may hold values from -0.1875 to 0.1875
- w_key: bfloat16 [1024, 1024], P(None, 'mp'), may hold values from -0.1875 to 0.1875
- w_value: bfloat16 [1024, 1024], P(None, 'mp'), may hold values from -0.1875 to 0.1875
- w_out: bfloat16 [1024, 1024], P('mp'), may hold values from -4 to 4
- b_out: float32 [1024], replicated, may hold values from -2 to 2
- gain_ffn: float32 [1024], replicated, may hold values from 0.5 to 1.5
- w_up: bfloat16 [1024, 4096], P(None, 'mp'), may hold values from -0.1875 to 0.1875
- b_up: bfloat16 [4096], P('mp'), may hold values from -3 to 3
- w_down: bfloat16 [4096, 1024], P('mp'), may hold values from -0.09375 to 0.09375
- b_down: float32 [1024], replicated, may hold values from -2 to 2
Outputs:
- output: float32 [65536, 1024], P(('dp', 'mp'))
- grad_inputs: float32 [65536, 1024], P(('dp', 'mp'))
- grad_skip: float32 [65536, 1024], P(('dp', 'mp'))
- grad_w_concat: float32 [2048, 1024], replicated
- grad_b_concat: float32 [1024], replicated
- grad_gain_attn: float32 [1024], replicated
- grad_w_query: float32 [1024, 1024], P(None, 'mp')
- grad_w_key: float32 [1024, 1024], P(None, 'mp')
- grad_w_value: float32 [1024, 1024], P(None, 'mp')
- grad_w_out: float32 [1024, 1024], P('mp')
- grad_b_out: float32 [1024], replicated
- grad_gain_ffn: float32 [1024], replicated
- grad_w_up: float32 [1024, 4096], P(None, 'mp')
- grad_b_up: float32 [4096], P('mp')
- grad_w_down: float32 [4096, 1024], P('mp')
- grad_b_down: float32 [1024], replicated
The draws below stay inside these ranges and needn't reach their ends.
Inputs may be any that keep to these rules, and one draw needn't show every extreme that they name: `lengths`: row g holds group g's utterances, laid end to end from the group's first row; they sum to at most 4096, each is 1 or more, and the first is at least 3712 long.
All inputs are finite; a program needn't handle non-finite values.
Results may differ from the reference program's by a relative error of at most 0.02.
Values may be sent and summed in bfloat16 or wider, within the bound.
A program may use at most 576 MiB of HBM per device.

```python
import jax
import jax.numpy as jnp
from jax import lax

D = 1024
HEAD_DIM = 64
FF = 4096
SEQS = 8
GRP_TOK = 4096
TOKENS = 65536
N_DP = 16


def draw_lengths(key, part):
    key = jax.random.fold_in(key, 7)
    first_key, rest_key = jax.random.split(key)
    longest = GRP_TOK * 15 // 16
    first = jax.random.randint(first_key, (N_DP,), GRP_TOK * 29 // 32, longest + 1)
    first = jnp.where(jnp.arange(N_DP) == 0, longest, first)
    share = (GRP_TOK - first) // (SEQS - 1)
    others = jax.random.randint(rest_key, (N_DP, SEQS - 1), 1, share[:, None] + 1)
    others = others.at[0, 0].set(1)
    return jnp.concatenate([first[:, None], others], axis=1).astype(jnp.int32)


def levels(own_key, shape, pieces, low, largest):
    def one(position, parts):
        draws = jax.random.uniform(jax.random.fold_in(jax.random.fold_in(own_key, 6), position), (parts,), jnp.float32, low / len(pieces), largest / len(pieces))
        return jnp.repeat(jnp.exp(draws), shape[position] // parts).reshape((-1,) + (1,) * (len(shape) - position - 1))

    level = one(*pieces[0])
    for cut in pieces[1:]:
        level = level * one(*cut)
    return level


def bell_draw(key, dims, deviation, reach, cuts=(), kind=jnp.bfloat16):
    array = jax.random.normal(key, dims, jnp.float32) * deviation
    if len(cuts) > 0:
        array = levels(key, dims, cuts, -0.22, 0.18) * array
    return jnp.clip(array, min=-reach, max=reach).astype(kind)


def setup_inputs(seed: int = 0) -> dict:
    key_list = jax.random.split(jax.random.key(seed), 18)
    inputs = bell_draw(key_list[0], (TOKENS, D), 1.0, 6.0, ((0, 32),))
    skip_in = bell_draw(key_list[1], (TOKENS, D), 1.0, 6.0, ((0, 32),))
    cotangent = bell_draw(key_list[2], (TOKENS, D), 1.0, 6.0, ((0, 32),))
    lengths = draw_lengths(jax.random.fold_in(key_list[17], 71), 0)
    w_concat = bell_draw(key_list[4], (2 * D, D), (2 * D) ** -0.5, 0.125)
    b_concat = bell_draw(key_list[5], (D,), 0.3, 2.0, (), jnp.float32)
    gain_attn = jnp.clip(1.0 + 0.1 * jax.random.normal(key_list[6], (D,), jnp.float32), 0.5, 1.5)
    w_query = bell_draw(key_list[7], (D, D), D ** -0.5, 0.1875, ((1, 2),))
    w_key = bell_draw(key_list[8], (D, D), D ** -0.5, 0.1875, ((1, 2),))
    w_value = bell_draw(key_list[9], (D, D), D ** -0.5, 0.1875, ((1, 2),))
    w_out = bell_draw(key_list[10], (D, D), 2 ** -0.5, 4.0, ((0, 2),))
    b_out = bell_draw(key_list[11], (D,), 0.3, 2.0, (), jnp.float32)
    gain_ffn = jnp.clip(1.0 + 0.1 * jax.random.normal(key_list[12], (D,), jnp.float32), 0.5, 1.5)
    w_up = bell_draw(key_list[13], (D, FF), D ** -0.5, 0.1875, ((1, 2),))
    b_up = bell_draw(key_list[14], (FF,), 0.5, 3.0, ((0, 2),))
    w_down = bell_draw(key_list[15], (FF, D), FF ** -0.5, 0.09375, ((0, 2),))
    b_down = bell_draw(key_list[16], (D,), 0.3, 2.0, (), jnp.float32)
    return {"inputs": inputs, "skip_in": skip_in, "cotangent": cotangent, "lengths": lengths, "w_concat": w_concat, "b_concat": b_concat, "gain_attn": gain_attn, "w_query": w_query, "w_key": w_key, "w_value": w_value, "w_out": w_out, "b_out": b_out, "gain_ffn": gain_ffn, "w_up": w_up, "b_up": b_up, "w_down": w_down, "b_down": b_down}


HIGH = lax.Precision.HIGHEST
EPS = 1e-06

@jax.custom_vjp
def low(v):
    return lax.optimization_barrier(v.astype(jnp.bfloat16)).astype(jnp.float32)

@jax.custom_vjp
def low_back(v):
    return v

def low_keep(v):
    return (low(v), None)

def low_pass(kept, grad):
    return (grad,)

def back_keep(v):
    return (v, None)

def back_low(kept, grad):
    return (low(grad),)
low.defvjp(low_keep, low_pass)
low_back.defvjp(back_keep, back_low)

def layout(lengths_row, count):
    ends = jnp.cumsum(lengths_row).astype(jnp.int32)
    starts = (ends - lengths_row).astype(jnp.int32)
    places = jnp.arange(count, dtype=jnp.int32)
    seg = lax.optimization_barrier(jnp.sum((places[:, None] >= ends[None, :]).astype(jnp.int32), axis=1)).astype(jnp.int32)
    owner = seg[:, None] == jnp.arange(lengths_row.shape[0], dtype=jnp.int32)[None, :]
    start_of = lax.optimization_barrier(jnp.sum(jnp.where(owner, starts[None, :], 0), axis=1)).astype(jnp.int32)
    pos = (places - start_of).astype(jnp.float32)
    valid = (places < ends[-1]).astype(jnp.float32)
    return (seg, pos, valid)

def tables(pos):
    half = HEAD_DIM // 2
    freq = jnp.exp(-jnp.log(10000.0) * jnp.arange(half, dtype=jnp.float32) * 2.0 / HEAD_DIM)
    angle = pos[:, None] * freq[None, :]
    return (jnp.cos(angle), jnp.sin(angle))

def rotate(x, cosine, sine):
    count = x.shape[0]
    shaped = x.reshape(count, -1, HEAD_DIM)
    half = HEAD_DIM // 2
    first, second = (shaped[..., :half], shaped[..., half:])
    cc, ss = (cosine[:, None, :], sine[:, None, :])
    return jnp.concatenate([first * cc - second * ss, second * cc + first * ss], -1).reshape(count, -1)

def matmul(a, b):
    return jnp.dot(a, b, precision=HIGH)

def rms(v, gain):
    return v * lax.rsqrt(lax.optimization_barrier(jnp.mean(v * v, axis=-1, keepdims=True)) + EPS) * gain

def attend(query, keys, values, seg):
    count = query.shape[0]
    block = min(512, count)
    nblocks = count // block
    heads = query.shape[1] // HEAD_DIM
    qh = query.reshape(nblocks, block, heads, HEAD_DIM)
    kh = keys.reshape(count, heads, HEAD_DIM)
    vh = values.reshape(count, heads, HEAD_DIM)
    segs = seg.reshape(nblocks, block)

    @jax.checkpoint
    def one_block(items):
        qblock, sblock = items
        scores = jnp.einsum('qhd,khd->hqk', qblock, kh, precision=HIGH) * 0.125
        scores = low_back(scores)
        allowed = sblock[:, None] == seg[None, :]
        scores = jnp.where(allowed[None], scores, -1e+30)
        top = lax.optimization_barrier(jnp.max(scores, axis=-1, keepdims=True))
        expo = jnp.exp(scores - top)
        probs = expo / lax.optimization_barrier(jnp.sum(expo, axis=-1, keepdims=True))
        mixed = jnp.einsum('hqk,khd->qhd', low(probs), vh, precision=HIGH)
        return low(low_back(mixed))
    outs = lax.map(one_block, (qh, segs))
    return outs.reshape(count, heads * HEAD_DIM)

def layer(xg, sg, lrow, wc, bc, g1, wq, wk, wv, wo, bo, g2, w1, b1, w2, b2):
    count = xg.shape[0]
    seg, pos, valid = layout(lrow, count)
    cosine, sine = tables(pos)
    joined = jnp.concatenate([xg, sg], axis=1)
    h0 = low_back(matmul(joined, wc) + bc)
    n1 = low(rms(h0, g1))
    qp = low_back(matmul(n1, wq))
    kp = low_back(matmul(n1, wk))
    vp = low_back(matmul(n1, wv))
    query = low(rotate(qp, cosine, sine))
    keys = low(rotate(kp, cosine, sine))
    values = low(vp)
    mixed = attend(query, keys, values, seg)
    h1 = h0 + low_back(matmul(mixed, wo)) + bo
    n2 = low(rms(h1, g2))
    upper = low_back(matmul(n2, w1) + b1)
    hidden = low(jax.nn.gelu(upper, approximate=False))
    branch = low_back(matmul(hidden, w2))
    return valid[:, None] * (h1 + branch + b2)

def reference(inputs, skip_in, cotangent, lengths, w_concat, b_concat, gain_attn, w_query, w_key, w_value, w_out, b_out, gain_ffn, w_up, b_up, w_down, b_down):
    params = tuple((p.astype(jnp.float32) for p in (w_concat, b_concat, gain_attn, w_query, w_key, w_value, w_out, b_out, gain_ffn, w_up, b_up, w_down, b_down)))
    xs = inputs.astype(jnp.float32).reshape(N_DP, GRP_TOK, D)
    ss = skip_in.astype(jnp.float32).reshape(N_DP, GRP_TOK, D)
    ds = cotangent.astype(jnp.float32).reshape(N_DP, GRP_TOK, D)

    def step(carry, item):
        xg, sg, dg, lrow = item

        def forward(xx, sk, *weights):
            return layer(xx, sk, lrow, *weights)
        result, pull = jax.vjp(forward, xg, sg, *params)
        grads = pull(dg)
        carry = tuple((c + g for c, g in zip(carry, grads[2:])))
        return (carry, (result, grads[0], grads[1]))
    init = tuple((jnp.zeros_like(p) for p in params))
    total, (ys, dxs, dss) = lax.scan(step, init, (xs, ss, ds, lengths))
    return (ys.reshape(-1, D), dxs.reshape(-1, D), dss.reshape(-1, D), total[0], total[1], total[2], total[3], total[4], total[5], total[6], total[7], total[8], total[9], total[10], total[11], total[12])
```

```python
import functools

import jax
import jax.numpy as jnp
from jax import lax
from jax.experimental import pallas as pl
from jax.experimental.pallas import tpu as pltpu
from jax.sharding import Mesh
from jax.sharding import PartitionSpec as P

HEAD_DIM = 64
HALF = HEAD_DIM // 2
EPS = 1e-06
FIRST_LEAST = 3712
FIRST_MOST = 3840
SEGS = 16
LOG2E = 1.4426950408889634
LN2 = 0.6931471805599453
VMEM = 60 * 2**20

BF = jnp.bfloat16
F32 = jnp.float32


def dot(left, right, dims=((1,), (0,))):
    return lax.dot_general(left, right, (dims, ((), ())), preferred_element_type=F32)


def dot_tn(left, right):
    return dot(left, right, ((0,), (0,)))


def dot_nt(left, right):
    return dot(left, right, ((1,), (1,)))


def layout(lengths_row, count):
    ends = jnp.cumsum(lengths_row)
    starts = ends - lengths_row
    places = jnp.arange(count, dtype=jnp.int32)
    seg = jnp.sum((places[:, None] >= ends[None, :]).astype(jnp.int32), axis=1)
    owner = seg[:, None] == jnp.arange(lengths_row.shape[0], dtype=jnp.int32)[None, :]
    start_of = jnp.sum(jnp.where(owner, starts[None, :], 0), axis=1)
    pos = (places - start_of).astype(F32)
    valid = (places < ends[-1]).astype(F32)
    return (ends.astype(jnp.int32), pos, valid)


def tables(pos):
    freq = jnp.exp(-jnp.log(10000.0) * jnp.arange(HALF, dtype=F32) * 2.0 / HEAD_DIM)
    angle = freq[:, None] * pos[None, :]
    return (jnp.cos(angle), jnp.sin(angle))


def norm_back(grad, stream, scale, gain):
    tilted = grad * gain
    grad_gain = jnp.sum(grad * stream * scale, axis=0)
    grad_stream = scale * tilted - stream * scale**3 * jnp.mean(
        tilted * stream, axis=-1, keepdims=True
    )
    return (grad_stream, grad_gain)


def params():
    return pltpu.CompilerParams(vmem_limit_bytes=VMEM)


def cost(flops, moved):
    return pl.CostEstimate(flops=flops // 8, bytes_accessed=moved // 8, transcendentals=0)


def project_kernel(x_ref, w_ref, cos_ref, sin_ref, q_ref, k_ref, v_ref):
    x = x_ref[...]
    c, s = cos_ref[...], sin_ref[...]
    width = q_ref.shape[0]
    for out, first, factor in ((q_ref, 0, 0.125 * LOG2E), (k_ref, width, 1.0)):
        t = dot_nt(w_ref[first : first + width, :], x)
        for h in range(0, width, HEAD_DIM):
            a, b = t[h : h + HALF], t[h + HALF : h + HEAD_DIM]
            out[h : h + HALF, :] = ((a * c - b * s) * factor).astype(BF)
            out[h + HALF : h + HEAD_DIM, :] = ((b * c + a * s) * factor).astype(BF)
    v_ref[...] = dot_nt(w_ref[2 * width :, :], x).astype(BF)


def project(x, w, cosine, sine):
    count, depth = x.shape
    width = w.shape[0] // 3
    block = min(512, count)
    table = pl.BlockSpec((HALF, block), lambda i: (0, i))
    out = pl.BlockSpec((width, block), lambda i: (0, i))
    return pl.pallas_call(
        project_kernel,
        grid=(count // block,),
        in_specs=[
            pl.BlockSpec((block, depth), lambda i: (i, 0)),
            pl.BlockSpec(w.shape, lambda i: (0, 0)),
            table,
            table,
        ],
        out_specs=[out] * 3,
        out_shape=[jax.ShapeDtypeStruct((width, count), BF)] * 3,
        compiler_params=params(),
        name="project",
    )(x, w, cosine, sine)


def segments(ends_ref, first, count):
    pos = lax.broadcasted_iota(jnp.int32, (1, count), 1) + first
    seg = jnp.zeros((1, count), jnp.int32)
    for i in range(ends_ref.shape[0]):
        seg = seg + (pos >= ends_ref[i]).astype(jnp.int32)
    return lax.broadcasted_iota(jnp.int32, (SEGS, 1), 0) == seg


def zeros(rows, count):
    return jnp.zeros((rows, count), F32)


def key_pieces(count):
    if count == 4096:
        main = [(k0, 384) for k0 in range(0, FIRST_MOST, 384)]
        whole = [(k0, 1024) for k0 in range(0, count, 1024)]
        return [
            (0, 2048, main),
            (2048, 1536, main),
            (3584, 256, whole),
            (FIRST_MOST, 256, [(FIRST_LEAST, count - FIRST_LEAST)]),
        ]
    step = min(512, count)
    every = [(k0, step) for k0 in range(0, count, step)]
    return [(q0, step, every) for q0 in range(0, count, step)]


def attend_kernel(cut, ends_ref, part_ref, q_ref, k_ref, v_ref, o_ref, l_ref, kaug, qaug, vaug):
    count = k_ref.shape[1]
    here = q_ref.shape[1]
    part = part_ref[0]
    same = segments(ends_ref, 0, count)
    kaug[...] = (
        jnp.concatenate([k_ref[...].astype(F32), jnp.where(same, 0.0, -1e30), zeros(48, count)], 0)
        .T.astype(BF)
    )
    mine = segments(ends_ref, part * here, here)
    qaug[...] = jnp.concatenate(
        [q_ref[...].astype(F32), jnp.where(mine, 1.0, 0.0), zeros(48, here)], 0
    ).astype(BF)
    first = lax.broadcasted_iota(jnp.int32, (SEGS, count), 0) == 0
    vaug[...] = jnp.concatenate([v_ref[...].astype(F32), jnp.where(first, 1.0, 0.0)], 0).astype(BF)

    def block(q0, width, pieces):
        queries = qaug[:, q0 : q0 + width]
        top = jnp.full((1, width), -jnp.inf, F32)
        acc = jnp.zeros((HEAD_DIM + SEGS, width), F32)
        for k0, n in pieces:
            scores = dot(kaug[k0 : k0 + n, :], queries)
            higher = jnp.maximum(top, jnp.max(scores, axis=0, keepdims=True))
            probs = jnp.exp2(scores - higher).astype(BF)
            acc = acc * jnp.exp2(top - higher) + dot(vaug[:, k0 : k0 + n], probs)
            top = higher
        total = acc[HEAD_DIM : HEAD_DIM + 1]
        o_ref[:, q0 : q0 + width] = (acc[:HEAD_DIM] / total).astype(BF)
        l_ref[0, :, q0 : q0 + width] = top + jnp.log2(total)

    pieces = key_pieces(count)
    for p in range(cut):
        low, high = p * here, (p + 1) * here

        @pl.when(part == p)
        def _():
            for q0, width, keys in pieces:
                if low <= q0 < high:
                    block(q0 - low, width, keys)


def attend(ends, part, query, keys, values, cut):
    rows, count = query.shape
    heads = rows // HEAD_DIM
    here = count // cut
    whole = pl.BlockSpec((HEAD_DIM, count), lambda h, e, p: (h, 0))
    return pl.pallas_call(
        functools.partial(attend_kernel, cut),
        grid_spec=pltpu.PrefetchScalarGridSpec(
            num_scalar_prefetch=2,
            grid=(heads,),
            in_specs=[
                pl.BlockSpec((HEAD_DIM, here), lambda h, e, p: (h, p[0])),
                whole,
                whole,
            ],
            out_specs=[
                pl.BlockSpec((HEAD_DIM, here), lambda h, e, p: (h, 0)),
                pl.BlockSpec((1, 1, here), lambda h, e, p: (h, 0, 0)),
            ],
            scratch_shapes=[
                pltpu.VMEM((count, 128), BF),
                pltpu.VMEM((128, here), BF),
                pltpu.VMEM((HEAD_DIM + SEGS, count), BF),
            ],
        ),
        out_shape=[
            jax.ShapeDtypeStruct((rows, here), BF),
            jax.ShapeDtypeStruct((heads, 1, here), F32),
        ],
        compiler_params=params(),
        name="attend",
        cost_estimate=cost(4 * rows * here * count, 8 * rows * count),
    )(ends, part, query, keys, values)


def local_segments(ends_ref, part, count):
    return segments(ends_ref, part * count, count)


def spans(first, last, step):
    return [(k0, min(step, last - k0)) for k0 in range(first, last, step)]


def regions(query_part, key_parts, half):
    edge, start = FIRST_MOST - half, FIRST_LEAST - half

    def keys(first, last, p):
        return [(p, k0, n) for k0, n in spans(first, last, 1024)]

    if query_part == 0:
        found = []
        for p in key_parts:
            found += keys(0, half, 0) if p == 0 else keys(0, edge, 1)
        return [(0, half, found)]
    low = edge - 256
    if list(key_parts) == [0]:
        return [(0, edge, keys(0, half, 0)), (edge, half - edge, [])]
    main, mixed, last = [], [], []
    for p in key_parts:
        if p == 0:
            main += keys(0, half, 0)
            mixed += keys(0, half, 0)
        else:
            main += keys(0, edge, 1)
            mixed += keys(0, half, 1)
            last += [(1, start, half - start)]
    return [(0, low, main), (low, 256, mixed), (edge, half - edge, last)]


def half_kernel(query_far, key_sides, given, last, ends_ref, part_ref, *refs):
    refs = list(refs)
    q_ref = refs.pop(0)
    kv = {side: (refs.pop(0), refs.pop(0)) for side in key_sides}
    acc_in, top_in = (refs.pop(0), refs.pop(0)) if given else (None, None)
    out_ref, top_ref = refs.pop(0), refs.pop(0)
    qaug = refs.pop(0)
    kaug = {side: refs.pop(0) for side in key_sides}
    vaug = {side: refs.pop(0) for side in key_sides}
    half = q_ref.shape[1]
    rank = part_ref[0]

    @pl.when(pl.program_id(0) == 0)
    def _():
        for side in key_sides:
            same = local_segments(ends_ref, rank if side == 0 else 1 - rank, half)
            blank = zeros(HEAD_DIM, half)
            kaug[side][...] = (
                jnp.concatenate([blank, jnp.where(same, 0.0, -1e30), zeros(48, half)], 0)
                .T.astype(BF)
            )
            first = lax.broadcasted_iota(jnp.int32, (SEGS, half), 0) == 0
            vaug[side][HEAD_DIM:, :] = jnp.where(first, 1.0, 0.0).astype(BF)
        mine = local_segments(ends_ref, 1 - rank if query_far else rank, half)
        qaug[HEAD_DIM:, :] = jnp.concatenate(
            [jnp.where(mine, 1.0, 0.0), zeros(48, half)], 0
        ).astype(BF)

    for side in key_sides:
        kaug[side][:, :HEAD_DIM] = kv[side][0][...].T
        vaug[side][:HEAD_DIM, :] = kv[side][1][...]
    qaug[:HEAD_DIM, :] = q_ref[...]

    for here in range(2):
        query_part = 1 - here if query_far else here
        part_of = {side: here if side == 0 else 1 - here for side in key_sides}
        side_of = {p: side for side, p in part_of.items()}

        @pl.when(rank == here)
        def _():
            for q0, width, pieces in regions(query_part, list(side_of), half):
                there = slice(q0, q0 + width)
                queries = qaug[:, there]
                if given:
                    top, acc = top_in[0, :, there], acc_in[0, :, there]
                else:
                    top = jnp.full((1, width), -jnp.inf, F32)
                    acc = jnp.zeros((HEAD_DIM + SEGS, width), F32)
                for p, k0, n in pieces:
                    side = side_of[p]
                    scores = dot(kaug[side][k0 : k0 + n, :], queries)
                    higher = jnp.maximum(top, jnp.max(scores, axis=0, keepdims=True))
                    probs = jnp.exp2(scores - higher).astype(BF)
                    acc = acc * jnp.exp2(top - higher) + dot(vaug[side][:, k0 : k0 + n], probs)
                    top = higher
                if last:
                    total = acc[HEAD_DIM : HEAD_DIM + 1]
                    out_ref[:, there] = (acc[:HEAD_DIM] / total).astype(BF)
                    top_ref[0, :, there] = top + jnp.log2(total)
                else:
                    out_ref[0, :, there] = acc
                    top_ref[0, :, there] = top


def attend_half(name, ends, rank, query, query_far, keys, carry=None, last=True):
    rows, half = query.shape
    heads = rows // HEAD_DIM
    sides = sorted(keys)
    head = pl.BlockSpec((HEAD_DIM, half), lambda h, e, r: (h, 0))
    tall = pl.BlockSpec((1, HEAD_DIM + SEGS, half), lambda h, e, r: (h, 0, 0))
    line = pl.BlockSpec((1, 1, half), lambda h, e, r: (h, 0, 0))
    operands = [query]
    for side in sides:
        operands += list(keys[side])
    specs = [head] * len(operands)
    if carry is not None:
        operands += list(carry)
        specs += [tall, line]
    return pl.pallas_call(
        functools.partial(half_kernel, query_far, sides, carry is not None, last),
        grid_spec=pltpu.PrefetchScalarGridSpec(
            num_scalar_prefetch=2,
            grid=(heads,),
            in_specs=specs,
            out_specs=[head if last else tall, line],
            scratch_shapes=[pltpu.VMEM((128, half), BF)]
            + [pltpu.VMEM((half, 128), BF)] * len(sides)
            + [pltpu.VMEM((HEAD_DIM + SEGS, half), BF)] * len(sides),
        ),
        out_shape=[
            jax.ShapeDtypeStruct((rows, half), BF)
            if last
            else jax.ShapeDtypeStruct((heads, HEAD_DIM + SEGS, half), F32),
            jax.ShapeDtypeStruct((heads, 1, half), F32),
        ],
        compiler_params=params(),
        name=name,
        cost_estimate=cost(16 * rows * half * half * len(sides), 8 * rows * half),
    )(ends, rank, *operands)


def split3(x):
    a = x.astype(BF).astype(F32)
    b = (x - a).astype(BF).astype(F32)
    row = lax.broadcasted_iota(jnp.int32, (SEGS, 1), 0)
    return jnp.where(row == 0, a, jnp.where(row == 1, b, jnp.where(row == 2, x - a - b, 0.0)))


def attend_back_kernel(
    ends_ref, q_ref, k_ref, v_ref, g_ref, o_ref, l_ref, cos_ref, sin_ref, d_ref,
    kaug, vaug, qaug, gaug, pair, dq,
):
    count = k_ref.shape[1]
    same = segments(ends_ref, 0, count)
    row = lax.broadcasted_iota(jnp.int32, (SEGS, count), 0)
    shift = jnp.where(row < 3, 1.0, 0.0)
    g = g_ref[...].astype(F32)
    q = q_ref[...].astype(F32)
    delta = jnp.sum(g * o_ref[...].astype(F32), axis=0, keepdims=True)
    kaug[...] = (
        jnp.concatenate(
            [k_ref[...].astype(F32), jnp.where(same, 0.0, -1e30), shift, zeros(32, count)], 0
        )
        .T.astype(BF)
    )
    vaug[...] = (
        jnp.concatenate([v_ref[...].astype(F32), shift, zeros(48, count)], 0).T.astype(BF)
    )
    qaug[...] = jnp.concatenate(
        [q, jnp.where(same, 1.0, 0.0), split3(-l_ref[0]), zeros(32, count)], 0
    ).astype(BF)
    gaug[...] = jnp.concatenate([g, split3(-delta), zeros(48, count)], 0).astype(BF)
    pair[...] = jnp.concatenate([q, g], 0).T.astype(BF)
    dq[...] = jnp.zeros_like(dq)

    def turn(grad, c, s, factor):
        a, b = grad[:HALF], grad[HALF:]
        return (
            jnp.concatenate([a * c + b * s, b * c - a * s], 0) * factor
        ).astype(BF)

    def chunk(k0, n, queries):
        where = pl.ds(k0, n)
        kb, vb, kt = kaug[where, :], vaug[where, :], k_ref[:, where]
        dk = jnp.zeros((n, HEAD_DIM), F32)
        dv = jnp.zeros((n, HEAD_DIM), F32)
        for q0, width in queries:
            there = slice(q0, q0 + width)
            probs = jnp.exp2(dot(kb, qaug[:, there]))
            tilt = (probs * dot(vb, gaug[:, there])).astype(BF)
            dv = dv + dot(probs.astype(BF), pair[there, HEAD_DIM:])
            dk = dk + dot(tilt, pair[there, :HEAD_DIM])
            dq[:, there] += dot(kt, tilt)
        c, s = cos_ref[:, where], sin_ref[:, where]
        d_ref[1, 0, :, where] = turn(dk.T, c, s, LN2)
        d_ref[2, 0, :, where] = dv.T.astype(BF)

    if count == 4096:
        main = [(q0, 1920) for q0 in range(0, FIRST_MOST, 1920)]

        def step(i, carry):
            chunk(pl.multiple_of(i * 512, 512), 512, main)
            return carry

        lax.fori_loop(0, 7, step, 0)
        chunk(3584, 256, [(q0, 1024) for q0 in range(0, count, 1024)])
        chunk(FIRST_MOST, count - FIRST_MOST, [(3584, 512)])
    else:
        size = min(512, count)

        def step(i, carry):
            chunk(pl.multiple_of(i * size, size), size, [(q, size) for q in range(0, count, size)])
            return carry

        lax.fori_loop(0, count // size, step, 0)
    d_ref[0, 0] = turn(dq[...], cos_ref[...], sin_ref[...], 0.125)


def attend_back(ends, query, keys, values, grad, mixed, logsum, cosine, sine):
    rows, count = query.shape
    heads = rows // HEAD_DIM
    whole = pl.BlockSpec((HEAD_DIM, count), lambda h, e: (h, 0))
    table = pl.BlockSpec((HALF, count), lambda h, e: (0, 0))
    out = pl.pallas_call(
        attend_back_kernel,
        grid_spec=pltpu.PrefetchScalarGridSpec(
            num_scalar_prefetch=1,
            grid=(heads,),
            in_specs=[whole] * 5
            + [pl.BlockSpec((1, 1, count), lambda h, e: (h, 0, 0)), table, table],
            out_specs=pl.BlockSpec((3, 1, HEAD_DIM, count), lambda h, e: (0, h, 0, 0)),
            scratch_shapes=[
                pltpu.VMEM((count, 128), BF),
                pltpu.VMEM((count, 128), BF),
                pltpu.VMEM((128, count), BF),
                pltpu.VMEM((128, count), BF),
                pltpu.VMEM((count, 128), BF),
                pltpu.VMEM((HEAD_DIM, count), F32),
            ],
        ),
        out_shape=jax.ShapeDtypeStruct((3, heads, HEAD_DIM, count), BF),
        compiler_params=params(),
        name="attend_back",
        cost_estimate=cost(10 * rows * count * count, 16 * rows * count),
    )(ends, query, keys, values, grad, mixed, logsum, cosine, sine)
    return out.reshape(3 * rows, count)


def turn_back(grad, c, s, factor):
    a, b = grad[:HALF], grad[HALF:]
    return (jnp.concatenate([a * c + b * s, b * c - a * s], 0) * factor).astype(BF)


def back_chunks(key_part, query_parts, half):
    edge = FIRST_MOST - half
    low = edge - 256
    found = []
    if key_part == 0:
        queries = []
        for p in query_parts:
            queries += [(p, 0, half if p == 0 else edge)]
        return [(0, half, 512, queries)]
    main = [(p, 0, half if p == 0 else edge) for p in query_parts]
    found.append((0, low, 512, main))
    found.append((low, 256, 256, [(p, 0, half) for p in query_parts]))
    if 1 in query_parts:
        found.append((edge, half - edge, 256, [(1, low, half - low)]))
    return found


def half_back_kernel(near_only, ends_ref, part_ref, *refs):
    refs = list(refs)
    sides = (0,) if near_only else (0, 1)
    given = {side: [refs.pop(0) for _ in range(8)] for side in sides}
    if near_only:
        partial_ref = refs.pop(0)
        while len(refs) > 1 + 7:
            refs.pop(0)
        out_ref = refs.pop(0)
    else:
        while len(refs) > 2 + 7:
            refs.pop(0)
        out_ref, partial_ref = refs.pop(0), refs.pop(0)
    kaug, vaug, qaug, gaug, pair, dq, sums = refs
    rank = part_ref[0]
    half = given[0][0].shape[1]

    @pl.when(pl.program_id(0) == 0)
    def _():
        row = lax.broadcasted_iota(jnp.int32, (SEGS, half), 0)
        shift = jnp.where(row < 3, 1.0, 0.0)
        blank = zeros(HEAD_DIM, half)
        for side in sides:
            there = slice(side * half, side * half + half)
            same = local_segments(ends_ref, rank if side == 0 else 1 - rank, half)
            kaug[there, :] = (
                jnp.concatenate([blank, jnp.where(same, 0.0, -1e30), shift, zeros(32, half)], 0)
                .T.astype(BF)
            )
            vaug[there, :] = jnp.concatenate([blank, shift, zeros(48, half)], 0).T.astype(BF)
            qaug[HEAD_DIM:, there] = jnp.concatenate(
                [jnp.where(same, 1.0, 0.0), zeros(48, half)], 0
            ).astype(BF)
            gaug[HEAD_DIM:, there] = blank.astype(BF)

    for side in sides:
        q_ref, k_ref, v_ref, g_ref, o_ref, l_ref = given[side][:6]
        there = slice(side * half, side * half + half)
        g = g_ref[...]
        q = q_ref[...]
        delta = jnp.sum(g.astype(F32) * o_ref[...].astype(F32), axis=0, keepdims=True)
        kaug[there, :HEAD_DIM] = k_ref[...].T
        vaug[there, :HEAD_DIM] = v_ref[...].T
        qaug[:HEAD_DIM, there] = q
        qaug[HEAD_DIM + SEGS : HEAD_DIM + 2 * SEGS, there] = split3(-l_ref[0]).astype(BF)
        gaug[:HEAD_DIM, there] = g
        gaug[HEAD_DIM : HEAD_DIM + SEGS, there] = split3(-delta).astype(BF)
        pair[there, :] = jnp.concatenate([q, g], 0).T
    if near_only:
        dq[...] = partial_ref[0, 0]
        sums[...] = partial_ref[1:, 0]
    else:
        dq[...] = jnp.zeros_like(dq)
        sums[...] = jnp.zeros_like(sums)

    def chunk(side, k0, n, queries):
        where = pl.ds(side * half + k0, n)
        kb, vb, kt = kaug[where, :], vaug[where, :], given[side][1][:, pl.ds(k0, n)]
        dk = jnp.zeros((n, HEAD_DIM), F32)
        dv = jnp.zeros((n, HEAD_DIM), F32)
        for q0, width in queries:
            there = slice(q0, q0 + width)
            probs = jnp.exp2(dot(kb, qaug[:, there]))
            tilt = (probs * dot(vb, gaug[:, there])).astype(BF)
            dv = dv + dot(probs.astype(BF), pair[there, HEAD_DIM:])
            dk = dk + dot(tilt, pair[there, :HEAD_DIM])
            dq[:, there] += dot(kt, tilt)
        if side == 0 and not near_only:
            sums[0, :, pl.ds(k0, n)] = dk.T
            sums[1, :, pl.ds(k0, n)] = dv.T
            return
        dk, dv = dk.T, dv.T
        if near_only:
            dk = dk + sums[0, :, pl.ds(k0, n)]
            dv = dv + sums[1, :, pl.ds(k0, n)]
        c, s = given[side][6][:, pl.ds(k0, n)], given[side][7][:, pl.ds(k0, n)]
        out_ref[1, 0, :, pl.ds(k0, n)] = turn_back(dk, c, s, LN2)
        out_ref[2, 0, :, pl.ds(k0, n)] = dv.astype(BF)

    for here in range(2):

        @pl.when(rank == here)
        def _():
            side_of = {here: 0, 1 - here: 1}
            for key_part, side in side_of.items():
                if near_only and side == 1:
                    continue
                if near_only:
                    query_parts = [here]
                else:
                    query_parts = [0, 1] if side == 1 else [1 - here]
                for k0, total, n, queries in back_chunks(key_part, query_parts, half):
                    spread = [(side_of[p] * half + q0, width) for p, q0, width in queries]
                    if total == n:
                        chunk(side, k0, n, spread)
                        continue

                    def step(i, carry):
                        chunk(side, pl.multiple_of(k0 + i * n, n), n, spread)
                        return carry

                    lax.fori_loop(0, total // n, step, 0)

    if near_only:
        c, s = given[0][6][...], given[0][7][...]
        out_ref[0, 0] = turn_back(dq[...], c, s, 0.125)
    else:
        c, s = given[1][6][...], given[1][7][...]
        out_ref[0, 0] = turn_back(dq[:, half:], c, s, 0.125)
        partial_ref[0, 0] = dq[:, :half]
        partial_ref[1:, 0] = sums[...]


def half_back(name, ends, rank, sides, first, count, partial=None, written=(), after=None):
    rows, half = sides[0][0].shape
    heads = rows // HEAD_DIM
    near_only = partial is not None
    head = pl.BlockSpec((HEAD_DIM, half), lambda h, e, r: (h + first, 0))
    line = pl.BlockSpec((1, 1, half), lambda h, e, r: (h + first, 0, 0))
    table = pl.BlockSpec((HALF, half), lambda h, e, r: (0, 0))
    block = pl.BlockSpec((3, 1, HEAD_DIM, half), lambda h, e, r: (0, h + first, 0, 0))
    anywhere = pl.BlockSpec(memory_space=pl.ANY)
    operands, specs = [], []
    for side in sides:
        operands += list(side)
        specs += [head] * 5 + [line, table, table]
    result = jax.ShapeDtypeStruct((3, heads, HEAD_DIM, half), BF)
    if near_only:
        operands.append(partial)
        specs.append(block)
    aliases = {2 + len(operands) + i: i for i in range(len(written))}
    operands += list(written)
    specs += [anywhere] * len(written)
    if after is not None:
        operands.append(after)
        specs.append(anywhere)
    out_specs = [block] if near_only else [block, block]
    out_shape = [result, jax.ShapeDtypeStruct(result.shape, F32)][: len(out_specs)]
    wide = half * len(sides)
    return pl.pallas_call(
        functools.partial(half_back_kernel, near_only),
        grid_spec=pltpu.PrefetchScalarGridSpec(
            num_scalar_prefetch=2,
            grid=(count,),
            in_specs=specs,
            out_specs=out_specs,
            scratch_shapes=[
                pltpu.VMEM((wide, 128), BF),
                pltpu.VMEM((wide, 128), BF),
                pltpu.VMEM((128, wide), BF),
                pltpu.VMEM((128, wide), BF),
                pltpu.VMEM((wide, 128), BF),
                pltpu.VMEM((HEAD_DIM, wide), F32),
                pltpu.VMEM((2, HEAD_DIM, half), F32),
            ],
        ),
        out_shape=out_shape,
        input_output_aliases=aliases,
        compiler_params=params(),
        name=name,
        cost_estimate=cost(40 * count * HEAD_DIM * half * half * (1 if near_only else 3), 40 * count * HEAD_DIM * half),
    )(ends, rank, *operands)


def ffn_kernel(step, given, src_ref, dst_ref, n_ref, g_ref, up_ref, bias_ref, down_ref, *refs):
    branch_in, dn_in = refs[:2] if given else (None, None)
    branch_ref, dn_ref, dw_ref, dbias_ref, branch, dn, sems = refs[3 if given else 0 :]

    rows, depth = n_ref.shape
    steps = [(i, slice(r0, r0 + step)) for i, r0 in enumerate(range(0, rows, step))]
    opening = (pl.program_id(0) == 0) & (pl.program_id(1) == 0)
    closing = (pl.program_id(0) == pl.num_programs(0) - 1) & (
        pl.program_id(1) == pl.num_programs(1) - 1
    )

    def moves(i, part, out):
        if out:
            pairs = ((branch, branch_ref), (dn, dn_ref))
        else:
            pairs = ((branch_in, branch), (dn_in, dn))
        return [
            pltpu.make_async_copy(src.at[part, :], dst.at[part, :], sems.at[j, i])
            for j, (src, dst) in enumerate(pairs)
        ]

    @pl.when(opening)
    def _():
        if given:
            for i, part in steps:
                for move in moves(i, part, False):
                    move.start()
        else:
            branch[...] = jnp.zeros_like(branch)
            dn[...] = jnp.zeros_like(dn)

    up = up_ref[...].reshape(depth, -1)
    down, bias = down_ref[0, 0], bias_ref[0].astype(F32)
    width = up.shape[1]
    dup = jnp.zeros((width, depth), F32)
    ddown = jnp.zeros((width, depth), F32)
    dbias = jnp.zeros((1, width), F32)
    for i, part in steps:
        x, y = n_ref[part, :], g_ref[part, :]
        u = dot(x, up) + bias
        dz = dot_nt(y, down)
        normal = 0.5 * (1.0 + lax.erf(u * 0.7071067811865476))
        density = jnp.exp(-0.5 * u * u) * 0.3989422804014327
        z = (u * normal).astype(BF)
        du = (dz * (normal + u * density)).astype(BF)
        if given:

            @pl.when(opening)
            def _():
                for move in moves(i, part, False):
                    move.wait()

        branch[part, :] += dot(z, down)
        dn[part, :] += dot_nt(du, up)

        @pl.when(closing)
        def _():
            for move in moves(i, part, True):
                move.start()

        ddown = ddown + dot_tn(z, y)
        dup = dup + dot_tn(du, x)
        dbias = dbias + jnp.sum(du.astype(F32), axis=0, keepdims=True)
    dw_ref[0, 0, :width, :] = dup.astype(BF)
    dw_ref[0, 0, width:, :] = ddown.astype(BF)
    dbias_ref[0] = dbias

    @pl.when(closing)
    def _():
        for i, part in steps:
            for move in moves(i, part, True):
                move.wait()


def ffn_block(hidden):
    return min(512, hidden // 2)


def ffn(name, n2, grad, up, bias, down, extra, parts, src, dst, before=None):
    rows, depth = n2.shape
    hidden = up.shape[3]
    block = ffn_block(hidden)
    per = hidden // 2 // block
    step = min(512, rows)
    once = pl.BlockSpec(
        (rows, depth), lambda p, i, f, t: (0, 0), pipeline_mode=pl.Buffered(1)
    )
    anywhere = pl.BlockSpec(memory_space=pl.ANY)
    operands = [n2, grad, up, bias, down] + ([] if before is None else list(before))
    return pl.pallas_call(
        functools.partial(ffn_kernel, step, before is not None),
        grid_spec=pltpu.PrefetchScalarGridSpec(
            num_scalar_prefetch=2,
            grid=(src.shape[0], 2 * per),
            in_specs=[
                once,
                once,
                pl.BlockSpec((2, 1, depth // 2, block), lambda p, i, f, t: (0, f[p], 0, i)),
                pl.BlockSpec((1, 1, block), lambda p, i, f, t: (f[p], 0, i)),
                pl.BlockSpec(
                    (1, 1, block, depth), lambda p, i, f, t: (i // per, f[p], i % per, 0)
                ),
            ]
            + ([] if before is None else [anywhere] * 3),
            out_specs=[anywhere] * 2
            + [
                pl.BlockSpec(
                    (1, 1, 2 * block, depth), lambda p, i, f, t: (i // per, t[p], i % per, 0)
                ),
                pl.BlockSpec((1, 1, block), lambda p, i, f, t: (p, 0, i)),
            ],
            scratch_shapes=[pltpu.VMEM((rows, depth), F32)] * 2
            + [pltpu.SemaphoreType.DMA((2, rows // step))],
        ),
        out_shape=[jax.ShapeDtypeStruct((rows, depth), F32)] * 2
        + [
            jax.ShapeDtypeStruct((2, parts, hidden + extra, depth), BF),
            jax.ShapeDtypeStruct((src.shape[0], 1, hidden), F32),
        ],
        input_output_aliases={} if before is None else {9: 2},
        compiler_params=params(),
        name=name,
        cost_estimate=cost(12 * rows * depth * hidden * src.shape[0], 8 * depth * hidden * src.shape[0]),
    )(src, dst, *operands)


def out_back_kernel(mixed_ref, grad_ref, sums_ref, after_ref, out_ref):
    out_ref[0, 0] = dot(mixed_ref[...], grad_ref[...]).astype(BF)


def out_back(mixed_rows, grad, sums, extra, after):
    heads, rows = mixed_rows.shape
    _, parts, total, depth = sums.shape
    return pl.pallas_call(
        out_back_kernel,
        grid=(parts, 2),
        in_specs=[
            pl.BlockSpec((extra, rows), lambda p, c: (2 * p + c, 0)),
            pl.BlockSpec((rows, depth), lambda p, c: (0, 0)),
            pl.BlockSpec(memory_space=pl.ANY),
            pl.BlockSpec(memory_space=pl.ANY),
        ],
        out_specs=pl.BlockSpec((1, 1, extra, depth), lambda p, c: (c, p, total // extra - 1, 0)),
        out_shape=jax.ShapeDtypeStruct(sums.shape, BF),
        input_output_aliases={2: 0},
        compiler_params=params(),
        name="out_back",
        cost_estimate=cost(2 * rows * depth * heads, 2 * heads * depth),
    )(mixed_rows, grad, sums, after)


def project_back_kernel(*refs):
    out_ref = refs[-1]
    pairs = refs[:-2]
    total = dot(pairs[1][...], pairs[0][...])
    for i in range(2, len(pairs), 2):
        total = total + dot(pairs[i + 1][...], pairs[i][...])
    out_ref[...] = total.T.astype(BF)


def project_back(pairs, after):
    total = pairs[0][1].shape[0]
    depth = pairs[0][0].shape[1]
    block = total // 3
    specs, operands = [], []
    for x, grad in pairs:
        specs += [
            pl.BlockSpec(x.shape, lambda i: (0, 0)),
            pl.BlockSpec((block, x.shape[0]), lambda i: (i, 0)),
        ]
        operands += [x, grad]
    return pl.pallas_call(
        project_back_kernel,
        grid=(3,),
        in_specs=specs + [pl.BlockSpec(memory_space=pl.ANY)],
        out_specs=pl.BlockSpec((depth, block), lambda i: (0, i)),
        out_shape=jax.ShapeDtypeStruct((depth, total), BF),
        compiler_params=params(),
        name="project_back",
        cost_estimate=cost(4 * pairs[0][0].shape[0] * depth * total, 8 * depth * total),
    )(*operands, after)


MESH = pl.DeviceIdType.MESH


def sum_all_kernel(
    big_ref, small_ref, after_ref, out_ref, small_out_ref,
    buf, done, core_in, x_in, y_in, z_in, small, small_in, small_z, local, send, recv, small_send, small_recv,
):
    o, c, m = lax.axis_index("dpo"), lax.axis_index("core"), lax.axis_index("mp")
    y, z = lax.rem(o, 2), lax.div(o, 2)
    zs = 4
    half = buf.shape[0] // 2
    quarter, eighth, last = half // 2, half // 4, half // 16
    sibling = (o, 1 - c, m)
    across = (o, c, 1 - m)
    beside = (z * 2 + 1 - y, c, m)

    def along(j):
        return (j * 2 + y, c, m)

    load = pltpu.make_async_copy(big_ref, buf, local.at[0])
    load.start()
    barrier = pltpu.get_barrier_semaphore()
    others = [lax.rem(z + d, zs) for d in range(1, zs)]
    for device in [sibling, across, beside] + [along(j) for j in others]:
        pl.semaphore_signal(barrier, inc=1, device_id=device, device_id_type=MESH)
    pl.semaphore_wait(barrier, 6)
    small[0] = small_ref[...]
    load.wait()

    def copy(src, dst, i, device, sems=(send, recv)):
        return pltpu.make_async_remote_copy(
            src_ref=src, dst_ref=dst, send_sem=sems[0].at[i], recv_sem=sems[1].at[i],
            device_id=device, device_id_type=MESH,
        )

    def rows(first, n, of=buf):
        return of.at[pl.ds(pl.multiple_of(first, last), n)]

    def back(first, n, i, device):
        return copy(rows(first, n, done), rows(first, n, done), i, device)

    def add(first, n, arrived):
        step = min(128, n)

        def one(i, carry):
            there = pl.ds(pl.multiple_of(first + i * step, last), step)
            here = pl.ds(pl.multiple_of(i * step, step), step)
            buf[there, :] = (
                buf[there, :].astype(F32) + arrived[here, :].astype(F32)
            ).astype(BF)
            return carry

        lax.fori_loop(0, n // step, one, 0)

    started = []

    def go(*args, **kwargs):
        one = copy(*args, **kwargs)
        one.start()
        started.append(one)
        return one

    tiny = (small_send, small_recv)
    mine = c * half
    theirs = (1 - c) * half
    core_a = go(rows(theirs + (1 - m) * quarter, quarter), core_in.at[0], 0, sibling)
    core_b = go(rows(theirs + m * quarter, quarter), core_in.at[1], 1, sibling)
    tiny_core = go(small.at[0], small_in.at[0], 0, sibling, sems=tiny)
    base_far, base = mine + (1 - m) * quarter, mine + m * quarter
    core_a.wait_recv()
    add(base_far, quarter, core_in.at[0])
    x_a = go(rows(base_far + (1 - y) * eighth, eighth), x_in.at[0], 2, across)
    x_b = go(rows(base_far + y * eighth, eighth), x_in.at[1], 3, across)
    tiny_core.wait_recv()
    small[1] = small[0] + small_in[0]
    tiny_x = go(small.at[1], small_in.at[1], 1, across, sems=tiny)
    core_b.wait_recv()
    add(base, quarter, core_in.at[1])
    far_y, near_y = base + (1 - y) * eighth, base + y * eighth
    x_a.wait_recv()
    add(far_y, eighth, x_in.at[0])
    y_a = go(rows(far_y, eighth), y_in, 4, beside)
    tiny_x.wait_recv()
    small[2] = small[1] + small_in[1]
    tiny_y = go(small.at[2], small_in.at[2], 2, beside, sems=tiny)
    x_b.wait_recv()
    add(near_y, eighth, x_in.at[1])
    y_a.wait_recv()
    add(near_y, eighth, y_in)
    for d in range(1, zs):
        j = lax.rem(z + d, zs)
        there = copy(rows(near_y + j * last, last), z_in.at[z], 5 + z, along(j))
        there.start()
        started.append(there)
    tiny_y.wait_recv()
    small_z[z] = small[2] + small_in[2]
    for d in range(1, zs):
        j = lax.rem(z + d, zs)
        there = copy(small_z.at[z], small_z.at[z], 3 + z, along(j), sems=tiny)
        there.start()
        started.append(there)
    own = near_y + z * last
    total = buf[pl.ds(pl.multiple_of(own, last), last), :].astype(F32)
    for d in range(1, zs):
        j = lax.rem(z + d, zs)
        copy(rows(own, last), z_in.at[j], 5 + j, along(j)).wait_recv()
        total = total + z_in[j].astype(F32)
    done[pl.ds(pl.multiple_of(own, last), last), :] = total.astype(BF)

    def hand(first, n, i, device):
        one = back(first, n, i, device)
        one.start()
        started.append(one)
        return one

    for d in range(1, zs):
        hand(own, last, 9 + z, along(lax.rem(z + d, zs)))
    for d in range(1, zs):
        j = lax.rem(z + d, zs)
        back(near_y + j * last, last, 9 + j, along(j)).wait_recv()
    y_back = hand(near_y, eighth, 13, beside)
    x_back = hand(near_y, eighth, 14, across)
    core_back = hand(near_y, eighth, 15, sibling)
    y_back.wait_recv()
    x_more = hand(far_y, eighth, 16, across)
    core_more = hand(far_y, eighth, 17, sibling)
    x_back.wait_recv()
    core_x = hand(base_far + y * eighth, eighth, 18, sibling)
    x_more.wait_recv()
    core_y = hand(base_far + (1 - y) * eighth, eighth, 19, sibling)
    for d in range(1, zs):
        j = lax.rem(z + d, zs)
        copy(small_z.at[j], small_z.at[j], 3 + j, along(j), sems=tiny).wait_recv()
    small_out_ref[...] = (small_z[0] + small_z[1]) + (small_z[2] + small_z[3])
    for one in (core_back, core_more, core_x, core_y):
        one.wait_recv()
    for one in started:
        one.wait_send()
    store = pltpu.make_async_copy(done, out_ref, local.at[1])
    store.start()
    store.wait()


def sum_all(big, small, after):
    rows, width = big.shape
    quarter, eighth, last = rows // 4, rows // 8, rows // 32
    anywhere = pl.BlockSpec(memory_space=pl.ANY)
    whole = pl.BlockSpec(memory_space=pltpu.VMEM)
    dma = pltpu.SemaphoreType.DMA
    return pl.pallas_call(
        sum_all_kernel,
        in_specs=[anywhere, whole, anywhere],
        out_specs=[anywhere, whole],
        out_shape=[
            jax.ShapeDtypeStruct(big.shape, BF),
            jax.ShapeDtypeStruct(small.shape, F32),
        ],
        scratch_shapes=[
            pltpu.VMEM((rows, width), BF),
            pltpu.VMEM((rows, width), BF),
            pltpu.VMEM((2, quarter, width), BF),
            pltpu.VMEM((2, eighth, width), BF),
            pltpu.VMEM((eighth, width), BF),
            pltpu.VMEM((4, last, width), BF),
            pltpu.VMEM((3,) + small.shape, F32),
            pltpu.VMEM((3,) + small.shape, F32),
            pltpu.VMEM((4,) + small.shape, F32),
            dma((2,)),
            dma((20,)),
            dma((20,)),
            dma((7,)),
            dma((7,)),
        ],
        compiler_params=pltpu.CompilerParams(
            collective_id=0, has_side_effects=True, vmem_limit_bytes=VMEM
        ),
        name="sum_all",
        cost_estimate=cost(rows * width, 8 * rows * width),
    )(big, small, after)


def join_back_kernel(grad_ref, w_ref, first_ref, second_ref):
    grad = grad_ref[...]
    width = first_ref.shape[1]
    first_ref[...] = dot_nt(grad, w_ref[:width, :])
    second_ref[...] = dot_nt(grad, w_ref[width:, :])


def join_back(grad, w):
    rows, depth = grad.shape
    width = w.shape[0] // 2
    block = min(256, rows)
    out = pl.BlockSpec((block, width), lambda i: (i, 0))
    return pl.pallas_call(
        join_back_kernel,
        grid=(rows // block,),
        in_specs=[
            pl.BlockSpec((block, depth), lambda i: (i, 0)),
            pl.BlockSpec(w.shape, lambda i: (0, 0)),
        ],
        out_specs=[out, out],
        out_shape=[jax.ShapeDtypeStruct((rows, width), F32)] * 2,
        compiler_params=params(),
        name="join_back",
        cost_estimate=cost(rows * depth * width, 8 * rows * width),
    )(grad, w)


def unpack_kernel(core_ref, own_ref, sibling_ref, up_ref, down_ref):
    mine = core_ref[0] == pl.program_id(0)
    width = down_ref.shape[0]
    block = jnp.where(mine, own_ref[...].astype(F32), sibling_ref[...].astype(F32))
    up_ref[...] = block[:width].T
    down_ref[...] = block[width:]


def unpack(core, own, sibling, hidden):
    depth = own.shape[1]
    block = ffn_block(hidden)
    per = hidden // 2 // block
    piece = pl.BlockSpec((2 * block, depth), lambda c, i, k: (i, 0))
    return pl.pallas_call(
        unpack_kernel,
        grid_spec=pltpu.PrefetchScalarGridSpec(
            num_scalar_prefetch=1,
            grid=(2, per),
            in_specs=[piece, piece],
            out_specs=[
                pl.BlockSpec((depth, block), lambda c, i, k: (0, c * per + i)),
                pl.BlockSpec((block, depth), lambda c, i, k: (c * per + i, 0)),
            ],
        ),
        out_shape=[
            jax.ShapeDtypeStruct((depth, hidden), F32),
            jax.ShapeDtypeStruct((hidden, depth), F32),
        ],
        compiler_params=params(),
        name="unpack",
        cost_estimate=cost(depth * hidden, 12 * depth * hidden),
    )(core, own, sibling)


def body(
    inputs, skip_in, cotangent, lengths, w_concat, b_concat, gain_attn, w_query, w_key, w_value,
    w_out, b_out, gain_ffn, w_up, b_up, w_down, b_down,
):
    parts = lax.axis_size("mp")
    rank = lax.axis_index("mp")
    core = lax.axis_index("core")
    dp = ("dpo", "core")
    rows, width = inputs.shape
    group = rows * parts
    paired = parts == 2 and group == 4096
    ends, pos_all, valid_all = layout(lengths[0], group)
    valid_here = lax.dynamic_slice_in_dim(valid_all, rank * rows, rows, 0)[:, None]
    each, hidden = w_out.shape[0], b_up.shape[0]
    extra = each // 2
    index = rank.reshape(1)
    other = 1 - index
    zero = jnp.zeros((1,), jnp.int32)

    def across(x):
        return lax.ppermute(x, "mp", [(0, 1), (1, 0)])

    def piece(x, i, size, axis=0):
        return lax.dynamic_slice_in_dim(x, i * size, size, axis)

    def order(near, far, axis):
        return jnp.where(
            rank == 0, jnp.concatenate([near, far], axis), jnp.concatenate([far, near], axis)
        )

    joined = jnp.concatenate([inputs, skip_in], axis=1)
    h0 = dot(joined, w_concat) + b_concat
    scale_one = lax.rsqrt(jnp.mean(h0 * h0, axis=-1, keepdims=True) + EPS)
    n1 = (h0 * scale_one * gain_attn).astype(BF)
    n1_far = across(n1) if paired else lax.all_gather(n1, "mp", axis=0, tiled=True)
    def gather(w):
        half = w.shape[0] // 2
        return lax.all_gather(piece(w, core, half), ("core", "mp"), axis=0).reshape(
            2, parts, half, w.shape[1]
        )

    w_qkv = jnp.concatenate([w_query, w_key, w_value], axis=1)
    w_turned = w_qkv.T
    if paired:
        bias_far = across(b_up)
        out_far = across(w_out)
        tables_near = tables(piece(pos_all, rank, rows))
        q_near, k_near, v_near = project(n1, w_turned, *tables_near)
        start = attend_half(
            "near_near", ends, index, q_near, False, {0: (k_near, v_near)}, last=False
        )
        n1_far, start, w_up_late, w_down_late = lax.optimization_barrier(
            (n1_far, start, w_up, w_down)
        )
        up_all = gather(w_up_late)
        down_all = gather(w_down_late)
        tables_far = tables(piece(pos_all, 1 - rank, rows))
        q_far, k_far, v_far = project(n1_far, w_turned, *tables_far)
        mixed_far, log_far = attend_half(
            "far_all", ends, index, q_far, True, {0: (k_near, v_near), 1: (k_far, v_far)}
        )
        mixed_in = across(mixed_far)
        mixed_near, log_near = attend_half(
            "near_far", ends, index, q_near, False, {1: (k_far, v_far)}, carry=start
        )
        mixed_rows = order(mixed_near, mixed_in, 0)
        attended = dot_tn(mixed_near, w_out) + dot_tn(mixed_in, out_far)
    else:
        bias_all = lax.all_gather(b_up, "mp", axis=0).reshape(parts, 1, -1)
        w_out_all = lax.all_gather(w_out, "mp", axis=0, tiled=True)
        up_all = gather(w_up)
        down_all = gather(w_down)
        cosine, sine = tables(pos_all)
        query, keys, values = project(n1_far, w_turned, cosine, sine)
        mixed, logsum = attend(ends, zero, query, keys, values, 1)
        mixed_rows = lax.all_to_all(mixed, "mp", 1, 0, tiled=True)
        attended = dot_tn(mixed_rows, w_out_all)
    h1 = h0 + attended + b_out
    scale_two = lax.rsqrt(jnp.mean(h1 * h1, axis=-1, keepdims=True) + EPS)
    n2 = (h1 * scale_two * gain_ffn).astype(BF)
    grad_rows = cotangent.astype(F32) * valid_here
    grad_low = grad_rows.astype(BF)
    if paired:
        branch, grad_n2, sums, bias_near = ffn(
            "ffn_near", n2, grad_low, w_up.reshape(2, 1, width // 2, hidden),
            b_up.reshape(1, 1, hidden), w_down.reshape(2, 1, hidden // 2, width),
            extra, parts, zero, index,
        )
        both = jnp.stack([bias_far, bias_far]).reshape(2, 1, hidden)
        branch, grad_n2, sums, grad_bias = ffn(
            "ffn_far", n2, grad_low, up_all, both, down_all, extra, parts, other, other,
            before=(branch, grad_n2, sums),
        )
        grad_bias = order(bias_near, grad_bias, 0)
    else:
        every = jnp.arange(parts, dtype=jnp.int32)
        branch, grad_n2, sums, grad_bias = ffn(
            "ffn", n2, grad_low, up_all, bias_all, down_all, extra, parts, every, every
        )
    output = valid_here * (h1 + branch + b_down)
    grad_h1, grad_gain_ffn = norm_back(grad_n2, h1, scale_two, gain_ffn)
    grad_h1 = grad_h1 + grad_rows
    grad_h1_low = grad_h1.astype(BF)
    if paired:
        grad_far = across(dot_nt(out_far, grad_h1_low).astype(BF))
        grad_near = dot_nt(w_out, grad_h1_low).astype(BF)
        landed = grad_far
    else:
        landed = grad_mixed = lax.all_to_all(
            dot_nt(w_out_all, grad_h1_low).astype(BF), "mp", 0, 1, tiled=True
        )
    sums = out_back(mixed_rows, grad_h1_low, sums, extra, landed)
    small = [jnp.sum(grad_rows, 0), grad_gain_ffn, jnp.sum(grad_h1, 0)]
    part = lax.psum_scatter(
        sums.reshape((2 * parts,) + sums.shape[2:]), ("core", "mp"), scatter_dimension=0, tiled=True
    )[0]
    summed = lax.psum(part, "dpo")

    if paired:
        near = (q_near, k_near, v_near, grad_near, mixed_near, log_near) + tables_near
        far = (q_far, k_far, v_far, grad_far, mixed_far, log_far) + tables_far
        heads = each // HEAD_DIM
        calls = 4
        step = heads // calls
        written = ()
        for i in range(calls):
            written = half_back(
                f"back_far{i}", ends, index, (near, far), i * step, step, written=written,
                after=part if i == calls // 2 else None,
            )
        back_far, partial = written
        back_far = back_far.reshape(3 * each, rows)
        sent = across(dot(back_far, w_qkv, ((0,), (1,))).astype(BF))
        written = ()
        for i in range(2):
            written = half_back(
                f"back_near{i}", ends, index, (near,), i * heads // 2, heads // 2,
                partial=partial, written=written, after=summed if i else None,
            )
        back_near = written[0].reshape(3 * each, rows)
        grad_n1 = dot(back_near, w_qkv, ((0,), (1,))) + sent.astype(F32)
        pairs = [(n1, back_near), (n1_far, back_far)]
    else:
        back = attend_back(ends, query, keys, values, grad_mixed, mixed, logsum, cosine, sine)
        grad_n1 = dot(back, w_qkv, ((0,), (1,))).astype(BF)
        grad_n1 = lax.psum_scatter(grad_n1, "mp", scatter_dimension=0, tiled=True).astype(F32)
        pairs = [(n1_far, back)]
    turned = project_back(pairs, summed)
    grad_qkv = lax.psum(turned, dp).astype(F32)
    sibling = lax.ppermute(summed, "core", [(0, 1), (1, 0)])
    grad_up, grad_down = unpack(core.reshape(1), summed, sibling, hidden)
    own_out, sibling_out = summed[hidden:].astype(F32), sibling[hidden:].astype(F32)
    grad_out = jnp.where(
        core == 0,
        jnp.concatenate([own_out, sibling_out]),
        jnp.concatenate([sibling_out, own_out]),
    )

    grad_h0, grad_gain_attn = norm_back(grad_n1, h0, scale_one, gain_attn)
    grad_h0_low = (grad_h0 + grad_h1).astype(BF)
    grad_w_concat = dot_tn(joined, grad_h0_low).astype(BF)
    small = small + [jnp.sum(grad_h0_low.astype(F32), axis=0), grad_gain_attn]
    small = jnp.concatenate(small + [grad_bias.reshape(-1)]).reshape(-1, width)
    small = jnp.pad(small, ((0, -small.shape[0] % 8), (0, 0)))
    if paired and lax.axis_size("dpo") == 8:
        tail, small = sum_all(grad_w_concat, small, turned)
    else:
        tail, small = lax.psum((grad_w_concat, small), dp + ("mp",))
    grad_inputs, grad_skip = join_back(grad_h0_low, w_concat)
    wide = w_query.shape[1]
    return (
        output,
        grad_inputs,
        grad_skip,
        tail.astype(F32),
        small[3],
        small[4],
        grad_qkv[:, :wide],
        grad_qkv[:, wide : 2 * wide],
        grad_qkv[:, 2 * wide :],
        grad_out,
        small[2],
        small[1],
        grad_up,
        piece(small[5 : 5 + parts * hidden // width].reshape(-1), rank, hidden),
        grad_down,
        small[0],
    )


def solution(mesh):
    dp, mp = mesh.shape["dp"], mesh.shape["mp"]
    mesh = Mesh(mesh.devices.reshape(dp // 2, 2, mp), ("dpo", "core", "mp"))
    rows = P(("dpo", "core", "mp"), None)
    columns = P(None, "mp")
    upright = P("mp", None)
    return jax.shard_map(
        body,
        mesh=mesh,
        in_specs=(
            rows, rows, rows, P(("dpo", "core"), None), P(), P(), P(), columns, columns, columns,
            upright, P(), P(), columns, P("mp"), upright, P(),
        ),
        out_specs=(
            rows, rows, rows, P(), P(), P(), columns, columns, columns,
            upright, P(), P(), columns, P("mp"), upright, P(),
        ),
        check_vma=False,
    )
```

```python
import functools

import jax
import jax.numpy as jnp
from jax import lax
from jax.experimental import pallas as pl
from jax.experimental.pallas import tpu as pltpu
from jax.sharding import Mesh
from jax.sharding import PartitionSpec as P

HEAD_DIM = 64
HALF = HEAD_DIM // 2
EPS = 1e-06
FIRST_LEAST = 3712
FIRST_MOST = 3840
SEGS = 16
LOG2E = 1.4426950408889634
LN2 = 0.6931471805599453
VMEM = 60 * 2**20

BF = jnp.bfloat16
F32 = jnp.float32


def dot(left, right, dims=((1,), (0,))):
    return lax.dot_general(left, right, (dims, ((), ())), preferred_element_type=F32)


def dot_tn(left, right):
    return dot(left, right, ((0,), (0,)))


def dot_nt(left, right):
    return dot(left, right, ((1,), (1,)))


def layout(lengths_row, count):
    ends = jnp.cumsum(lengths_row)
    starts = ends - lengths_row
    places = jnp.arange(count, dtype=jnp.int32)
    seg = jnp.sum((places[:, None] >= ends[None, :]).astype(jnp.int32), axis=1)
    owner = seg[:, None] == jnp.arange(lengths_row.shape[0], dtype=jnp.int32)[None, :]
    start_of = jnp.sum(jnp.where(owner, starts[None, :], 0), axis=1)
    pos = (places - start_of).astype(F32)
    valid = (places < ends[-1]).astype(F32)
    return (ends.astype(jnp.int32), pos, valid)


def tables(pos):
    freq = jnp.exp(-jnp.log(10000.0) * jnp.arange(HALF, dtype=F32) * 2.0 / HEAD_DIM)
    angle = freq[:, None] * pos[None, :]
    return (jnp.cos(angle), jnp.sin(angle))


def norm_back(grad, stream, scale, gain):
    tilted = grad * gain
    grad_gain = jnp.sum(grad * stream * scale, axis=0)
    grad_stream = scale * tilted - stream * scale**3 * jnp.mean(
        tilted * stream, axis=-1, keepdims=True
    )
    return (grad_stream, grad_gain)


def params():
    return pltpu.CompilerParams(vmem_limit_bytes=VMEM)


def cost(flops, moved):
    return pl.CostEstimate(flops=flops // 64, bytes_accessed=moved // 64, transcendentals=0)


def project_kernel(x_ref, w_ref, cos_ref, sin_ref, q_ref, k_ref, v_ref):
    x = x_ref[...]
    c, s = cos_ref[...], sin_ref[...]
    width = q_ref.shape[0]
    for out, first, factor in ((q_ref, 0, 0.125 * LOG2E), (k_ref, width, 1.0)):
        t = dot_nt(w_ref[first : first + width, :], x)
        for h in range(0, width, HEAD_DIM):
            a, b = t[h : h + HALF], t[h + HALF : h + HEAD_DIM]
            out[h : h + HALF, :] = ((a * c - b * s) * factor).astype(BF)
            out[h + HALF : h + HEAD_DIM, :] = ((b * c + a * s) * factor).astype(BF)
    v_ref[...] = dot_nt(w_ref[2 * width :, :], x).astype(BF)


def project(x, w, cosine, sine):
    count, depth = x.shape
    width = w.shape[0] // 3
    block = min(512, count)
    table = pl.BlockSpec((HALF, block), lambda i: (0, i))
    out = pl.BlockSpec((width, block), lambda i: (0, i))
    return pl.pallas_call(
        project_kernel,
        grid=(count // block,),
        in_specs=[
            pl.BlockSpec((block, depth), lambda i: (i, 0)),
            pl.BlockSpec(w.shape, lambda i: (0, 0)),
            table,
            table,
        ],
        out_specs=[out] * 3,
        out_shape=[jax.ShapeDtypeStruct((width, count), BF)] * 3,
        compiler_params=params(),
        name="project",
    )(x, w, cosine, sine)


def segments(ends_ref, first, count):
    pos = lax.broadcasted_iota(jnp.int32, (1, count), 1) + first
    seg = jnp.zeros((1, count), jnp.int32)
    for i in range(ends_ref.shape[0]):
        seg = seg + (pos >= ends_ref[i]).astype(jnp.int32)
    return lax.broadcasted_iota(jnp.int32, (SEGS, 1), 0) == seg


def zeros(rows, count):
    return jnp.zeros((rows, count), F32)


def key_pieces(count):
    if count == 4096:
        main = [(k0, 384) for k0 in range(0, FIRST_MOST, 384)]
        whole = [(k0, 1024) for k0 in range(0, count, 1024)]
        return [
            (0, 2048, main),
            (2048, 1536, main),
            (3584, 256, whole),
            (FIRST_MOST, 256, [(FIRST_LEAST, count - FIRST_LEAST)]),
        ]
    step = min(512, count)
    every = [(k0, step) for k0 in range(0, count, step)]
    return [(q0, step, every) for q0 in range(0, count, step)]


def attend_kernel(cut, ends_ref, part_ref, q_ref, k_ref, v_ref, o_ref, l_ref, kaug, qaug, vaug):
    count = k_ref.shape[1]
    here = q_ref.shape[1]
    part = part_ref[0]
    same = segments(ends_ref, 0, count)
    kaug[...] = (
        jnp.concatenate([k_ref[...].astype(F32), jnp.where(same, 0.0, -1e30), zeros(48, count)], 0)
        .T.astype(BF)
    )
    mine = segments(ends_ref, part * here, here)
    qaug[...] = jnp.concatenate(
        [q_ref[...].astype(F32), jnp.where(mine, 1.0, 0.0), zeros(48, here)], 0
    ).astype(BF)
    first = lax.broadcasted_iota(jnp.int32, (SEGS, count), 0) == 0
    vaug[...] = jnp.concatenate([v_ref[...].astype(F32), jnp.where(first, 1.0, 0.0)], 0).astype(BF)

    def block(q0, width, pieces):
        queries = qaug[:, q0 : q0 + width]
        top = jnp.full((1, width), -jnp.inf, F32)
        acc = jnp.zeros((HEAD_DIM + SEGS, width), F32)
        for k0, n in pieces:
            scores = dot(kaug[k0 : k0 + n, :], queries)
            higher = jnp.maximum(top, jnp.max(scores, axis=0, keepdims=True))
            probs = jnp.exp2(scores - higher).astype(BF)
            acc = acc * jnp.exp2(top - higher) + dot(vaug[:, k0 : k0 + n], probs)
            top = higher
        total = acc[HEAD_DIM : HEAD_DIM + 1]
        o_ref[:, q0 : q0 + width] = (acc[:HEAD_DIM] / total).astype(BF)
        l_ref[0, :, q0 : q0 + width] = top + jnp.log2(total)

    pieces = key_pieces(count)
    for p in range(cut):
        low, high = p * here, (p + 1) * here

        @pl.when(part == p)
        def _():
            for q0, width, keys in pieces:
                if low <= q0 < high:
                    block(q0 - low, width, keys)


def attend(ends, part, query, keys, values, cut):
    rows, count = query.shape
    heads = rows // HEAD_DIM
    here = count // cut
    whole = pl.BlockSpec((HEAD_DIM, count), lambda h, e, p: (h, 0))
    return pl.pallas_call(
        functools.partial(attend_kernel, cut),
        grid_spec=pltpu.PrefetchScalarGridSpec(
            num_scalar_prefetch=2,
            grid=(heads,),
            in_specs=[
                pl.BlockSpec((HEAD_DIM, here), lambda h, e, p: (h, p[0])),
                whole,
                whole,
            ],
            out_specs=[
                pl.BlockSpec((HEAD_DIM, here), lambda h, e, p: (h, 0)),
                pl.BlockSpec((1, 1, here), lambda h, e, p: (h, 0, 0)),
            ],
            scratch_shapes=[
                pltpu.VMEM((count, 128), BF),
                pltpu.VMEM((128, here), BF),
                pltpu.VMEM((HEAD_DIM + SEGS, count), BF),
            ],
        ),
        out_shape=[
            jax.ShapeDtypeStruct((rows, here), BF),
            jax.ShapeDtypeStruct((heads, 1, here), F32),
        ],
        compiler_params=params(),
        name="attend",
        cost_estimate=cost(4 * rows * here * count, 8 * rows * count),
    )(ends, part, query, keys, values)


def local_segments(ends_ref, part, count):
    return segments(ends_ref, part * count, count)


def spans(first, last, step):
    return [(k0, min(step, last - k0)) for k0 in range(first, last, step)]


def regions(query_part, key_parts, half):
    edge, start = FIRST_MOST - half, FIRST_LEAST - half

    def keys(first, last, p):
        return [(p, k0, n) for k0, n in spans(first, last, 1024)]

    if query_part == 0:
        found = []
        for p in key_parts:
            found += keys(0, half, 0) if p == 0 else keys(0, edge, 1)
        return [(0, half, found)]
    low = edge - 256
    if list(key_parts) == [0]:
        return [(0, edge, keys(0, half, 0)), (edge, half - edge, [])]
    main, mixed, last = [], [], []
    for p in key_parts:
        if p == 0:
            main += keys(0, half, 0)
            mixed += keys(0, half, 0)
        else:
            main += keys(0, edge, 1)
            mixed += keys(0, half, 1)
            last += [(1, start, half - start)]
    return [(0, low, main), (low, 256, mixed), (edge, half - edge, last)]


def half_kernel(query_far, key_sides, given, last, ends_ref, part_ref, *refs):
    refs = list(refs)
    q_ref = refs.pop(0)
    kv = {side: (refs.pop(0), refs.pop(0)) for side in key_sides}
    acc_in, top_in = (refs.pop(0), refs.pop(0)) if given else (None, None)
    out_ref, top_ref = refs.pop(0), refs.pop(0)
    qaug = refs.pop(0)
    kaug = {side: refs.pop(0) for side in key_sides}
    vaug = {side: refs.pop(0) for side in key_sides}
    half = q_ref.shape[1]
    rank = part_ref[0]

    @pl.when(pl.program_id(0) == 0)
    def _():
        for side in key_sides:
            same = local_segments(ends_ref, rank if side == 0 else 1 - rank, half)
            blank = zeros(HEAD_DIM, half)
            kaug[side][...] = (
                jnp.concatenate([blank, jnp.where(same, 0.0, -1e30), zeros(48, half)], 0)
                .T.astype(BF)
            )
            first = lax.broadcasted_iota(jnp.int32, (SEGS, half), 0) == 0
            vaug[side][HEAD_DIM:, :] = jnp.where(first, 1.0, 0.0).astype(BF)
        mine = local_segments(ends_ref, 1 - rank if query_far else rank, half)
        qaug[HEAD_DIM:, :] = jnp.concatenate(
            [jnp.where(mine, 1.0, 0.0), zeros(48, half)], 0
        ).astype(BF)

    for side in key_sides:
        kaug[side][:, :HEAD_DIM] = kv[side][0][...].T
        vaug[side][:HEAD_DIM, :] = kv[side][1][...]
    qaug[:HEAD_DIM, :] = q_ref[...]

    for here in range(2):
        query_part = 1 - here if query_far else here
        part_of = {side: here if side == 0 else 1 - here for side in key_sides}
        side_of = {p: side for side, p in part_of.items()}

        @pl.when(rank == here)
        def _():
            for q0, width, pieces in regions(query_part, list(side_of), half):
                there = slice(q0, q0 + width)
                queries = qaug[:, there]
                if given:
                    top, acc = top_in[0, :, there], acc_in[0, :, there]
                else:
                    top = jnp.full((1, width), -jnp.inf, F32)
                    acc = jnp.zeros((HEAD_DIM + SEGS, width), F32)
                for p, k0, n in pieces:
                    side = side_of[p]
                    scores = dot(kaug[side][k0 : k0 + n, :], queries)
                    higher = jnp.maximum(top, jnp.max(scores, axis=0, keepdims=True))
                    probs = jnp.exp2(scores - higher).astype(BF)
                    acc = acc * jnp.exp2(top - higher) + dot(vaug[side][:, k0 : k0 + n], probs)
                    top = higher
                if last:
                    total = acc[HEAD_DIM : HEAD_DIM + 1]
                    out_ref[:, there] = (acc[:HEAD_DIM] / total).astype(BF)
                    top_ref[0, :, there] = top + jnp.log2(total)
                else:
                    out_ref[0, :, there] = acc
                    top_ref[0, :, there] = top


def attend_half(name, ends, rank, query, query_far, keys, carry=None, last=True):
    rows, half = query.shape
    heads = rows // HEAD_DIM
    sides = sorted(keys)
    head = pl.BlockSpec((HEAD_DIM, half), lambda h, e, r: (h, 0))
    tall = pl.BlockSpec((1, HEAD_DIM + SEGS, half), lambda h, e, r: (h, 0, 0))
    line = pl.BlockSpec((1, 1, half), lambda h, e, r: (h, 0, 0))
    operands = [query]
    for side in sides:
        operands += list(keys[side])
    specs = [head] * len(operands)
    if carry is not None:
        operands += list(carry)
        specs += [tall, line]
    return pl.pallas_call(
        functools.partial(half_kernel, query_far, sides, carry is not None, last),
        grid_spec=pltpu.PrefetchScalarGridSpec(
            num_scalar_prefetch=2,
            grid=(heads,),
            in_specs=specs,
            out_specs=[head if last else tall, line],
            scratch_shapes=[pltpu.VMEM((128, half), BF)]
            + [pltpu.VMEM((half, 128), BF)] * len(sides)
            + [pltpu.VMEM((HEAD_DIM + SEGS, half), BF)] * len(sides),
        ),
        out_shape=[
            jax.ShapeDtypeStruct((rows, half), BF)
            if last
            else jax.ShapeDtypeStruct((heads, HEAD_DIM + SEGS, half), F32),
            jax.ShapeDtypeStruct((heads, 1, half), F32),
        ],
        compiler_params=params(),
        name=name,
        cost_estimate=cost(16 * rows * half * half * len(sides), 8 * rows * half),
    )(ends, rank, *operands)


def split3(x):
    a = x.astype(BF).astype(F32)
    b = (x - a).astype(BF).astype(F32)
    row = lax.broadcasted_iota(jnp.int32, (SEGS, 1), 0)
    return jnp.where(row == 0, a, jnp.where(row == 1, b, jnp.where(row == 2, x - a - b, 0.0)))


def attend_back_kernel(
    ends_ref, q_ref, k_ref, v_ref, g_ref, o_ref, l_ref, cos_ref, sin_ref, d_ref,
    kaug, vaug, qaug, gaug, pair, dq,
):
    count = k_ref.shape[1]
    same = segments(ends_ref, 0, count)
    row = lax.broadcasted_iota(jnp.int32, (SEGS, count), 0)
    shift = jnp.where(row < 3, 1.0, 0.0)
    g = g_ref[...].astype(F32)
    q = q_ref[...].astype(F32)
    delta = jnp.sum(g * o_ref[...].astype(F32), axis=0, keepdims=True)
    kaug[...] = (
        jnp.concatenate(
            [k_ref[...].astype(F32), jnp.where(same, 0.0, -1e30), shift, zeros(32, count)], 0
        )
        .T.astype(BF)
    )
    vaug[...] = (
        jnp.concatenate([v_ref[...].astype(F32), shift, zeros(48, count)], 0).T.astype(BF)
    )
    qaug[...] = jnp.concatenate(
        [q, jnp.where(same, 1.0, 0.0), split3(-l_ref[0]), zeros(32, count)], 0
    ).astype(BF)
    gaug[...] = jnp.concatenate([g, split3(-delta), zeros(48, count)], 0).astype(BF)
    pair[...] = jnp.concatenate([q, g], 0).T.astype(BF)
    dq[...] = jnp.zeros_like(dq)

    def turn(grad, c, s, factor):
        a, b = grad[:HALF], grad[HALF:]
        return (
            jnp.concatenate([a * c + b * s, b * c - a * s], 0) * factor
        ).astype(BF)

    def chunk(k0, n, queries):
        where = pl.ds(k0, n)
        kb, vb, kt = kaug[where, :], vaug[where, :], k_ref[:, where]
        dk = jnp.zeros((n, HEAD_DIM), F32)
        dv = jnp.zeros((n, HEAD_DIM), F32)
        for q0, width in queries:
            there = slice(q0, q0 + width)
            probs = jnp.exp2(dot(kb, qaug[:, there]))
            tilt = (probs * dot(vb, gaug[:, there])).astype(BF)
            dv = dv + dot(probs.astype(BF), pair[there, HEAD_DIM:])
            dk = dk + dot(tilt, pair[there, :HEAD_DIM])
            dq[:, there] += dot(kt, tilt)
        c, s = cos_ref[:, where], sin_ref[:, where]
        d_ref[1, 0, :, where] = turn(dk.T, c, s, LN2)
        d_ref[2, 0, :, where] = dv.T.astype(BF)

    if count == 4096:
        main = [(q0, 1920) for q0 in range(0, FIRST_MOST, 1920)]

        def step(i, carry):
            chunk(pl.multiple_of(i * 512, 512), 512, main)
            return carry

        lax.fori_loop(0, 7, step, 0)
        chunk(3584, 256, [(q0, 1024) for q0 in range(0, count, 1024)])
        chunk(FIRST_MOST, count - FIRST_MOST, [(3584, 512)])
    else:
        size = min(512, count)

        def step(i, carry):
            chunk(pl.multiple_of(i * size, size), size, [(q, size) for q in range(0, count, size)])
            return carry

        lax.fori_loop(0, count // size, step, 0)
    d_ref[0, 0] = turn(dq[...], cos_ref[...], sin_ref[...], 0.125)


def attend_back(ends, query, keys, values, grad, mixed, logsum, cosine, sine):
    rows, count = query.shape
    heads = rows // HEAD_DIM
    whole = pl.BlockSpec((HEAD_DIM, count), lambda h, e: (h, 0))
    table = pl.BlockSpec((HALF, count), lambda h, e: (0, 0))
    out = pl.pallas_call(
        attend_back_kernel,
        grid_spec=pltpu.PrefetchScalarGridSpec(
            num_scalar_prefetch=1,
            grid=(heads,),
            in_specs=[whole] * 5
            + [pl.BlockSpec((1, 1, count), lambda h, e: (h, 0, 0)), table, table],
            out_specs=pl.BlockSpec((3, 1, HEAD_DIM, count), lambda h, e: (0, h, 0, 0)),
            scratch_shapes=[
                pltpu.VMEM((count, 128), BF),
                pltpu.VMEM((count, 128), BF),
                pltpu.VMEM((128, count), BF),
                pltpu.VMEM((128, count), BF),
                pltpu.VMEM((count, 128), BF),
                pltpu.VMEM((HEAD_DIM, count), F32),
            ],
        ),
        out_shape=jax.ShapeDtypeStruct((3, heads, HEAD_DIM, count), BF),
        compiler_params=params(),
        name="attend_back",
        cost_estimate=cost(10 * rows * count * count, 16 * rows * count),
    )(ends, query, keys, values, grad, mixed, logsum, cosine, sine)
    return out.reshape(3 * rows, count)


def turn_back(grad, c, s, factor):
    a, b = grad[:HALF], grad[HALF:]
    return (jnp.concatenate([a * c + b * s, b * c - a * s], 0) * factor).astype(BF)


def back_chunks(key_part, query_parts, half):
    edge = FIRST_MOST - half
    low = edge - 256
    found = []
    if key_part == 0:
        queries = []
        for p in query_parts:
            queries += [(p, 0, half if p == 0 else edge)]
        return [(0, half, 512, queries)]
    main = [(p, 0, half if p == 0 else edge) for p in query_parts]
    found.append((0, low, 512, main))
    found.append((low, 256, 256, [(p, 0, half) for p in query_parts]))
    if 1 in query_parts:
        found.append((edge, half - edge, 256, [(1, low, half - low)]))
    return found


def half_back_kernel(near_only, given_partial, finish, ends_ref, part_ref, *refs):
    refs = list(refs)
    sides = (0,) if near_only else (0, 1)
    given = {side: [refs.pop(0) for _ in range(8)] for side in sides}
    partial_in = refs.pop(0) if given_partial else None
    while len(refs) > (1 if near_only else 2) + 7:
        refs.pop(0)
    out_ref = None if near_only else refs.pop(0)
    near_ref = refs.pop(0)
    kaug, vaug, qaug, gaug, pair, dq, sums = refs
    rank = part_ref[0]
    half = given[0][0].shape[1]

    @pl.when(pl.program_id(0) == 0)
    def _():
        row = lax.broadcasted_iota(jnp.int32, (SEGS, half), 0)
        shift = jnp.where(row < 3, 1.0, 0.0)
        blank = zeros(HEAD_DIM, half)
        for side in sides:
            there = slice(side * half, side * half + half)
            same = local_segments(ends_ref, rank if side == 0 else 1 - rank, half)
            kaug[there, :] = (
                jnp.concatenate([blank, jnp.where(same, 0.0, -1e30), shift, zeros(32, half)], 0)
                .T.astype(BF)
            )
            vaug[there, :] = jnp.concatenate([blank, shift, zeros(48, half)], 0).T.astype(BF)
            qaug[HEAD_DIM:, there] = jnp.concatenate(
                [jnp.where(same, 1.0, 0.0), zeros(48, half)], 0
            ).astype(BF)
            gaug[HEAD_DIM:, there] = blank.astype(BF)

    for side in sides:
        q_ref, k_ref, v_ref, g_ref, o_ref, l_ref = given[side][:6]
        there = slice(side * half, side * half + half)
        g = g_ref[...]
        q = q_ref[...]
        delta = jnp.sum(g.astype(F32) * o_ref[...].astype(F32), axis=0, keepdims=True)
        kaug[there, :HEAD_DIM] = k_ref[...].T
        vaug[there, :HEAD_DIM] = v_ref[...].T
        qaug[:HEAD_DIM, there] = q
        qaug[HEAD_DIM + SEGS : HEAD_DIM + 2 * SEGS, there] = split3(-l_ref[0]).astype(BF)
        gaug[:HEAD_DIM, there] = g
        gaug[HEAD_DIM : HEAD_DIM + SEGS, there] = split3(-delta).astype(BF)
        pair[there, :] = jnp.concatenate([q, g], 0).T
    dq[...] = jnp.zeros_like(dq)
    if given_partial:
        dq[:, :half] = partial_in[0, 0]
        sums[...] = partial_in[1:, 0]
    else:
        sums[...] = jnp.zeros_like(sums)

    def chunk(side, k0, n, queries):
        where = pl.ds(side * half + k0, n)
        kb, vb, kt = kaug[where, :], vaug[where, :], given[side][1][:, pl.ds(k0, n)]
        dk = jnp.zeros((n, HEAD_DIM), F32)
        dv = jnp.zeros((n, HEAD_DIM), F32)
        for q0, width in queries:
            there = slice(q0, q0 + width)
            probs = jnp.exp2(dot(kb, qaug[:, there]))
            tilt = (probs * dot(vb, gaug[:, there])).astype(BF)
            dv = dv + dot(probs.astype(BF), pair[there, HEAD_DIM:])
            dk = dk + dot(tilt, pair[there, :HEAD_DIM])
            dq[:, there] += dot(kt, tilt)
        dk, dv = dk.T, dv.T
        if side == 0:
            sums[0, :, pl.ds(k0, n)] += dk
            sums[1, :, pl.ds(k0, n)] += dv
            return
        c, s = given[side][6][:, pl.ds(k0, n)], given[side][7][:, pl.ds(k0, n)]
        out_ref[1, 0, :, pl.ds(k0, n)] = turn_back(dk, c, s, LN2)
        out_ref[2, 0, :, pl.ds(k0, n)] = dv.astype(BF)

    for here in range(2):

        @pl.when(rank == here)
        def _():
            side_of = {here: 0, 1 - here: 1}
            for key_part, side in side_of.items():
                if near_only and side == 1:
                    continue
                if near_only:
                    query_parts = [here]
                else:
                    query_parts = [0, 1] if side == 1 else [1 - here]
                for k0, total, n, queries in back_chunks(key_part, query_parts, half):
                    spread = [(side_of[p] * half + q0, width) for p, q0, width in queries]
                    if total == n:
                        chunk(side, k0, n, spread)
                        continue

                    def step(i, carry):
                        chunk(side, pl.multiple_of(k0 + i * n, n), n, spread)
                        return carry

                    lax.fori_loop(0, total // n, step, 0)

    if not near_only:
        out_ref[0, 0] = turn_back(dq[:, half:], given[1][6][...], given[1][7][...], 0.125)
    if finish:
        c, s = given[0][6][...], given[0][7][...]
        near_ref[0, 0] = turn_back(dq[:, :half], c, s, 0.125)
        near_ref[1, 0] = turn_back(sums[0], c, s, LN2)
        near_ref[2, 0] = sums[1].astype(BF)
    else:
        near_ref[0, 0] = dq[:, :half]
        near_ref[1:, 0] = sums[...]


def half_back(name, ends, rank, sides, first, count, finish, partial=None, written=(), after=None):
    rows, half = sides[0][0].shape
    heads = rows // HEAD_DIM
    near_only = len(sides) == 1
    head = pl.BlockSpec((HEAD_DIM, half), lambda h, e, r: (h + first, 0))
    line = pl.BlockSpec((1, 1, half), lambda h, e, r: (h + first, 0, 0))
    table = pl.BlockSpec((HALF, half), lambda h, e, r: (0, 0))
    block = pl.BlockSpec((3, 1, HEAD_DIM, half), lambda h, e, r: (0, h + first, 0, 0))
    anywhere = pl.BlockSpec(memory_space=pl.ANY)
    operands, specs = [], []
    for side in sides:
        operands += list(side)
        specs += [head] * 5 + [line, table, table]
    result = jax.ShapeDtypeStruct((3, heads, HEAD_DIM, half), BF)
    if partial is not None:
        operands.append(partial)
        specs.append(block)
    aliases = {}
    for i, array in enumerate(written):
        if array is not None:
            aliases[2 + len(operands)] = i
            operands.append(array)
            specs.append(anywhere)
    if after is not None:
        operands.append(after)
        specs.append(anywhere)
    near_result = result if finish else jax.ShapeDtypeStruct(result.shape, F32)
    out_shape = [near_result] if near_only else [result, near_result]
    out_specs = [block] * len(out_shape)
    wide = half * len(sides)
    return pl.pallas_call(
        functools.partial(half_back_kernel, near_only, partial is not None, finish),
        grid_spec=pltpu.PrefetchScalarGridSpec(
            num_scalar_prefetch=2,
            grid=(count,),
            in_specs=specs,
            out_specs=out_specs,
            scratch_shapes=[
                pltpu.VMEM((wide, 128), BF),
                pltpu.VMEM((wide, 128), BF),
                pltpu.VMEM((128, wide), BF),
                pltpu.VMEM((128, wide), BF),
                pltpu.VMEM((wide, 128), BF),
                pltpu.VMEM((HEAD_DIM, wide), F32),
                pltpu.VMEM((2, HEAD_DIM, half), F32),
            ],
        ),
        out_shape=out_shape,
        input_output_aliases=aliases,
        compiler_params=params(),
        name=name,
        cost_estimate=cost(40 * count * HEAD_DIM * half * half * (1 if near_only else 3), 40 * count * HEAD_DIM * half),
    )(ends, rank, *operands)


def ffn_kernel(step, given, src_ref, dst_ref, n_ref, g_ref, up_ref, bias_ref, down_ref, *refs):
    branch_in, dn_in = refs[:2] if given else (None, None)
    branch_ref, dn_ref, dw_ref, dbias_ref, branch, dn, sems = refs[3 if given else 0 :]

    rows, depth = n_ref.shape
    steps = [(i, slice(r0, r0 + step)) for i, r0 in enumerate(range(0, rows, step))]
    opening = (pl.program_id(0) == 0) & (pl.program_id(1) == 0)
    closing = (pl.program_id(0) == pl.num_programs(0) - 1) & (
        pl.program_id(1) == pl.num_programs(1) - 1
    )

    def moves(i, part, out):
        if out:
            pairs = ((branch, branch_ref), (dn, dn_ref))
        else:
            pairs = ((branch_in, branch), (dn_in, dn))
        return [
            pltpu.make_async_copy(src.at[part, :], dst.at[part, :], sems.at[j, i])
            for j, (src, dst) in enumerate(pairs)
        ]

    @pl.when(opening)
    def _():
        if given:
            for i, part in steps:
                for move in moves(i, part, False):
                    move.start()
        else:
            branch[...] = jnp.zeros_like(branch)
            dn[...] = jnp.zeros_like(dn)

    up = up_ref[...].reshape(depth, -1)
    down, bias = down_ref[0, 0], bias_ref[0].astype(F32)
    width = up.shape[1]
    dup = jnp.zeros((width, depth), F32)
    ddown = jnp.zeros((width, depth), F32)
    dbias = jnp.zeros((1, width), F32)
    for i, part in steps:
        x, y = n_ref[part, :], g_ref[part, :]
        u = dot(x, up) + bias
        dz = dot_nt(y, down)
        normal = 0.5 * (1.0 + lax.erf(u * 0.7071067811865476))
        density = jnp.exp(-0.5 * u * u) * 0.3989422804014327
        z = (u * normal).astype(BF)
        du = (dz * (normal + u * density)).astype(BF)
        if given:

            @pl.when(opening)
            def _():
                for move in moves(i, part, False):
                    move.wait()

        branch[part, :] += dot(z, down)
        dn[part, :] += dot_nt(du, up)

        @pl.when(closing)
        def _():
            for move in moves(i, part, True):
                move.start()

        ddown = ddown + dot_tn(z, y)
        dup = dup + dot_tn(du, x)
        dbias = dbias + jnp.sum(du.astype(F32), axis=0, keepdims=True)
    dw_ref[0, 0, :width, :] = dup.astype(BF)
    dw_ref[0, 0, width:, :] = ddown.astype(BF)
    dbias_ref[0] = dbias

    @pl.when(closing)
    def _():
        for i, part in steps:
            for move in moves(i, part, True):
                move.wait()


def ffn_block(hidden):
    return min(512, hidden // 2)


def ffn(name, n2, grad, up, bias, down, extra, parts, src, dst, before=None):
    rows, depth = n2.shape
    hidden = up.shape[3]
    block = ffn_block(hidden)
    per = hidden // 2 // block
    step = min(512, rows)
    once = pl.BlockSpec(
        (rows, depth), lambda p, i, f, t: (0, 0), pipeline_mode=pl.Buffered(1)
    )
    anywhere = pl.BlockSpec(memory_space=pl.ANY)
    operands = [n2, grad, up, bias, down] + ([] if before is None else list(before))
    return pl.pallas_call(
        functools.partial(ffn_kernel, step, before is not None),
        grid_spec=pltpu.PrefetchScalarGridSpec(
            num_scalar_prefetch=2,
            grid=(src.shape[0], 2 * per),
            in_specs=[
                once,
                once,
                pl.BlockSpec((2, 1, depth // 2, block), lambda p, i, f, t: (0, f[p], 0, i)),
                pl.BlockSpec((1, 1, block), lambda p, i, f, t: (f[p], 0, i)),
                pl.BlockSpec(
                    (1, 1, block, depth), lambda p, i, f, t: (i // per, f[p], i % per, 0)
                ),
            ]
            + ([] if before is None else [anywhere] * 3),
            out_specs=[anywhere] * 2
            + [
                pl.BlockSpec(
                    (1, 1, 2 * block, depth), lambda p, i, f, t: (i // per, t[p], i % per, 0)
                ),
                pl.BlockSpec((1, 1, block), lambda p, i, f, t: (p, 0, i)),
            ],
            scratch_shapes=[pltpu.VMEM((rows, depth), F32)] * 2
            + [pltpu.SemaphoreType.DMA((2, rows // step))],
        ),
        out_shape=[jax.ShapeDtypeStruct((rows, depth), F32)] * 2
        + [
            jax.ShapeDtypeStruct((2, parts, hidden + extra, depth), BF),
            jax.ShapeDtypeStruct((src.shape[0], 1, hidden), F32),
        ],
        input_output_aliases={} if before is None else {9: 2},
        compiler_params=params(),
        name=name,
        cost_estimate=cost(12 * rows * depth * hidden * src.shape[0], 8 * depth * hidden * src.shape[0]),
    )(src, dst, *operands)


def out_back_kernel(mixed_ref, grad_ref, sums_ref, out_ref):
    out_ref[0, 0] = dot(mixed_ref[...], grad_ref[...]).astype(BF)


def out_back(mixed_rows, grad, sums, extra):
    heads, rows = mixed_rows.shape
    _, parts, total, depth = sums.shape
    return pl.pallas_call(
        out_back_kernel,
        grid=(parts, 2),
        in_specs=[
            pl.BlockSpec((extra, rows), lambda p, c: (2 * p + c, 0)),
            pl.BlockSpec((rows, depth), lambda p, c: (0, 0)),
            pl.BlockSpec(memory_space=pl.ANY),
        ],
        out_specs=pl.BlockSpec((1, 1, extra, depth), lambda p, c: (c, p, total // extra - 1, 0)),
        out_shape=jax.ShapeDtypeStruct(sums.shape, BF),
        input_output_aliases={2: 0},
        compiler_params=params(),
        name="out_back",
        cost_estimate=cost(2 * rows * depth * heads, 2 * heads * depth),
    )(mixed_rows, grad, sums)


def project_back_kernel(*refs):
    out_ref = refs[-1]
    pairs = refs[:-2]
    total = dot(pairs[1][...], pairs[0][...])
    for i in range(2, len(pairs), 2):
        total = total + dot(pairs[i + 1][...], pairs[i][...])
    out_ref[...] = total.astype(BF)


def project_back(pairs, after):
    total = pairs[0][1].shape[0]
    depth = pairs[0][0].shape[1]
    block = total // 3
    specs, operands = [], []
    for x, grad in pairs:
        specs += [
            pl.BlockSpec(x.shape, lambda i: (0, 0)),
            pl.BlockSpec((block, x.shape[0]), lambda i: (i, 0)),
        ]
        operands += [x, grad]
    return pl.pallas_call(
        project_back_kernel,
        grid=(3,),
        in_specs=specs + [pl.BlockSpec(memory_space=pl.ANY)],
        out_specs=pl.BlockSpec((block, depth), lambda i: (i, 0)),
        out_shape=jax.ShapeDtypeStruct((total, depth), BF),
        compiler_params=params(),
        name="project_back",
        cost_estimate=cost(4 * pairs[0][0].shape[0] * depth * total, 8 * depth * total),
    )(*operands, after)


def turn_kernel(x_ref, *out_refs):
    for i, out_ref in enumerate(out_refs):

        @pl.when(pl.program_id(0) == i)
        def _():
            out_ref[...] = x_ref[...].astype(F32).T


def turn(x, parts):
    rows, depth = x.shape
    block = rows // parts
    return pl.pallas_call(
        turn_kernel,
        grid=(parts,),
        in_specs=[pl.BlockSpec((block, depth), lambda i: (i, 0))],
        out_specs=[pl.BlockSpec((depth, block), lambda i: (0, 0))] * parts,
        out_shape=[jax.ShapeDtypeStruct((depth, block), F32)] * parts,
        compiler_params=params(),
        name="turn",
        cost_estimate=cost(rows * depth, 6 * rows * depth),
    )(x)


MESH = pl.DeviceIdType.MESH


def sum_all_kernel(
    big_ref, side_ref, small_ref, out_ref, side_out_ref, small_out_ref,
    buf, done, core_in, x_in, y_in, z_in, side, side_done, side_core, side_y, side_z,
    small, small_in, small_z, local, send, recv, side_send, side_recv, small_send, small_recv,
):
    o, c, m = lax.axis_index("dpo"), lax.axis_index("core"), lax.axis_index("mp")
    y, z = lax.rem(o, 2), lax.div(o, 2)
    zs = 4
    half = buf.shape[0] // 2
    quarter, eighth, last = half // 2, half // 4, half // 16
    side_half = side.shape[0] // 2
    side_quarter, side_last = side_half // 2, side_half // 8
    sibling = (o, 1 - c, m)
    across = (o, c, 1 - m)
    beside = (z * 2 + 1 - y, c, m)
    others = [lax.rem(z + d, zs) for d in range(1, zs)]

    def along(j):
        return (j * 2 + y, c, m)

    loads = [
        pltpu.make_async_copy(big_ref, buf, local.at[0]),
        pltpu.make_async_copy(side_ref, side, local.at[1]),
    ]
    for load in loads:
        load.start()
    barrier = pltpu.get_barrier_semaphore()
    for device in [sibling, across, beside] + [along(j) for j in others]:
        pl.semaphore_signal(barrier, inc=1, device_id=device, device_id_type=MESH)
    pl.semaphore_wait(barrier, 6)
    small[0] = small_ref[...]

    started = []

    def go(src, dst, sems, i, device):
        one = pltpu.make_async_remote_copy(
            src_ref=src, dst_ref=dst, send_sem=sems[0].at[i], recv_sem=sems[1].at[i],
            device_id=device, device_id_type=MESH,
        )
        one.start()
        started.append(one)
        return one

    def arrived(dst, sems, i, device):
        pltpu.make_async_remote_copy(
            src_ref=dst, dst_ref=dst, send_sem=sems[0].at[i], recv_sem=sems[1].at[i],
            device_id=device, device_id_type=MESH,
        ).wait_recv()

    def view(of, first, n, unit):
        return of.at[pl.ds(pl.multiple_of(first, unit), n)]

    def rows(first, n, of=buf):
        return view(of, first, n, last)

    def side_rows(first, n, of=side):
        return view(of, first, n, side_last)

    def add(of, first, n, unit, got):
        step = unit if n % 128 or 128 % unit else 128

        def one(i, carry):
            there = pl.ds(pl.multiple_of(first + i * step, unit), step)
            here = pl.ds(pl.multiple_of(i * step, step), step)
            of[there, :] = (of[there, :].astype(F32) + got[here, :].astype(F32)).astype(BF)
            return carry

        lax.fori_loop(0, n // step, one, 0)

    main, extra, tiny = (send, recv), (side_send, side_recv), (small_send, small_recv)
    mine, theirs = c * half, (1 - c) * half
    side_mine, side_theirs = c * side_half, (1 - c) * side_half
    base_far, base = mine + (1 - m) * quarter, mine + m * quarter
    far_y, near_y = base + (1 - y) * eighth, base + y * eighth
    side_far, side_near = side_mine + (1 - y) * side_quarter, side_mine + y * side_quarter
    own, side_own = near_y + z * last, side_near + z * side_last

    loads[0].wait()
    core_a = go(rows(theirs + (1 - m) * quarter, quarter), core_in.at[0], main, 0, sibling)
    loads[1].wait()
    side_a = go(
        side_rows(side_theirs + (1 - y) * side_quarter, side_quarter), side_core.at[0], extra, 0,
        sibling,
    )
    core_b = go(rows(theirs + m * quarter, quarter), core_in.at[1], main, 1, sibling)
    side_b = go(
        side_rows(side_theirs + y * side_quarter, side_quarter), side_core.at[1], extra, 1, sibling
    )
    tiny_core = go(small.at[0], small_in.at[0], tiny, 0, sibling)
    core_a.wait_recv()
    add(buf, base_far, quarter, last, core_in.at[0])
    x_a = go(rows(base_far + (1 - y) * eighth, eighth), x_in.at[0], main, 2, across)
    x_b = go(rows(base_far + y * eighth, eighth), x_in.at[1], main, 3, across)
    side_a.wait_recv()
    add(side, side_far, side_quarter, side_last, side_core.at[0])
    side_c = go(side_rows(side_far, side_quarter), side_y, extra, 2, beside)
    tiny_core.wait_recv()
    small[1] = small[0] + small_in[0]
    tiny_x = go(small.at[1], small_in.at[1], tiny, 1, across)
    core_b.wait_recv()
    add(buf, base, quarter, last, core_in.at[1])
    side_b.wait_recv()
    add(side, side_near, side_quarter, side_last, side_core.at[1])
    x_a.wait_recv()
    add(buf, far_y, eighth, last, x_in.at[0])
    y_a = go(rows(far_y, eighth), y_in, main, 4, beside)
    tiny_x.wait_recv()
    small[2] = small[1] + small_in[1]
    tiny_y = go(small.at[2], small_in.at[2], tiny, 2, beside)
    side_c.wait_recv()
    add(side, side_near, side_quarter, side_last, side_y)
    for j in others:
        go(side_rows(side_near + j * side_last, side_last), side_z.at[z], extra, 3 + z, along(j))
    x_b.wait_recv()
    add(buf, near_y, eighth, last, x_in.at[1])
    y_a.wait_recv()
    add(buf, near_y, eighth, last, y_in)
    for j in others:
        go(rows(near_y + j * last, last), z_in.at[z], main, 5 + z, along(j))
    tiny_y.wait_recv()
    small_z[z] = small[2] + small_in[2]
    for j in others:
        go(small_z.at[z], small_z.at[z], tiny, 3 + z, along(j))
    total = side[pl.ds(pl.multiple_of(side_own, side_last), side_last), :].astype(F32)
    for j in others:
        arrived(side_z.at[j], extra, 3 + j, along(j))
        total = total + side_z[j].astype(F32)
    side_done[pl.ds(pl.multiple_of(side_own, side_last), side_last), :] = total.astype(BF)

    def hand(first, n, i, device):
        there = rows(first, n, done)
        return go(there, there, main, i, device)

    def side_hand(first, n, i, device):
        there = side_rows(first, n, side_done)
        return go(there, there, extra, i, device)

    for j in others:
        side_hand(side_own, side_last, 7 + z, along(j))
    total = buf[pl.ds(pl.multiple_of(own, last), last), :].astype(F32)
    for j in others:
        arrived(z_in.at[j], main, 5 + j, along(j))
        total = total + z_in[j].astype(F32)
    done[pl.ds(pl.multiple_of(own, last), last), :] = total.astype(BF)
    for j in others:
        hand(own, last, 9 + z, along(j))
    for j in others:
        arrived(rows(near_y + j * last, last, done), main, 9 + j, along(j))
    x_back = hand(near_y, eighth, 14, across)
    y_back = hand(near_y, eighth, 13, beside)
    core_back = hand(near_y, eighth, 15, sibling)
    for j in others:
        there = side_rows(side_near + j * side_last, side_last, side_done)
        arrived(there, extra, 7 + j, along(j))
    side_back = side_hand(side_near, side_quarter, 11, beside)
    side_core_back = side_hand(side_near, side_quarter, 12, sibling)
    y_back.wait_recv()
    x_more = hand(far_y, eighth, 16, across)
    core_more = hand(far_y, eighth, 17, sibling)
    x_back.wait_recv()
    core_x = hand(base_far + y * eighth, eighth, 18, sibling)
    side_back.wait_recv()
    side_core_more = side_hand(side_far, side_quarter, 13, sibling)
    x_more.wait_recv()
    core_y = hand(base_far + (1 - y) * eighth, eighth, 19, sibling)
    for j in others:
        arrived(small_z.at[j], tiny, 3 + j, along(j))
    small_out_ref[...] = (small_z[0] + small_z[1]) + (small_z[2] + small_z[3])
    for one in (side_core_back, side_core_more):
        one.wait_recv()
    stores = [pltpu.make_async_copy(side_done, side_out_ref, local.at[1])]
    stores[0].start()
    for one in (core_back, core_more, core_x, core_y):
        one.wait_recv()
    stores.append(pltpu.make_async_copy(done, out_ref, local.at[0]))
    stores[1].start()
    for one in started:
        one.wait_send()
    for store in stores:
        store.wait()


def sum_all(big, side, small):
    rows, width = big.shape
    quarter, eighth, last = rows // 4, rows // 8, rows // 32
    side_quarter, side_last = side.shape[0] // 4, side.shape[0] // 16
    anywhere = pl.BlockSpec(memory_space=pl.ANY)
    whole = pl.BlockSpec(memory_space=pltpu.VMEM)
    dma = pltpu.SemaphoreType.DMA
    return pl.pallas_call(
        sum_all_kernel,
        in_specs=[anywhere, anywhere, whole],
        out_specs=[anywhere, anywhere, whole],
        out_shape=[
            jax.ShapeDtypeStruct(big.shape, BF),
            jax.ShapeDtypeStruct(side.shape, BF),
            jax.ShapeDtypeStruct(small.shape, F32),
        ],
        scratch_shapes=[
            pltpu.VMEM((rows, width), BF),
            pltpu.VMEM((rows, width), BF),
            pltpu.VMEM((2, quarter, width), BF),
            pltpu.VMEM((2, eighth, width), BF),
            pltpu.VMEM((eighth, width), BF),
            pltpu.VMEM((4, last, width), BF),
            pltpu.VMEM(side.shape, BF),
            pltpu.VMEM(side.shape, BF),
            pltpu.VMEM((2, side_quarter, width), BF),
            pltpu.VMEM((side_quarter, width), BF),
            pltpu.VMEM((4, side_last, width), BF),
            pltpu.VMEM((3,) + small.shape, F32),
            pltpu.VMEM((3,) + small.shape, F32),
            pltpu.VMEM((4,) + small.shape, F32),
            dma((2,)),
            dma((20,)),
            dma((20,)),
            dma((14,)),
            dma((14,)),
            dma((7,)),
            dma((7,)),
        ],
        compiler_params=pltpu.CompilerParams(
            collective_id=0, has_side_effects=True, vmem_limit_bytes=VMEM
        ),
        name="sum_all",
        cost_estimate=cost(rows * width, 8 * rows * width),
    )(big, side, small)


def join_back_kernel(grad_ref, w_ref, first_ref, second_ref):
    grad = grad_ref[...]
    width = first_ref.shape[1]
    first_ref[...] = dot_nt(grad, w_ref[:width, :])
    second_ref[...] = dot_nt(grad, w_ref[width:, :])


def join_back(grad, w):
    rows, depth = grad.shape
    width = w.shape[0] // 2
    block = min(256, rows)
    out = pl.BlockSpec((block, width), lambda i: (i, 0))
    return pl.pallas_call(
        join_back_kernel,
        grid=(rows // block,),
        in_specs=[
            pl.BlockSpec((block, depth), lambda i: (i, 0)),
            pl.BlockSpec(w.shape, lambda i: (0, 0)),
        ],
        out_specs=[out, out],
        out_shape=[jax.ShapeDtypeStruct((rows, width), F32)] * 2,
        compiler_params=params(),
        name="join_back",
        cost_estimate=cost(rows * depth * width, 8 * rows * width),
    )(grad, w)


def unpack_kernel(core_ref, own_ref, sibling_ref, up_ref, down_ref):
    mine = core_ref[0] == pl.program_id(0)
    width = down_ref.shape[0]
    block = jnp.where(mine, own_ref[...].astype(F32), sibling_ref[...].astype(F32))
    up_ref[...] = block[:width].T
    down_ref[...] = block[width:]


def unpack(core, own, sibling, hidden):
    depth = own.shape[1]
    block = ffn_block(hidden)
    per = hidden // 2 // block
    piece = pl.BlockSpec((2 * block, depth), lambda c, i, k: (i, 0))
    return pl.pallas_call(
        unpack_kernel,
        grid_spec=pltpu.PrefetchScalarGridSpec(
            num_scalar_prefetch=1,
            grid=(2, per),
            in_specs=[piece, piece],
            out_specs=[
                pl.BlockSpec((depth, block), lambda c, i, k: (0, c * per + i)),
                pl.BlockSpec((block, depth), lambda c, i, k: (c * per + i, 0)),
            ],
        ),
        out_shape=[
            jax.ShapeDtypeStruct((depth, hidden), F32),
            jax.ShapeDtypeStruct((hidden, depth), F32),
        ],
        compiler_params=params(),
        name="unpack",
        cost_estimate=cost(depth * hidden, 12 * depth * hidden),
    )(core, own, sibling)


def body(
    inputs, skip_in, cotangent, lengths, w_concat, b_concat, gain_attn, w_query, w_key, w_value,
    w_out, b_out, gain_ffn, w_up, b_up, w_down, b_down,
):
    parts = lax.axis_size("mp")
    rank = lax.axis_index("mp")
    core = lax.axis_index("core")
    dp = ("dpo", "core")
    rows, width = inputs.shape
    group = rows * parts
    paired = parts == 2 and group == 4096
    ends, pos_all, valid_all = layout(lengths[0], group)
    valid_here = lax.dynamic_slice_in_dim(valid_all, rank * rows, rows, 0)[:, None]
    each, hidden = w_out.shape[0], b_up.shape[0]
    extra = each // 2
    index = rank.reshape(1)
    other = 1 - index
    zero = jnp.zeros((1,), jnp.int32)

    def across(x):
        return lax.ppermute(x, "mp", [(0, 1), (1, 0)])

    def piece(x, i, size, axis=0):
        return lax.dynamic_slice_in_dim(x, i * size, size, axis)

    def order(near, far, axis):
        return jnp.where(
            rank == 0, jnp.concatenate([near, far], axis), jnp.concatenate([far, near], axis)
        )

    joined = jnp.concatenate([inputs, skip_in], axis=1)
    h0 = dot(joined, w_concat) + b_concat
    scale_one = lax.rsqrt(jnp.mean(h0 * h0, axis=-1, keepdims=True) + EPS)
    n1 = (h0 * scale_one * gain_attn).astype(BF)
    if paired:
        bias_far, out_far = across(b_up), across(w_out)
        n1, bias_far, out_far = lax.optimization_barrier((n1, bias_far, out_far))
        n1_far = across(n1)
    else:
        n1_far = lax.all_gather(n1, "mp", axis=0, tiled=True)
    def gather(w):
        half = w.shape[0] // 2
        return lax.all_gather(piece(w, core, half), ("core", "mp"), axis=0).reshape(
            2, parts, half, w.shape[1]
        )

    w_qkv = jnp.concatenate([w_query, w_key, w_value], axis=1)
    w_turned = w_qkv.T
    if paired:
        tables_near = tables(piece(pos_all, rank, rows))
        q_near, k_near, v_near = project(n1, w_turned, *tables_near)
        start = attend_half(
            "near_near", ends, index, q_near, False, {0: (k_near, v_near)}, last=False
        )
        n1_far, start, w_up_late, w_down_late = lax.optimization_barrier(
            (n1_far, start, w_up, w_down)
        )
        up_all = gather(w_up_late)
        down_all = gather(w_down_late)
        tables_far = tables(piece(pos_all, 1 - rank, rows))
        q_far, k_far, v_far = project(n1_far, w_turned, *tables_far)
        mixed_far, log_far = attend_half(
            "far_all", ends, index, q_far, True, {0: (k_near, v_near), 1: (k_far, v_far)}
        )
        mixed_in = across(mixed_far)
        mixed_near, log_near = attend_half(
            "near_far", ends, index, q_near, False, {1: (k_far, v_far)}, carry=start
        )
        mixed_rows = order(mixed_near, mixed_in, 0)
        attended = dot_tn(mixed_near, w_out) + dot_tn(mixed_in, out_far)
    else:
        bias_all = lax.all_gather(b_up, "mp", axis=0).reshape(parts, 1, -1)
        w_out_all = lax.all_gather(w_out, "mp", axis=0, tiled=True)
        up_all = gather(w_up)
        down_all = gather(w_down)
        cosine, sine = tables(pos_all)
        query, keys, values = project(n1_far, w_turned, cosine, sine)
        mixed, logsum = attend(ends, zero, query, keys, values, 1)
        mixed_rows = lax.all_to_all(mixed, "mp", 1, 0, tiled=True)
        attended = dot_tn(mixed_rows, w_out_all)
    h1 = h0 + attended + b_out
    scale_two = lax.rsqrt(jnp.mean(h1 * h1, axis=-1, keepdims=True) + EPS)
    n2 = (h1 * scale_two * gain_ffn).astype(BF)
    grad_rows = cotangent.astype(F32) * valid_here
    grad_low = grad_rows.astype(BF)
    if paired:
        branch, grad_n2, sums, bias_near = ffn(
            "ffn_near", n2, grad_low, w_up.reshape(2, 1, width // 2, hidden),
            b_up.reshape(1, 1, hidden), w_down.reshape(2, 1, hidden // 2, width),
            extra, parts, zero, index,
        )
        both = jnp.stack([bias_far, bias_far]).reshape(2, 1, hidden)
        branch, grad_n2, sums, grad_bias = ffn(
            "ffn_far", n2, grad_low, up_all, both, down_all, extra, parts, other, other,
            before=(branch, grad_n2, sums),
        )
        grad_bias = order(bias_near, grad_bias, 0)
    else:
        every = jnp.arange(parts, dtype=jnp.int32)
        branch, grad_n2, sums, grad_bias = ffn(
            "ffn", n2, grad_low, up_all, bias_all, down_all, extra, parts, every, every
        )
    output = valid_here * (h1 + branch + b_down)
    grad_h1, grad_gain_ffn = norm_back(grad_n2, h1, scale_two, gain_ffn)
    grad_h1 = grad_h1 + grad_rows
    grad_h1_low = grad_h1.astype(BF)
    if paired:
        grad_far = across(dot_nt(out_far, grad_h1_low).astype(BF))
        grad_near = dot_nt(w_out, grad_h1_low).astype(BF)
    else:
        grad_mixed = lax.all_to_all(
            dot_nt(w_out_all, grad_h1_low).astype(BF), "mp", 0, 1, tiled=True
        )
    sums = out_back(mixed_rows, grad_h1_low, sums, extra)
    small = [jnp.sum(grad_rows, 0), grad_gain_ffn, jnp.sum(grad_h1, 0)]
    part = lax.psum_scatter(
        sums.reshape((2 * parts,) + sums.shape[2:]), ("core", "mp"), scatter_dimension=0, tiled=True
    )[0]
    summed = lax.psum(part, "dpo")

    if paired:
        near = (q_near, k_near, v_near, grad_near, mixed_near, log_near) + tables_near
        far = (q_far, k_far, v_far, grad_far, mixed_far, log_far) + tables_far
        heads = each // HEAD_DIM
        back = functools.partial(half_back, ends=ends, rank=index)
        both = (near, far)
        middle = heads // 2
        opening = back("back_near0", sides=(near,), first=0, count=middle, finish=False)[0]
        written, at = (), 0
        for i, count in enumerate((middle // 2, middle // 4, middle - middle // 2 - middle // 4)):
            written = back(
                f"back_first{i}", sides=both, first=at, count=count, finish=True,
                partial=opening, written=written, after=part if i == 2 else None,
            )
            at += count
        back_far, back_near = written
        partial = None
        for i in range(2):
            back_far, partial = back(
                f"back_second{i}", sides=both, first=at, count=middle // 2, finish=False,
                written=(back_far, partial),
            )
            at += middle // 2
        back_far = back_far.reshape(3 * each, rows)
        sent = across(dot(back_far, w_qkv, ((0,), (1,))).astype(BF))
        back_near = back(
            "back_near1", sides=(near,), first=middle, count=heads - middle, finish=True,
            partial=partial, written=(back_near,),
        )[0].reshape(3 * each, rows)
        grad_n1 = dot(back_near, w_qkv, ((0,), (1,))) + sent.astype(F32)
        pairs = [(n1, back_near), (n1_far, back_far)]
    else:
        back = attend_back(ends, query, keys, values, grad_mixed, mixed, logsum, cosine, sine)
        grad_n1 = dot(back, w_qkv, ((0,), (1,))).astype(BF)
        grad_n1 = lax.psum_scatter(grad_n1, "mp", scatter_dimension=0, tiled=True).astype(F32)
        pairs = [(n1_far, back)]
    sibling = lax.ppermute(summed, "core", [(0, 1), (1, 0)])
    grad_up, grad_down = unpack(core.reshape(1), summed, sibling, hidden)
    own_out, sibling_out = summed[hidden:].astype(F32), sibling[hidden:].astype(F32)
    grad_out = jnp.where(
        core == 0,
        jnp.concatenate([own_out, sibling_out]),
        jnp.concatenate([sibling_out, own_out]),
    )

    grad_qkv = project_back(pairs, grad_up)

    grad_h0, grad_gain_attn = norm_back(grad_n1, h0, scale_one, gain_attn)
    grad_h0_low = (grad_h0 + grad_h1).astype(BF)
    grad_w_concat = dot_tn(joined, grad_h0_low).astype(BF)
    small = small + [jnp.sum(grad_h0_low.astype(F32), axis=0), grad_gain_attn]
    small = jnp.concatenate(small + [grad_bias.reshape(-1)]).reshape(-1, width)
    small = jnp.pad(small, ((0, -small.shape[0] % 8), (0, 0)))
    if paired and lax.axis_size("dpo") == 8:
        tail, grad_qkv, small = sum_all(grad_w_concat, grad_qkv, small)
    else:
        tail, small = lax.psum((grad_w_concat, small), dp + ("mp",))
        grad_qkv = lax.psum(grad_qkv, dp)
    grad_inputs, grad_skip = join_back(grad_h0_low, w_concat)
    grad_query, grad_key, grad_value = turn(grad_qkv, 3)
    return (
        output,
        grad_inputs,
        grad_skip,
        tail.astype(F32),
        small[3],
        small[4],
        grad_query,
        grad_key,
        grad_value,
        grad_out,
        small[2],
        small[1],
        grad_up,
        piece(small[5 : 5 + parts * hidden // width].reshape(-1), rank, hidden),
        grad_down,
        small[0],
    )


def solution(mesh):
    dp, mp = mesh.shape["dp"], mesh.shape["mp"]
    mesh = Mesh(mesh.devices.reshape(dp // 2, 2, mp), ("dpo", "core", "mp"))
    rows = P(("dpo", "core", "mp"), None)
    columns = P(None, "mp")
    upright = P("mp", None)
    return jax.shard_map(
        body,
        mesh=mesh,
        in_specs=(
            rows, rows, rows, P(("dpo", "core"), None), P(), P(), P(), columns, columns, columns,
            upright, P(), P(), columns, P("mp"), upright, P(),
        ),
        out_specs=(
            rows, rows, rows, P(), P(), P(), columns, columns, columns,
            upright, P(), P(), columns, P("mp"), upright, P(),
        ),
        check_vma=False,
    )
```

```python
import functools

import jax
import jax.numpy as jnp
from jax import lax
from jax.experimental import pallas as pl
from jax.experimental.pallas import tpu as pltpu
from jax.sharding import Mesh
from jax.sharding import PartitionSpec as P

HEAD_DIM = 64
HALF = HEAD_DIM // 2
EPS = 1e-06
FIRST_LEAST = 3712
FIRST_MOST = 3840
SEGS = 16
LOG2E = 1.4426950408889634
LN2 = 0.6931471805599453
VMEM = 60 * 2**20

BF = jnp.bfloat16
F32 = jnp.float32


def dot(left, right, dims=((1,), (0,))):
    return lax.dot_general(left, right, (dims, ((), ())), preferred_element_type=F32)


def dot_tn(left, right):
    return dot(left, right, ((0,), (0,)))


def dot_nt(left, right):
    return dot(left, right, ((1,), (1,)))


def layout(lengths_row, count):
    ends = jnp.cumsum(lengths_row)
    starts = ends - lengths_row
    places = jnp.arange(count, dtype=jnp.int32)
    seg = jnp.sum((places[:, None] >= ends[None, :]).astype(jnp.int32), axis=1)
    owner = seg[:, None] == jnp.arange(lengths_row.shape[0], dtype=jnp.int32)[None, :]
    start_of = jnp.sum(jnp.where(owner, starts[None, :], 0), axis=1)
    pos = (places - start_of).astype(F32)
    valid = (places < ends[-1]).astype(F32)
    return (ends.astype(jnp.int32), pos, valid)


def tables(pos):
    freq = jnp.exp(-jnp.log(10000.0) * jnp.arange(HALF, dtype=F32) * 2.0 / HEAD_DIM)
    angle = freq[:, None] * pos[None, :]
    return (jnp.cos(angle), jnp.sin(angle))


def norm_back(grad, stream, scale, gain):
    tilted = grad * gain
    grad_gain = jnp.sum(grad * stream * scale, axis=0)
    grad_stream = scale * tilted - stream * scale**3 * jnp.mean(
        tilted * stream, axis=-1, keepdims=True
    )
    return (grad_stream, grad_gain)


def params():
    return pltpu.CompilerParams(vmem_limit_bytes=VMEM)


def cost(flops, moved):
    return pl.CostEstimate(flops=flops // 64, bytes_accessed=moved // 64, transcendentals=0)


def project_kernel(x_ref, w_ref, cos_ref, sin_ref, *refs):
    q_ref, k_ref, v_ref = refs[-3:]
    x = x_ref[...]
    c, s = cos_ref[...], sin_ref[...]
    width = q_ref.shape[0]
    for out, first, factor in ((q_ref, 0, 0.125 * LOG2E), (k_ref, width, 1.0)):
        t = dot_nt(w_ref[first : first + width, :], x)
        for h in range(0, width, HEAD_DIM):
            a, b = t[h : h + HALF], t[h + HALF : h + HEAD_DIM]
            out[h : h + HALF, :] = ((a * c - b * s) * factor).astype(BF)
            out[h + HALF : h + HEAD_DIM, :] = ((b * c + a * s) * factor).astype(BF)
    v_ref[...] = dot_nt(w_ref[2 * width :, :], x).astype(BF)


def project(x, w, cosine, sine, first=0, written=()):
    count, depth = x.shape
    total = cosine.shape[1]
    width = w.shape[0] // 3
    block = min(512, count)
    start = first // block
    table = pl.BlockSpec((HALF, block), lambda i: (0, i + start))
    out = pl.BlockSpec((width, block), lambda i: (0, i + start))
    return pl.pallas_call(
        project_kernel,
        grid=(count // block,),
        in_specs=[
            pl.BlockSpec((block, depth), lambda i: (i, 0)),
            pl.BlockSpec(w.shape, lambda i: (0, 0)),
            table,
            table,
        ]
        + [pl.BlockSpec(memory_space=pl.ANY)] * len(written),
        out_specs=[out] * 3,
        out_shape=[jax.ShapeDtypeStruct((width, total), BF)] * 3,
        input_output_aliases={4 + i: i for i in range(len(written))},
        compiler_params=params(),
        name="project",
    )(x, w, cosine, sine, *written)


def scale_of(stream):
    return lax.rsqrt(jnp.mean(stream * stream, axis=-1, keepdims=True) + EPS)


def norm_back_rows(grad, stream, gain):
    scale = scale_of(stream)
    tilted = grad * gain
    back = scale * tilted - stream * (scale * scale * scale) * jnp.mean(
        tilted * stream, axis=-1, keepdims=True
    )
    return back, jnp.sum(grad * stream * scale, axis=0, keepdims=True)


def add_up(ref, terms):
    for i, term in enumerate(terms):

        @pl.when(pl.program_id(0) == 0)
        def _():
            ref[i : i + 1, :] = term

        @pl.when(pl.program_id(0) > 0)
        def _():
            ref[i : i + 1, :] += term


def row_specs(rows, width, block, first=0):
    def tall(columns=width):
        return pl.BlockSpec((block, columns), lambda i: (i + first, 0))

    def whole(*shape):
        return pl.BlockSpec(shape, lambda i: (0, 0))

    return tall, whole


def enter_kernel(x_ref, s_ref, w_ref, b_ref, gain_ref, *refs):
    h_ref, n_ref = refs[-2:]
    width = x_ref.shape[1]
    h = dot(x_ref[...], w_ref[:width, :]) + dot(s_ref[...], w_ref[width:, :]) + b_ref[...]
    h_ref[...] = h
    n_ref[...] = (h * scale_of(h) * gain_ref[...]).astype(BF)


def enter(x, skip, w, bias, gain, first, count, written=()):
    rows, width = x.shape
    block = min(256, count)
    tall, whole = row_specs(rows, width, block, first // block)
    return pl.pallas_call(
        enter_kernel,
        grid=(count // block,),
        in_specs=[tall(), tall(), whole(*w.shape), whole(1, width), whole(1, width)]
        + [pl.BlockSpec(memory_space=pl.ANY)] * len(written),
        out_specs=[tall(), tall()],
        out_shape=[jax.ShapeDtypeStruct((rows, width), F32), jax.ShapeDtypeStruct((rows, width), BF)],
        input_output_aliases={5 + i: i for i in range(len(written))},
        compiler_params=params(),
        name="enter",
        cost_estimate=cost(4 * count * width * width, 10 * count * width),
    )(x, skip, w, bias[None], gain[None], *written)


def upper_kernel(h_ref, near_ref, in_ref, own_ref, far_ref, b_ref, gain_ref, h1_ref, n_ref):
    h = h_ref[...] + dot_tn(near_ref[...], own_ref[...]) + dot_tn(in_ref[...], far_ref[...])
    h = h + b_ref[...]
    h1_ref[...] = h
    n_ref[...] = (h * scale_of(h) * gain_ref[...]).astype(BF)


def upper(h0, near, arrived, own, far, bias, gain):
    rows, width = h0.shape
    block = min(256, rows)
    tall, whole = row_specs(rows, width, block)
    flat = pl.BlockSpec((near.shape[0], block), lambda i: (0, i))
    return pl.pallas_call(
        upper_kernel,
        grid=(rows // block,),
        in_specs=[
            tall(), flat, flat, whole(*own.shape), whole(*far.shape), whole(1, width), whole(1, width)
        ],
        out_specs=[tall(), tall()],
        out_shape=[jax.ShapeDtypeStruct((rows, width), F32), jax.ShapeDtypeStruct((rows, width), BF)],
        compiler_params=params(),
        name="upper",
        cost_estimate=cost(2 * rows * width * width, 12 * rows * width),
    )(h0, near, arrived, own, far, bias[None], gain[None])


def middle_kernel(
    h_ref, branch_ref, dn_ref, g_ref, valid_ref, bias_ref, gain_ref, own_ref, far_ref,
    out_ref, dh_ref, low_ref, near_ref, sent_ref, sums_ref,
):
    valid = valid_ref[...]
    h = h_ref[...]
    out_ref[...] = valid * (h + branch_ref[...] + bias_ref[...])
    g = g_ref[...].astype(F32) * valid
    back, gain_sum = norm_back_rows(dn_ref[...], h, gain_ref[...])
    dh = g + back
    dh_ref[...] = dh
    low = dh.astype(BF)
    low_ref[...] = low
    near_ref[...] = dot_nt(own_ref[...], low).astype(BF)
    sent_ref[...] = dot_nt(far_ref[...], low).astype(BF)
    add_up(
        sums_ref,
        [jnp.sum(g, 0, keepdims=True), gain_sum, jnp.sum(dh, 0, keepdims=True)],
    )


def middle(h1, branch, dn, cotangent, valid, bias, gain, own, far):
    rows, width = h1.shape
    block = min(256, rows)
    tall, whole = row_specs(rows, width, block)
    flat = pl.BlockSpec((own.shape[0], block), lambda i: (0, i))
    return pl.pallas_call(
        middle_kernel,
        grid=(rows // block,),
        in_specs=[tall(), tall(), tall(), tall(), tall(1), whole(1, width), whole(1, width)]
        + [whole(*own.shape)] * 2,
        out_specs=[tall(), tall(), tall(), flat, flat, whole(3, width)],
        out_shape=[
            jax.ShapeDtypeStruct((rows, width), F32),
            jax.ShapeDtypeStruct((rows, width), F32),
            jax.ShapeDtypeStruct((rows, width), BF),
            jax.ShapeDtypeStruct((own.shape[0], rows), BF),
            jax.ShapeDtypeStruct((own.shape[0], rows), BF),
            jax.ShapeDtypeStruct((3, width), F32),
        ],
        compiler_params=params(),
        name="middle",
        cost_estimate=cost(2 * rows * width * width, 24 * rows * width),
    )(h1, branch, dn, cotangent, valid, bias[None], gain[None], own, far)


def leave_kernel(back_ref, w_ref, sent_ref, h_ref, dh_ref, gain_ref, *refs):
    low_ref, sums_ref = refs[-2:]
    grad = dot_tn(back_ref[...], w_ref[...]) + sent_ref[...].astype(F32)
    back, gain_sum = norm_back_rows(grad, h_ref[...], gain_ref[...])
    low = (back + dh_ref[...]).astype(BF)
    low_ref[...] = low
    add_up(sums_ref, [jnp.sum(low.astype(F32), 0, keepdims=True), gain_sum])


def leave(back, w, sent, h0, dh1, gain, after):
    rows, width = h0.shape
    block = min(256, rows)
    tall, whole = row_specs(rows, width, block)
    return pl.pallas_call(
        leave_kernel,
        grid=(rows // block,),
        in_specs=[
            pl.BlockSpec((back.shape[0], block), lambda i: (0, i)),
            whole(*w.shape),
            tall(),
            tall(),
            tall(),
            whole(1, width),
        ]
        + [pl.BlockSpec(memory_space=pl.ANY)] * len(after),
        out_specs=[tall(), whole(2, width)],
        out_shape=[
            jax.ShapeDtypeStruct((rows, width), BF),
            jax.ShapeDtypeStruct((2, width), F32),
        ],
        compiler_params=params(),
        name="leave",
        cost_estimate=cost(2 * rows * width * back.shape[0], 16 * rows * width),
    )(back, w, sent, h0, dh1, gain[None], *after)


def segments(ends_ref, first, count):
    pos = lax.broadcasted_iota(jnp.int32, (1, count), 1) + first
    seg = jnp.zeros((1, count), jnp.int32)
    for i in range(ends_ref.shape[0]):
        seg = seg + (pos >= ends_ref[i]).astype(jnp.int32)
    return lax.broadcasted_iota(jnp.int32, (SEGS, 1), 0) == seg


def zeros(rows, count):
    return jnp.zeros((rows, count), F32)


def key_pieces(count):
    if count == 4096:
        main = [(k0, 384) for k0 in range(0, FIRST_MOST, 384)]
        whole = [(k0, 1024) for k0 in range(0, count, 1024)]
        return [
            (0, 2048, main),
            (2048, 1536, main),
            (3584, 256, whole),
            (FIRST_MOST, 256, [(FIRST_LEAST, count - FIRST_LEAST)]),
        ]
    step = min(512, count)
    every = [(k0, step) for k0 in range(0, count, step)]
    return [(q0, step, every) for q0 in range(0, count, step)]


def attend_kernel(cut, ends_ref, part_ref, q_ref, k_ref, v_ref, o_ref, l_ref, kaug, qaug, vaug):
    count = k_ref.shape[1]
    here = q_ref.shape[1]
    part = part_ref[0]
    same = segments(ends_ref, 0, count)
    kaug[...] = (
        jnp.concatenate([k_ref[...].astype(F32), jnp.where(same, 0.0, -1e30), zeros(48, count)], 0)
        .T.astype(BF)
    )
    mine = segments(ends_ref, part * here, here)
    qaug[...] = jnp.concatenate(
        [q_ref[...].astype(F32), jnp.where(mine, 1.0, 0.0), zeros(48, here)], 0
    ).astype(BF)
    first = lax.broadcasted_iota(jnp.int32, (SEGS, count), 0) == 0
    vaug[...] = jnp.concatenate([v_ref[...].astype(F32), jnp.where(first, 1.0, 0.0)], 0).astype(BF)

    def block(q0, width, pieces):
        queries = qaug[:, q0 : q0 + width]
        top = jnp.full((1, width), -jnp.inf, F32)
        acc = jnp.zeros((HEAD_DIM + SEGS, width), F32)
        for k0, n in pieces:
            scores = dot(kaug[k0 : k0 + n, :], queries)
            higher = jnp.maximum(top, jnp.max(scores, axis=0, keepdims=True))
            probs = jnp.exp2(scores - higher).astype(BF)
            acc = acc * jnp.exp2(top - higher) + dot(vaug[:, k0 : k0 + n], probs)
            top = higher
        total = acc[HEAD_DIM : HEAD_DIM + 1]
        o_ref[:, q0 : q0 + width] = (acc[:HEAD_DIM] / total).astype(BF)
        l_ref[0, :, q0 : q0 + width] = top + jnp.log2(total)

    pieces = key_pieces(count)
    for p in range(cut):
        low, high = p * here, (p + 1) * here

        @pl.when(part == p)
        def _():
            for q0, width, keys in pieces:
                if low <= q0 < high:
                    block(q0 - low, width, keys)


def attend(ends, part, query, keys, values, cut):
    rows, count = query.shape
    heads = rows // HEAD_DIM
    here = count // cut
    whole = pl.BlockSpec((HEAD_DIM, count), lambda h, e, p: (h, 0))
    return pl.pallas_call(
        functools.partial(attend_kernel, cut),
        grid_spec=pltpu.PrefetchScalarGridSpec(
            num_scalar_prefetch=2,
            grid=(heads,),
            in_specs=[
                pl.BlockSpec((HEAD_DIM, here), lambda h, e, p: (h, p[0])),
                whole,
                whole,
            ],
            out_specs=[
                pl.BlockSpec((HEAD_DIM, here), lambda h, e, p: (h, 0)),
                pl.BlockSpec((1, 1, here), lambda h, e, p: (h, 0, 0)),
            ],
            scratch_shapes=[
                pltpu.VMEM((count, 128), BF),
                pltpu.VMEM((128, here), BF),
                pltpu.VMEM((HEAD_DIM + SEGS, count), BF),
            ],
        ),
        out_shape=[
            jax.ShapeDtypeStruct((rows, here), BF),
            jax.ShapeDtypeStruct((heads, 1, here), F32),
        ],
        compiler_params=params(),
        name="attend",
        cost_estimate=cost(4 * rows * here * count, 8 * rows * count),
    )(ends, part, query, keys, values)


def local_segments(ends_ref, part, count):
    return segments(ends_ref, part * count, count)


def spans(first, last, step):
    return [(k0, min(step, last - k0)) for k0 in range(first, last, step)]


def regions(query_part, key_parts, half):
    edge, start = FIRST_MOST - half, FIRST_LEAST - half

    def keys(first, last, p):
        return [(p, k0, n) for k0, n in spans(first, last, 1024)]

    if query_part == 0:
        found = []
        for p in key_parts:
            found += keys(0, half, 0) if p == 0 else keys(0, edge, 1)
        return [(0, half, found)]
    low = edge - 256
    if list(key_parts) == [0]:
        return [(0, edge, keys(0, half, 0)), (edge, half - edge, [])]
    main, mixed, last = [], [], []
    for p in key_parts:
        if p == 0:
            main += keys(0, half, 0)
            mixed += keys(0, half, 0)
        else:
            main += keys(0, edge, 1)
            mixed += keys(0, half, 1)
            last += [(1, start, half - start)]
    return [(0, low, main), (low, 256, mixed), (edge, half - edge, last)]


def half_kernel(query_far, key_sides, given, last, ends_ref, part_ref, *refs):
    refs = list(refs)
    q_ref = refs.pop(0)
    kv = {side: (refs.pop(0), refs.pop(0)) for side in key_sides}
    acc_in, top_in = (refs.pop(0), refs.pop(0)) if given else (None, None)
    out_ref, top_ref = refs.pop(0), refs.pop(0)
    qaug = refs.pop(0)
    kaug = {side: refs.pop(0) for side in key_sides}
    vaug = {side: refs.pop(0) for side in key_sides}
    half = q_ref.shape[1]
    rank = part_ref[0]

    @pl.when(pl.program_id(0) == 0)
    def _():
        for side in key_sides:
            same = local_segments(ends_ref, rank if side == 0 else 1 - rank, half)
            blank = zeros(HEAD_DIM, half)
            kaug[side][...] = (
                jnp.concatenate([blank, jnp.where(same, 0.0, -1e30), zeros(48, half)], 0)
                .T.astype(BF)
            )
            first = lax.broadcasted_iota(jnp.int32, (SEGS, half), 0) == 0
            vaug[side][HEAD_DIM:, :] = jnp.where(first, 1.0, 0.0).astype(BF)
        mine = local_segments(ends_ref, 1 - rank if query_far else rank, half)
        qaug[HEAD_DIM:, :] = jnp.concatenate(
            [jnp.where(mine, 1.0, 0.0), zeros(48, half)], 0
        ).astype(BF)

    for side in key_sides:
        kaug[side][:, :HEAD_DIM] = kv[side][0][...].T
        vaug[side][:HEAD_DIM, :] = kv[side][1][...]
    qaug[:HEAD_DIM, :] = q_ref[...]

    for here in range(2):
        query_part = 1 - here if query_far else here
        part_of = {side: here if side == 0 else 1 - here for side in key_sides}
        side_of = {p: side for side, p in part_of.items()}

        @pl.when(rank == here)
        def _():
            for q0, width, pieces in regions(query_part, list(side_of), half):
                there = slice(q0, q0 + width)
                queries = qaug[:, there]
                if given:
                    top, acc = top_in[0, :, there], acc_in[0, :, there]
                else:
                    top = jnp.full((1, width), -jnp.inf, F32)
                    acc = jnp.zeros((HEAD_DIM + SEGS, width), F32)
                for p, k0, n in pieces:
                    side = side_of[p]
                    scores = dot(kaug[side][k0 : k0 + n, :], queries)
                    higher = jnp.maximum(top, jnp.max(scores, axis=0, keepdims=True))
                    probs = jnp.exp2(scores - higher).astype(BF)
                    acc = acc * jnp.exp2(top - higher) + dot(vaug[side][:, k0 : k0 + n], probs)
                    top = higher
                if last:
                    total = acc[HEAD_DIM : HEAD_DIM + 1]
                    out_ref[:, there] = (acc[:HEAD_DIM] / total).astype(BF)
                    top_ref[0, :, there] = top + jnp.log2(total)
                else:
                    out_ref[0, :, there] = acc
                    top_ref[0, :, there] = top


def attend_half(name, ends, rank, query, query_far, keys, carry=None, last=True):
    rows, half = query.shape
    heads = rows // HEAD_DIM
    sides = sorted(keys)
    head = pl.BlockSpec((HEAD_DIM, half), lambda h, e, r: (h, 0))
    tall = pl.BlockSpec((1, HEAD_DIM + SEGS, half), lambda h, e, r: (h, 0, 0))
    line = pl.BlockSpec((1, 1, half), lambda h, e, r: (h, 0, 0))
    operands = [query]
    for side in sides:
        operands += list(keys[side])
    specs = [head] * len(operands)
    if carry is not None:
        operands += list(carry)
        specs += [tall, line]
    return pl.pallas_call(
        functools.partial(half_kernel, query_far, sides, carry is not None, last),
        grid_spec=pltpu.PrefetchScalarGridSpec(
            num_scalar_prefetch=2,
            grid=(heads,),
            in_specs=specs,
            out_specs=[head if last else tall, line],
            scratch_shapes=[pltpu.VMEM((128, half), BF)]
            + [pltpu.VMEM((half, 128), BF)] * len(sides)
            + [pltpu.VMEM((HEAD_DIM + SEGS, half), BF)] * len(sides),
        ),
        out_shape=[
            jax.ShapeDtypeStruct((rows, half), BF)
            if last
            else jax.ShapeDtypeStruct((heads, HEAD_DIM + SEGS, half), F32),
            jax.ShapeDtypeStruct((heads, 1, half), F32),
        ],
        compiler_params=params(),
        name=name,
        cost_estimate=cost(16 * rows * half * half * len(sides), 8 * rows * half),
    )(ends, rank, *operands)


def split3(x):
    a = x.astype(BF).astype(F32)
    b = (x - a).astype(BF).astype(F32)
    row = lax.broadcasted_iota(jnp.int32, (SEGS, 1), 0)
    return jnp.where(row == 0, a, jnp.where(row == 1, b, jnp.where(row == 2, x - a - b, 0.0)))


def attend_back_kernel(
    ends_ref, q_ref, k_ref, v_ref, g_ref, o_ref, l_ref, cos_ref, sin_ref, d_ref,
    kaug, vaug, qaug, gaug, pair, dq,
):
    count = k_ref.shape[1]
    same = segments(ends_ref, 0, count)
    row = lax.broadcasted_iota(jnp.int32, (SEGS, count), 0)
    shift = jnp.where(row < 3, 1.0, 0.0)
    g = g_ref[...].astype(F32)
    q = q_ref[...].astype(F32)
    delta = jnp.sum(g * o_ref[...].astype(F32), axis=0, keepdims=True)
    kaug[...] = (
        jnp.concatenate(
            [k_ref[...].astype(F32), jnp.where(same, 0.0, -1e30), shift, zeros(32, count)], 0
        )
        .T.astype(BF)
    )
    vaug[...] = (
        jnp.concatenate([v_ref[...].astype(F32), shift, zeros(48, count)], 0).T.astype(BF)
    )
    qaug[...] = jnp.concatenate(
        [q, jnp.where(same, 1.0, 0.0), split3(-l_ref[0]), zeros(32, count)], 0
    ).astype(BF)
    gaug[...] = jnp.concatenate([g, split3(-delta), zeros(48, count)], 0).astype(BF)
    pair[...] = jnp.concatenate([q, g], 0).T.astype(BF)
    dq[...] = jnp.zeros_like(dq)

    def turn(grad, c, s, factor):
        a, b = grad[:HALF], grad[HALF:]
        return (
            jnp.concatenate([a * c + b * s, b * c - a * s], 0) * factor
        ).astype(BF)

    def chunk(k0, n, queries):
        where = pl.ds(k0, n)
        kb, vb, kt = kaug[where, :], vaug[where, :], k_ref[:, where]
        dk = jnp.zeros((n, HEAD_DIM), F32)
        dv = jnp.zeros((n, HEAD_DIM), F32)
        for q0, width in queries:
            there = slice(q0, q0 + width)
            probs = jnp.exp2(dot(kb, qaug[:, there]))
            tilt = (probs * dot(vb, gaug[:, there])).astype(BF)
            dv = dv + dot(probs.astype(BF), pair[there, HEAD_DIM:])
            dk = dk + dot(tilt, pair[there, :HEAD_DIM])
            dq[:, there] += dot(kt, tilt)
        c, s = cos_ref[:, where], sin_ref[:, where]
        d_ref[1, 0, :, where] = turn(dk.T, c, s, LN2)
        d_ref[2, 0, :, where] = dv.T.astype(BF)

    if count == 4096:
        main = [(q0, 1920) for q0 in range(0, FIRST_MOST, 1920)]

        def step(i, carry):
            chunk(pl.multiple_of(i * 512, 512), 512, main)
            return carry

        lax.fori_loop(0, 7, step, 0)
        chunk(3584, 256, [(q0, 1024) for q0 in range(0, count, 1024)])
        chunk(FIRST_MOST, count - FIRST_MOST, [(3584, 512)])
    else:
        size = min(512, count)

        def step(i, carry):
            chunk(pl.multiple_of(i * size, size), size, [(q, size) for q in range(0, count, size)])
            return carry

        lax.fori_loop(0, count // size, step, 0)
    d_ref[0, 0] = turn(dq[...], cos_ref[...], sin_ref[...], 0.125)


def attend_back(ends, query, keys, values, grad, mixed, logsum, cosine, sine):
    rows, count = query.shape
    heads = rows // HEAD_DIM
    whole = pl.BlockSpec((HEAD_DIM, count), lambda h, e: (h, 0))
    table = pl.BlockSpec((HALF, count), lambda h, e: (0, 0))
    out = pl.pallas_call(
        attend_back_kernel,
        grid_spec=pltpu.PrefetchScalarGridSpec(
            num_scalar_prefetch=1,
            grid=(heads,),
            in_specs=[whole] * 5
            + [pl.BlockSpec((1, 1, count), lambda h, e: (h, 0, 0)), table, table],
            out_specs=pl.BlockSpec((3, 1, HEAD_DIM, count), lambda h, e: (0, h, 0, 0)),
            scratch_shapes=[
                pltpu.VMEM((count, 128), BF),
                pltpu.VMEM((count, 128), BF),
                pltpu.VMEM((128, count), BF),
                pltpu.VMEM((128, count), BF),
                pltpu.VMEM((count, 128), BF),
                pltpu.VMEM((HEAD_DIM, count), F32),
            ],
        ),
        out_shape=jax.ShapeDtypeStruct((3, heads, HEAD_DIM, count), BF),
        compiler_params=params(),
        name="attend_back",
        cost_estimate=cost(10 * rows * count * count, 16 * rows * count),
    )(ends, query, keys, values, grad, mixed, logsum, cosine, sine)
    return out.reshape(3 * rows, count)


def turn_back(grad, c, s, factor):
    a, b = grad[:HALF], grad[HALF:]
    return (jnp.concatenate([a * c + b * s, b * c - a * s], 0) * factor).astype(BF)


def back_chunks(key_part, query_parts, half):
    edge = FIRST_MOST - half
    low = edge - 256
    found = []
    if key_part == 0:
        queries = []
        for p in query_parts:
            queries += [(p, 0, half if p == 0 else edge)]
        return [(0, half, 512, queries)]
    main = [(p, 0, half if p == 0 else edge) for p in query_parts]
    found.append((0, low, 512, main))
    found.append((low, 256, 256, [(p, 0, half) for p in query_parts]))
    if 1 in query_parts:
        found.append((edge, half - edge, 256, [(1, low, half - low)]))
    return found


def half_back_kernel(near_only, given_partial, finish, ends_ref, part_ref, *refs):
    refs = list(refs)
    sides = (0,) if near_only else (0, 1)
    given = {side: [refs.pop(0) for _ in range(8)] for side in sides}
    partial_in = refs.pop(0) if given_partial else None
    while len(refs) > (1 if near_only else 2) + 7:
        refs.pop(0)
    out_ref = None if near_only else refs.pop(0)
    near_ref = refs.pop(0)
    kaug, vaug, qaug, gaug, pair, dq, sums = refs
    rank = part_ref[0]
    half = given[0][0].shape[1]

    @pl.when(pl.program_id(0) == 0)
    def _():
        row = lax.broadcasted_iota(jnp.int32, (SEGS, half), 0)
        shift = jnp.where(row < 3, 1.0, 0.0)
        blank = zeros(HEAD_DIM, half)
        for side in sides:
            there = slice(side * half, side * half + half)
            same = local_segments(ends_ref, rank if side == 0 else 1 - rank, half)
            kaug[there, :] = (
                jnp.concatenate([blank, jnp.where(same, 0.0, -1e30), shift, zeros(32, half)], 0)
                .T.astype(BF)
            )
            vaug[there, :] = jnp.concatenate([blank, shift, zeros(48, half)], 0).T.astype(BF)
            qaug[HEAD_DIM:, there] = jnp.concatenate(
                [jnp.where(same, 1.0, 0.0), zeros(48, half)], 0
            ).astype(BF)
            gaug[HEAD_DIM:, there] = blank.astype(BF)

    for side in sides:
        q_ref, k_ref, v_ref, g_ref, o_ref, l_ref = given[side][:6]
        there = slice(side * half, side * half + half)
        g = g_ref[...]
        q = q_ref[...]
        delta = jnp.sum(g.astype(F32) * o_ref[...].astype(F32), axis=0, keepdims=True)
        kaug[there, :HEAD_DIM] = k_ref[...].T
        vaug[there, :HEAD_DIM] = v_ref[...].T
        qaug[:HEAD_DIM, there] = q
        qaug[HEAD_DIM + SEGS : HEAD_DIM + 2 * SEGS, there] = split3(-l_ref[0]).astype(BF)
        gaug[:HEAD_DIM, there] = g
        gaug[HEAD_DIM : HEAD_DIM + SEGS, there] = split3(-delta).astype(BF)
        pair[there, :] = jnp.concatenate([q, g], 0).T
    dq[...] = jnp.zeros_like(dq)
    if given_partial:
        dq[:, :half] = partial_in[0, 0]
        sums[...] = partial_in[1:, 0]
    else:
        sums[...] = jnp.zeros_like(sums)

    def chunk(side, k0, n, queries):
        where = pl.ds(side * half + k0, n)
        kb, vb, kt = kaug[where, :], vaug[where, :], given[side][1][:, pl.ds(k0, n)]
        dk = jnp.zeros((n, HEAD_DIM), F32)
        dv = jnp.zeros((n, HEAD_DIM), F32)
        for q0, width in queries:
            there = slice(q0, q0 + width)
            probs = jnp.exp2(dot(kb, qaug[:, there]))
            tilt = (probs * dot(vb, gaug[:, there])).astype(BF)
            dv = dv + dot(probs.astype(BF), pair[there, HEAD_DIM:])
            dk = dk + dot(tilt, pair[there, :HEAD_DIM])
            dq[:, there] += dot(kt, tilt)
        dk, dv = dk.T, dv.T
        if side == 0:
            sums[0, :, pl.ds(k0, n)] += dk
            sums[1, :, pl.ds(k0, n)] += dv
            return
        c, s = given[side][6][:, pl.ds(k0, n)], given[side][7][:, pl.ds(k0, n)]
        out_ref[1, 0, :, pl.ds(k0, n)] = turn_back(dk, c, s, LN2)
        out_ref[2, 0, :, pl.ds(k0, n)] = dv.astype(BF)

    for here in range(2):

        @pl.when(rank == here)
        def _():
            side_of = {here: 0, 1 - here: 1}
            for key_part, side in side_of.items():
                if near_only and side == 1:
                    continue
                if near_only:
                    query_parts = [here]
                else:
                    query_parts = [0, 1] if side == 1 else [1 - here]
                for k0, total, n, queries in back_chunks(key_part, query_parts, half):
                    spread = [(side_of[p] * half + q0, width) for p, q0, width in queries]
                    if total == n:
                        chunk(side, k0, n, spread)
                        continue

                    def step(i, carry):
                        chunk(side, pl.multiple_of(k0 + i * n, n), n, spread)
                        return carry

                    lax.fori_loop(0, total // n, step, 0)

    if not near_only:
        out_ref[0, 0] = turn_back(dq[:, half:], given[1][6][...], given[1][7][...], 0.125)
    if finish:
        c, s = given[0][6][...], given[0][7][...]
        near_ref[0, 0] = turn_back(dq[:, :half], c, s, 0.125)
        near_ref[1, 0] = turn_back(sums[0], c, s, LN2)
        near_ref[2, 0] = sums[1].astype(BF)
    else:
        near_ref[0, 0] = dq[:, :half]
        near_ref[1:, 0] = sums[...]


def half_back(name, ends, rank, sides, first, count, finish, partial=None, written=(), after=None):
    rows, half = sides[0][0].shape
    heads = rows // HEAD_DIM
    near_only = len(sides) == 1
    head = pl.BlockSpec((HEAD_DIM, half), lambda h, e, r: (h + first, 0))
    line = pl.BlockSpec((1, 1, half), lambda h, e, r: (h + first, 0, 0))
    table = pl.BlockSpec((HALF, half), lambda h, e, r: (0, 0))
    block = pl.BlockSpec((3, 1, HEAD_DIM, half), lambda h, e, r: (0, h + first, 0, 0))
    anywhere = pl.BlockSpec(memory_space=pl.ANY)
    operands, specs = [], []
    for side in sides:
        operands += list(side)
        specs += [head] * 5 + [line, table, table]
    result = jax.ShapeDtypeStruct((3, heads, HEAD_DIM, half), BF)
    if partial is not None:
        operands.append(partial)
        specs.append(block)
    aliases = {}
    for i, array in enumerate(written):
        if array is not None:
            aliases[2 + len(operands)] = i
            operands.append(array)
            specs.append(anywhere)
    if after is not None:
        operands.append(after)
        specs.append(anywhere)
    near_result = result if finish else jax.ShapeDtypeStruct(result.shape, F32)
    out_shape = [near_result] if near_only else [result, near_result]
    out_specs = [block] * len(out_shape)
    wide = half * len(sides)
    return pl.pallas_call(
        functools.partial(half_back_kernel, near_only, partial is not None, finish),
        grid_spec=pltpu.PrefetchScalarGridSpec(
            num_scalar_prefetch=2,
            grid=(count,),
            in_specs=specs,
            out_specs=out_specs,
            scratch_shapes=[
                pltpu.VMEM((wide, 128), BF),
                pltpu.VMEM((wide, 128), BF),
                pltpu.VMEM((128, wide), BF),
                pltpu.VMEM((128, wide), BF),
                pltpu.VMEM((wide, 128), BF),
                pltpu.VMEM((HEAD_DIM, wide), F32),
                pltpu.VMEM((2, HEAD_DIM, half), F32),
            ],
        ),
        out_shape=out_shape,
        input_output_aliases=aliases,
        compiler_params=params(),
        name=name,
        cost_estimate=cost(40 * count * HEAD_DIM * half * half * (1 if near_only else 3), 40 * count * HEAD_DIM * half),
    )(ends, rank, *operands)


def ffn_kernel(step, given, src_ref, dst_ref, n_ref, g_ref, up_ref, bias_ref, down_ref, *refs):
    branch_in, dn_in = refs[:2] if given else (None, None)
    branch_ref, dn_ref, dw_ref, dbias_ref, branch, dn, sems = refs[3 if given else 0 :]

    rows, depth = n_ref.shape
    steps = [(i, slice(r0, r0 + step)) for i, r0 in enumerate(range(0, rows, step))]
    opening = (pl.program_id(0) == 0) & (pl.program_id(1) == 0)
    closing = (pl.program_id(0) == pl.num_programs(0) - 1) & (
        pl.program_id(1) == pl.num_programs(1) - 1
    )

    def moves(i, part, out):
        if out:
            pairs = ((branch, branch_ref), (dn, dn_ref))
        else:
            pairs = ((branch_in, branch), (dn_in, dn))
        return [
            pltpu.make_async_copy(src.at[part, :], dst.at[part, :], sems.at[j, i])
            for j, (src, dst) in enumerate(pairs)
        ]

    @pl.when(opening)
    def _():
        if given:
            for i, part in steps:
                for move in moves(i, part, False):
                    move.start()
        else:
            branch[...] = jnp.zeros_like(branch)
            dn[...] = jnp.zeros_like(dn)

    up = up_ref[...].reshape(depth, -1)
    down, bias = down_ref[0, 0], bias_ref[0].astype(F32)
    width = up.shape[1]
    dup = jnp.zeros((width, depth), F32)
    ddown = jnp.zeros((width, depth), F32)
    dbias = jnp.zeros((1, width), F32)
    for i, part in steps:
        x, y = n_ref[part, :], g_ref[part, :]
        u = dot(x, up) + bias
        dz = dot_nt(y, down)
        normal = 0.5 * (1.0 + lax.erf(u * 0.7071067811865476))
        density = jnp.exp(-0.5 * u * u) * 0.3989422804014327
        z = (u * normal).astype(BF)
        du = (dz * (normal + u * density)).astype(BF)
        if given:

            @pl.when(opening)
            def _():
                for move in moves(i, part, False):
                    move.wait()

        branch[part, :] += dot(z, down)
        dn[part, :] += dot_nt(du, up)

        @pl.when(closing)
        def _():
            for move in moves(i, part, True):
                move.start()

        ddown = ddown + dot_tn(z, y)
        dup = dup + dot_tn(du, x)
        dbias = dbias + jnp.sum(du.astype(F32), axis=0, keepdims=True)
    dw_ref[0, 0, :width, :] = dup.astype(BF)
    dw_ref[0, 0, width:, :] = ddown.astype(BF)
    dbias_ref[0] = dbias

    @pl.when(closing)
    def _():
        for i, part in steps:
            for move in moves(i, part, True):
                move.wait()


def ffn_block(hidden):
    return min(512, hidden // 2)


def ffn(name, n2, grad, up, bias, down, extra, parts, src, dst, before=None):
    rows, depth = n2.shape
    hidden = up.shape[3]
    block = ffn_block(hidden)
    per = hidden // 2 // block
    step = min(512, rows)
    once = pl.BlockSpec(
        (rows, depth), lambda p, i, f, t: (0, 0), pipeline_mode=pl.Buffered(1)
    )
    anywhere = pl.BlockSpec(memory_space=pl.ANY)
    operands = [n2, grad, up, bias, down] + ([] if before is None else list(before))
    return pl.pallas_call(
        functools.partial(ffn_kernel, step, before is not None),
        grid_spec=pltpu.PrefetchScalarGridSpec(
            num_scalar_prefetch=2,
            grid=(src.shape[0], 2 * per),
            in_specs=[
                once,
                once,
                pl.BlockSpec((2, 1, depth // 2, block), lambda p, i, f, t: (0, f[p], 0, i)),
                pl.BlockSpec((1, 1, block), lambda p, i, f, t: (f[p], 0, i)),
                pl.BlockSpec(
                    (1, 1, block, depth), lambda p, i, f, t: (i // per, f[p], i % per, 0)
                ),
            ]
            + ([] if before is None else [anywhere] * 3),
            out_specs=[anywhere] * 2
            + [
                pl.BlockSpec(
                    (1, 1, 2 * block, depth), lambda p, i, f, t: (i // per, t[p], i % per, 0)
                ),
                pl.BlockSpec((1, 1, block), lambda p, i, f, t: (p, 0, i)),
            ],
            scratch_shapes=[pltpu.VMEM((rows, depth), F32)] * 2
            + [pltpu.SemaphoreType.DMA((2, rows // step))],
        ),
        out_shape=[jax.ShapeDtypeStruct((rows, depth), F32)] * 2
        + [
            jax.ShapeDtypeStruct((2, parts, hidden + extra, depth), BF),
            jax.ShapeDtypeStruct((src.shape[0], 1, hidden), F32),
        ],
        input_output_aliases={} if before is None else {9: 2},
        compiler_params=params(),
        name=name,
        cost_estimate=cost(12 * rows * depth * hidden * src.shape[0], 8 * depth * hidden * src.shape[0]),
    )(src, dst, *operands)


def out_back_kernel(part_ref, near_ref, in_ref, grad_ref, sums_ref, out_ref):
    for side, mixed_ref in enumerate((near_ref, in_ref)):

        @pl.when(pl.program_id(0) == side)
        def _():
            out_ref[0, 0] = dot(mixed_ref[...], grad_ref[...]).astype(BF)


def out_back(mixed, grad, sums, extra, parts):
    heads, rows = mixed[0].shape
    total, depth = sums.shape[2:]
    piece = pl.BlockSpec((extra, rows), lambda p, c, t: (c, 0))
    return pl.pallas_call(
        out_back_kernel,
        grid_spec=pltpu.PrefetchScalarGridSpec(
            num_scalar_prefetch=1,
            grid=(2, 2),
            in_specs=[
                piece,
                piece,
                pl.BlockSpec((rows, depth), lambda p, c, t: (0, 0)),
                pl.BlockSpec(memory_space=pl.ANY),
            ],
            out_specs=pl.BlockSpec(
                (1, 1, extra, depth), lambda p, c, t: (c, t[p], total // extra - 1, 0)
            ),
        ),
        out_shape=jax.ShapeDtypeStruct(sums.shape, BF),
        input_output_aliases={4: 0},
        compiler_params=params(),
        name="out_back",
        cost_estimate=cost(4 * rows * depth * heads, 4 * heads * depth),
    )(parts, *mixed, grad, sums)


def project_back_kernel(*refs):
    out_ref = refs[-1]
    pairs = refs[:-2]
    total = dot(pairs[1][...], pairs[0][...])
    for i in range(2, len(pairs), 2):
        total = total + dot(pairs[i + 1][...], pairs[i][...])
    out_ref[...] = total.astype(BF)


def project_back(pairs, after):
    total = pairs[0][1].shape[0]
    depth = pairs[0][0].shape[1]
    block = total // 3
    specs, operands = [], []
    for x, grad, at in pairs:
        specs += [
            pl.BlockSpec(x.shape, lambda i: (0, 0)),
            pl.BlockSpec((block, x.shape[0]), functools.partial(lambda at, i: (i, at), at)),
        ]
        operands += [x, grad]
    return pl.pallas_call(
        project_back_kernel,
        grid=(3,),
        in_specs=specs + [pl.BlockSpec(memory_space=pl.ANY)],
        out_specs=pl.BlockSpec((block, depth), lambda i: (i, 0)),
        out_shape=jax.ShapeDtypeStruct((total, depth), BF),
        compiler_params=params(),
        name="project_back",
        cost_estimate=cost(4 * pairs[0][0].shape[0] * depth * total, 8 * depth * total),
    )(*operands, after)


def turn_kernel(x_ref, *out_refs):
    for i, out_ref in enumerate(out_refs):

        @pl.when(pl.program_id(0) == i)
        def _():
            out_ref[...] = x_ref[...].astype(F32).T


def turn(x, parts):
    rows, depth = x.shape
    block = rows // parts
    return pl.pallas_call(
        turn_kernel,
        grid=(parts,),
        in_specs=[pl.BlockSpec((block, depth), lambda i: (i, 0))],
        out_specs=[pl.BlockSpec((depth, block), lambda i: (0, 0))] * parts,
        out_shape=[jax.ShapeDtypeStruct((depth, block), F32)] * parts,
        compiler_params=params(),
        name="turn",
        cost_estimate=cost(rows * depth, 6 * rows * depth),
    )(x)


MESH = pl.DeviceIdType.MESH


def sum_all_kernel(
    big_ref, small_ref, out_ref, small_out_ref,
    buf, done, core_in, x_in, y_in, z_in, small, small_in, small_z, local, send, recv, small_send, small_recv,
):
    o, c, m = lax.axis_index("dpo"), lax.axis_index("core"), lax.axis_index("mp")
    y, z = lax.rem(o, 2), lax.div(o, 2)
    zs = 4
    half = buf.shape[0] // 2
    quarter, eighth, last = half // 2, half // 4, half // 16
    sibling = (o, 1 - c, m)
    across = (o, c, 1 - m)
    beside = (z * 2 + 1 - y, c, m)

    def along(j):
        return (j * 2 + y, c, m)

    load = pltpu.make_async_copy(big_ref, buf, local.at[0])
    load.start()
    barrier = pltpu.get_barrier_semaphore()
    others = [lax.rem(z + d, zs) for d in range(1, zs)]
    for device in [sibling, across, beside] + [along(j) for j in others]:
        pl.semaphore_signal(barrier, inc=1, device_id=device, device_id_type=MESH)
    pl.semaphore_wait(barrier, 6)
    small[0] = small_ref[...]
    load.wait()

    def copy(src, dst, i, device, sems=(send, recv)):
        return pltpu.make_async_remote_copy(
            src_ref=src, dst_ref=dst, send_sem=sems[0].at[i], recv_sem=sems[1].at[i],
            device_id=device, device_id_type=MESH,
        )

    def rows(first, n, of=buf):
        return of.at[pl.ds(pl.multiple_of(first, last), n)]

    def back(first, n, i, device):
        return copy(rows(first, n, done), rows(first, n, done), i, device)

    def add(first, n, arrived):
        step = min(128, n)

        def one(i, carry):
            there = pl.ds(pl.multiple_of(first + i * step, last), step)
            here = pl.ds(pl.multiple_of(i * step, step), step)
            buf[there, :] = (
                buf[there, :].astype(F32) + arrived[here, :].astype(F32)
            ).astype(BF)
            return carry

        lax.fori_loop(0, n // step, one, 0)

    started = []

    def go(*args, **kwargs):
        one = copy(*args, **kwargs)
        one.start()
        started.append(one)
        return one

    tiny = (small_send, small_recv)
    mine = c * half
    theirs = (1 - c) * half
    core_a = go(rows(theirs + (1 - m) * quarter, quarter), core_in.at[0], 0, sibling)
    core_b = go(rows(theirs + m * quarter, quarter), core_in.at[1], 1, sibling)
    tiny_core = go(small.at[0], small_in.at[0], 0, sibling, sems=tiny)
    base_far, base = mine + (1 - m) * quarter, mine + m * quarter
    core_a.wait_recv()
    add(base_far, quarter, core_in.at[0])
    x_a = go(rows(base_far + (1 - y) * eighth, eighth), x_in.at[0], 2, across)
    x_b = go(rows(base_far + y * eighth, eighth), x_in.at[1], 3, across)
    tiny_core.wait_recv()
    small[1] = small[0] + small_in[0]
    tiny_x = go(small.at[1], small_in.at[1], 1, across, sems=tiny)
    core_b.wait_recv()
    add(base, quarter, core_in.at[1])
    far_y, near_y = base + (1 - y) * eighth, base + y * eighth
    x_a.wait_recv()
    add(far_y, eighth, x_in.at[0])
    y_a = go(rows(far_y, eighth), y_in, 4, beside)
    tiny_x.wait_recv()
    small[2] = small[1] + small_in[1]
    tiny_y = go(small.at[2], small_in.at[2], 2, beside, sems=tiny)
    x_b.wait_recv()
    add(near_y, eighth, x_in.at[1])
    y_a.wait_recv()
    add(near_y, eighth, y_in)
    for d in range(1, zs):
        j = lax.rem(z + d, zs)
        there = copy(rows(near_y + j * last, last), z_in.at[z], 5 + z, along(j))
        there.start()
        started.append(there)
    tiny_y.wait_recv()
    small_z[z] = small[2] + small_in[2]
    for d in range(1, zs):
        j = lax.rem(z + d, zs)
        there = copy(small_z.at[z], small_z.at[z], 3 + z, along(j), sems=tiny)
        there.start()
        started.append(there)
    own = near_y + z * last
    total = buf[pl.ds(pl.multiple_of(own, last), last), :].astype(F32)
    for d in range(1, zs):
        j = lax.rem(z + d, zs)
        copy(rows(own, last), z_in.at[j], 5 + j, along(j)).wait_recv()
        total = total + z_in[j].astype(F32)
    done[pl.ds(pl.multiple_of(own, last), last), :] = total.astype(BF)

    def hand(first, n, i, device):
        one = back(first, n, i, device)
        one.start()
        started.append(one)
        return one

    for d in range(1, zs):
        hand(own, last, 9 + z, along(lax.rem(z + d, zs)))
    for d in range(1, zs):
        j = lax.rem(z + d, zs)
        back(near_y + j * last, last, 9 + j, along(j)).wait_recv()
    y_back = hand(near_y, eighth, 13, beside)
    x_back = hand(near_y, eighth, 14, across)
    core_back = hand(near_y, eighth, 15, sibling)
    y_back.wait_recv()
    x_more = hand(far_y, eighth, 16, across)
    core_more = hand(far_y, eighth, 17, sibling)
    x_back.wait_recv()
    core_x = hand(base_far + y * eighth, eighth, 18, sibling)
    x_more.wait_recv()
    core_y = hand(base_far + (1 - y) * eighth, eighth, 19, sibling)
    for d in range(1, zs):
        j = lax.rem(z + d, zs)
        copy(small_z.at[j], small_z.at[j], 3 + j, along(j), sems=tiny).wait_recv()
    small_out_ref[...] = (small_z[0] + small_z[1]) + (small_z[2] + small_z[3])
    for one in (core_back, core_more, core_x, core_y):
        one.wait_recv()
    for one in started:
        one.wait_send()
    store = pltpu.make_async_copy(done, out_ref, local.at[1])
    store.start()
    store.wait()


def sum_all(big, small):
    rows, width = big.shape
    quarter, eighth, last = rows // 4, rows // 8, rows // 32
    anywhere = pl.BlockSpec(memory_space=pl.ANY)
    whole = pl.BlockSpec(memory_space=pltpu.VMEM)
    dma = pltpu.SemaphoreType.DMA
    return pl.pallas_call(
        sum_all_kernel,
        in_specs=[anywhere, whole],
        out_specs=[anywhere, whole],
        out_shape=[
            jax.ShapeDtypeStruct(big.shape, BF),
            jax.ShapeDtypeStruct(small.shape, F32),
        ],
        scratch_shapes=[
            pltpu.VMEM((rows, width), BF),
            pltpu.VMEM((rows, width), BF),
            pltpu.VMEM((2, quarter, width), BF),
            pltpu.VMEM((2, eighth, width), BF),
            pltpu.VMEM((eighth, width), BF),
            pltpu.VMEM((4, last, width), BF),
            pltpu.VMEM((3,) + small.shape, F32),
            pltpu.VMEM((3,) + small.shape, F32),
            pltpu.VMEM((4,) + small.shape, F32),
            dma((2,)),
            dma((20,)),
            dma((20,)),
            dma((7,)),
            dma((7,)),
        ],
        compiler_params=pltpu.CompilerParams(
            collective_id=0, has_side_effects=True, vmem_limit_bytes=VMEM
        ),
        name="sum_all",
        cost_estimate=cost(rows * width, 8 * rows * width),
    )(big, small)


def join_back_kernel(grad_ref, w_ref, first_ref, second_ref):
    grad = grad_ref[...]
    width = first_ref.shape[1]
    first_ref[...] = dot_nt(grad, w_ref[:width, :])
    second_ref[...] = dot_nt(grad, w_ref[width:, :])


def join_back(grad, w):
    rows, depth = grad.shape
    width = w.shape[0] // 2
    block = min(256, rows)
    out = pl.BlockSpec((block, width), lambda i: (i, 0))
    return pl.pallas_call(
        join_back_kernel,
        grid=(rows // block,),
        in_specs=[
            pl.BlockSpec((block, depth), lambda i: (i, 0)),
            pl.BlockSpec(w.shape, lambda i: (0, 0)),
        ],
        out_specs=[out, out],
        out_shape=[jax.ShapeDtypeStruct((rows, width), F32)] * 2,
        compiler_params=params(),
        name="join_back",
        cost_estimate=cost(rows * depth * width, 8 * rows * width),
    )(grad, w)


def concat_back_kernel(x_ref, s_ref, grad_ref, out_ref):
    for i, ref in enumerate((x_ref, s_ref)):

        @pl.when(pl.program_id(0) == i)
        def _():
            out_ref[...] = dot_tn(ref[...], grad_ref[...]).astype(BF)


def concat_back(x, skip, grad):
    rows, width = grad.shape
    block = min(512, width)
    per = width // block
    return pl.pallas_call(
        concat_back_kernel,
        grid=(2, per),
        in_specs=[
            pl.BlockSpec((rows, block), lambda i, j: (0, jnp.where(i == 0, j, per - 1))),
            pl.BlockSpec((rows, block), lambda i, j: (0, jnp.where(i == 0, 0, j))),
            pl.BlockSpec((rows, width), lambda i, j: (0, 0)),
        ],
        out_specs=pl.BlockSpec((block, width), lambda i, j: (i * per + j, 0)),
        out_shape=jax.ShapeDtypeStruct((2 * width, width), BF),
        compiler_params=params(),
        name="concat_back",
        cost_estimate=cost(4 * rows * width * width, 8 * rows * width),
    )(x, skip, grad)


def hold_kernel(x_ref, *refs):
    refs[-1][...] = x_ref[...]


def hold(x, after):
    rows, width = x.shape
    block = rows // 9 if rows % 9 == 0 else rows
    piece = pl.BlockSpec((block, width), lambda i: (i, 0))
    return pl.pallas_call(
        hold_kernel,
        grid=(rows // block,),
        in_specs=[piece] + [pl.BlockSpec(memory_space=pl.ANY)] * len(after),
        out_specs=piece,
        out_shape=jax.ShapeDtypeStruct(x.shape, x.dtype),
        compiler_params=params(),
        name="hold",
        cost_estimate=cost(rows * width, 4 * rows * width),
    )(x, *after)


def unpack_kernel(core_ref, own_ref, sibling_ref, up_ref, down_ref):
    mine = core_ref[0] == pl.program_id(0)
    width = down_ref.shape[0]
    block = jnp.where(mine, own_ref[...].astype(F32), sibling_ref[...].astype(F32))
    up_ref[...] = block[:width].T
    down_ref[...] = block[width:]


def unpack(core, own, sibling, hidden):
    depth = own.shape[1]
    block = ffn_block(hidden)
    per = hidden // 2 // block
    piece = pl.BlockSpec((2 * block, depth), lambda c, i, k: (i, 0))
    return pl.pallas_call(
        unpack_kernel,
        grid_spec=pltpu.PrefetchScalarGridSpec(
            num_scalar_prefetch=1,
            grid=(2, per),
            in_specs=[piece, piece],
            out_specs=[
                pl.BlockSpec((depth, block), lambda c, i, k: (0, c * per + i)),
                pl.BlockSpec((block, depth), lambda c, i, k: (c * per + i, 0)),
            ],
        ),
        out_shape=[
            jax.ShapeDtypeStruct((depth, hidden), F32),
            jax.ShapeDtypeStruct((hidden, depth), F32),
        ],
        compiler_params=params(),
        name="unpack",
        cost_estimate=cost(depth * hidden, 12 * depth * hidden),
    )(core, own, sibling)


def body(
    inputs, skip_in, cotangent, lengths, w_concat, b_concat, gain_attn, w_query, w_key, w_value,
    w_out, b_out, gain_ffn, w_up, b_up, w_down, b_down,
):
    parts = lax.axis_size("mp")
    rank = lax.axis_index("mp")
    core = lax.axis_index("core")
    dp = ("dpo", "core")
    rows, width = inputs.shape
    group = rows * parts
    paired = parts == 2 and group == 4096
    ends, pos_all, valid_all = layout(lengths[0], group)
    valid_here = lax.dynamic_slice_in_dim(valid_all, rank * rows, rows, 0)[:, None]
    each, hidden = w_out.shape[0], b_up.shape[0]
    extra = each // 2
    index = rank.reshape(1)
    other = 1 - index
    zero = jnp.zeros((1,), jnp.int32)

    def across(x):
        return lax.ppermute(x, "mp", [(0, 1), (1, 0)])

    def piece(x, i, size, axis=0):
        return lax.dynamic_slice_in_dim(x, i * size, size, axis)

    def order(near, far, axis):
        return jnp.where(
            rank == 0, jnp.concatenate([near, far], axis), jnp.concatenate([far, near], axis)
        )

    def core_half(w):
        return piece(w, core, w.shape[0] // 2)

    def gather(half):
        return lax.all_gather(half, ("core", "mp"), axis=0).reshape((2, parts) + half.shape)

    w_turned = jnp.concatenate([w_query.T, w_key.T, w_value.T], axis=0)
    grad_rows = cotangent.astype(F32) * valid_here
    grad_low = grad_rows.astype(BF)
    half_up, half_down = core_half(w_up), core_half(w_down)
    if paired:
        bias_far, out_far = across(b_up), across(w_out)
        h0, n1 = enter(inputs, skip_in, w_concat, b_concat, gain_attn, 0, rows)
        n1, bias_far, out_far = lax.optimization_barrier((n1, bias_far, out_far))
        n1_far = across(n1)
        tables_near = tables(piece(pos_all, rank, rows))
        q_near, k_near, v_near = project(n1, w_turned, *tables_near)
        start = attend_half(
            "near_near", ends, index, q_near, False, {0: (k_near, v_near)}, last=False
        )
        tables_far = tables(piece(pos_all, 1 - rank, rows))
        n1_far, start, half_up, half_down = lax.optimization_barrier(
            (n1_far, start, half_up, half_down)
        )
        up_all, down_all = gather(half_up), gather(half_down)
        q_far, k_far, v_far = project(n1_far, w_turned, *tables_far)
        mixed_far, log_far = attend_half(
            "far_all", ends, index, q_far, True, {0: (k_near, v_near), 1: (k_far, v_far)}
        )
        mixed_in = across(mixed_far)
        mixed_near, log_near = attend_half(
            "near_far", ends, index, q_near, False, {1: (k_far, v_far)}, carry=start
        )
        h1, n2 = upper(h0, mixed_near, mixed_in, w_out, out_far, b_out, gain_ffn)
        branch, grad_n2, sums, bias_near = ffn(
            "ffn_near", n2, grad_low, w_up.reshape(2, 1, width // 2, hidden),
            b_up.reshape(1, 1, hidden), w_down.reshape(2, 1, hidden // 2, width),
            extra, parts, zero, index,
        )
        both = jnp.stack([bias_far, bias_far]).reshape(2, 1, hidden)
        branch, grad_n2, sums, grad_bias = ffn(
            "ffn_far", n2, grad_low, up_all, both, down_all, extra, parts, other, other,
            before=(branch, grad_n2, sums),
        )
        grad_bias = order(bias_near, grad_bias, 0)
        output, grad_h1, grad_h1_low, grad_near, grad_sent, early = middle(
            h1, branch, grad_n2, cotangent, valid_here, b_down, gain_ffn, w_out, out_far
        )
        grad_far = across(grad_sent)
        sums = out_back(
            (mixed_near, mixed_in), grad_h1_low, sums, extra, jnp.concatenate([index, other])
        )
    else:
        joined = jnp.concatenate([inputs, skip_in], axis=1)
        h0 = dot(joined, w_concat) + b_concat
        scale_one = lax.rsqrt(jnp.mean(h0 * h0, axis=-1, keepdims=True) + EPS)
        n1 = (h0 * scale_one * gain_attn).astype(BF)
        n1_all = lax.all_gather(n1, "mp", axis=0, tiled=True)
        bias_all = lax.all_gather(b_up, "mp", axis=0).reshape(parts, 1, -1)
        w_out_all = lax.all_gather(w_out, "mp", axis=0, tiled=True)
        up_all, down_all = gather(half_up), gather(half_down)
        cosine, sine = tables(pos_all)
        query, keys, values = project(n1_all, w_turned, cosine, sine)
        mixed, logsum = attend(ends, zero, query, keys, values, 1)
        mixed_rows = lax.all_to_all(mixed, "mp", 1, 0, tiled=True)
        h1 = h0 + dot_tn(mixed_rows, w_out_all) + b_out
        scale_two = lax.rsqrt(jnp.mean(h1 * h1, axis=-1, keepdims=True) + EPS)
        n2 = (h1 * scale_two * gain_ffn).astype(BF)
        every = jnp.arange(parts, dtype=jnp.int32)
        branch, grad_n2, sums, grad_bias = ffn(
            "ffn", n2, grad_low, up_all, bias_all, down_all, extra, parts, every, every
        )
        output = valid_here * (h1 + branch + b_down)
        grad_h1, grad_gain_ffn = norm_back(grad_n2, h1, scale_two, gain_ffn)
        grad_h1 = grad_h1 + grad_rows
        grad_h1_low = grad_h1.astype(BF)
        grad_mixed = lax.all_to_all(
            dot_nt(w_out_all, grad_h1_low).astype(BF), "mp", 0, 1, tiled=True
        )
        grad_out = dot(mixed_rows, grad_h1_low).astype(BF)
        grad_out = grad_out.reshape(parts, 2, extra, width).transpose(1, 0, 2, 3)
        sums = lax.dynamic_update_slice(sums, grad_out, (0, 0, hidden, 0))
        early = jnp.stack([jnp.sum(grad_rows, 0), grad_gain_ffn, jnp.sum(grad_h1, 0)])
    def unpack_all(own):
        sibling = lax.ppermute(own, "core", [(0, 1), (1, 0)])
        up, down = unpack(core.reshape(1), own, sibling, hidden)
        first, second = own[hidden:].astype(F32), sibling[hidden:].astype(F32)
        out = jnp.where(
            core == 0, jnp.concatenate([first, second]), jnp.concatenate([second, first])
        )
        return up, down, out

    part = lax.psum_scatter(
        sums.reshape((2 * parts,) + sums.shape[2:]), ("core", "mp"), scatter_dimension=0, tiled=True
    )[0]
    summed = lax.psum(part, "dpo")
    if paired:
        near = (q_near, k_near, v_near, grad_near, mixed_near, log_near) + tables_near
        far = (q_far, k_far, v_far, grad_far, mixed_far, log_far) + tables_far
        heads = each // HEAD_DIM
        back = functools.partial(half_back, ends=ends, rank=index)
        both = (near, far)
        middle_head = heads // 2
        opening = back("back_near0", sides=(near,), first=0, count=middle_head, finish=False)[0]
        written, at = (), 0
        quarter = middle_head // 4
        for i, count in enumerate((2 * quarter, quarter, middle_head - 3 * quarter)):
            written = back(
                f"back_first{i}", sides=both, first=at, count=count, finish=True,
                partial=opening, written=written, after=part if i == 2 else None,
            )
            at += count
        back_far, back_near = written
        partial = None
        for i in range(2):
            back_far, partial = back(
                f"back_second{i}", sides=both, first=at, count=middle_head // 2, finish=False,
                written=(back_far, partial),
            )
            at += middle_head // 2
        back_far = back_far.reshape(3 * each, rows)
        grad_far_rows = dot_tn(back_far, w_turned).astype(BF)
        sent = across(grad_far_rows)
        back_near = back(
            "back_near1", sides=(near,), first=middle_head, count=heads - middle_head, finish=True,
            partial=partial, written=(back_near,), after=grad_far_rows,
        )[0].reshape(3 * each, rows)
        pairs = [(n1, back_near, 0), (n1_far, back_far, 0)]
        grad_qkv = project_back(pairs, index)
        grad_up, grad_down, grad_out = unpack_all(hold(summed, (grad_qkv, sent)))
        grad_h0_low, late = leave(
            back_near, w_turned, sent, h0, grad_h1, gain_attn, (grad_qkv,)
        )
    else:
        back = attend_back(ends, query, keys, values, grad_mixed, mixed, logsum, cosine, sine)
        grad_n1 = dot_tn(back, w_turned).astype(BF)
        grad_n1 = lax.psum_scatter(grad_n1, "mp", scatter_dimension=0, tiled=True).astype(F32)
        grad_up, grad_down, grad_out = unpack_all(summed)
        grad_qkv = project_back([(n1_all, back, 0)], index)
        grad_h0, grad_gain_attn = norm_back(grad_n1, h0, scale_one, gain_attn)
        grad_h0_low = (grad_h0 + grad_h1).astype(BF)
        late = jnp.stack([jnp.sum(grad_h0_low.astype(F32), axis=0), grad_gain_attn])
    grad_w_concat = concat_back(inputs, skip_in, grad_h0_low)
    small = jnp.concatenate([early, late, grad_bias.reshape(-1, width)])
    small = jnp.pad(small, ((0, -small.shape[0] % 8), (0, 0)))
    if paired and lax.axis_size("dpo") == 8:
        tail, small = sum_all(grad_w_concat, small)
        grad_qkv = lax.psum(grad_qkv, dp)
    else:
        tail, small = lax.psum((grad_w_concat, small), dp + ("mp",))
        grad_qkv = lax.psum(grad_qkv, dp)
    grad_inputs, grad_skip = join_back(grad_h0_low, w_concat)
    grad_query, grad_key, grad_value = turn(grad_qkv, 3)
    return (
        output,
        grad_inputs,
        grad_skip,
        tail.astype(F32),
        small[3],
        small[4],
        grad_query,
        grad_key,
        grad_value,
        grad_out,
        small[2],
        small[1],
        grad_up,
        piece(small[5 : 5 + parts * hidden // width].reshape(-1), rank, hidden),
        grad_down,
        small[0],
    )


def solution(mesh):
    dp, mp = mesh.shape["dp"], mesh.shape["mp"]
    mesh = Mesh(mesh.devices.reshape(dp // 2, 2, mp), ("dpo", "core", "mp"))
    rows = P(("dpo", "core", "mp"), None)
    columns = P(None, "mp")
    upright = P("mp", None)
    return jax.shard_map(
        body,
        mesh=mesh,
        in_specs=(
            rows, rows, rows, P(("dpo", "core"), None), P(), P(), P(), columns, columns, columns,
            upright, P(), P(), columns, P("mp"), upright, P(),
        ),
        out_specs=(
            rows, rows, rows, P(), P(), P(), columns, columns, columns,
            upright, P(), P(), columns, P("mp"), upright, P(),
        ),
        check_vma=False,
    )
```

```python
import functools

import jax
import jax.numpy as jnp
from jax import lax
from jax.experimental import pallas as pl
from jax.experimental.pallas import tpu as pltpu
from jax.sharding import Mesh
from jax.sharding import PartitionSpec as P

HEAD_DIM = 64
HALF = HEAD_DIM // 2
EPS = 1e-06
FIRST_LEAST = 3712
FIRST_MOST = 3840
SEGS = 16
LOG2E = 1.4426950408889634
LN2 = 0.6931471805599453
VMEM = 60 * 2**20

BF = jnp.bfloat16
F32 = jnp.float32


def dot(left, right, dims=((1,), (0,))):
    return lax.dot_general(left, right, (dims, ((), ())), preferred_element_type=F32)


def dot_tn(left, right):
    return dot(left, right, ((0,), (0,)))


def dot_nt(left, right):
    return dot(left, right, ((1,), (1,)))


def layout(lengths_row, count):
    ends = jnp.cumsum(lengths_row)
    starts = ends - lengths_row
    places = jnp.arange(count, dtype=jnp.int32)
    seg = jnp.sum((places[:, None] >= ends[None, :]).astype(jnp.int32), axis=1)
    owner = seg[:, None] == jnp.arange(lengths_row.shape[0], dtype=jnp.int32)[None, :]
    start_of = jnp.sum(jnp.where(owner, starts[None, :], 0), axis=1)
    pos = (places - start_of).astype(F32)
    valid = (places < ends[-1]).astype(F32)
    return (ends.astype(jnp.int32), pos, valid)


def tables(pos):
    freq = jnp.exp(-jnp.log(10000.0) * jnp.arange(HALF, dtype=F32) * 2.0 / HEAD_DIM)
    angle = freq[:, None] * pos[None, :]
    return (jnp.cos(angle), jnp.sin(angle))


def norm_back(grad, stream, scale, gain):
    tilted = grad * gain
    grad_gain = jnp.sum(grad * stream * scale, axis=0)
    grad_stream = scale * tilted - stream * scale**3 * jnp.mean(
        tilted * stream, axis=-1, keepdims=True
    )
    return (grad_stream, grad_gain)


def params():
    return pltpu.CompilerParams(vmem_limit_bytes=VMEM)


def cost(flops, moved):
    return pl.CostEstimate(flops=flops // 64, bytes_accessed=moved // 64, transcendentals=0)


def project_kernel(x_ref, w_ref, cos_ref, sin_ref, *refs):
    q_ref, k_ref, v_ref = refs[-3:]
    x = x_ref[...]
    c, s = cos_ref[...], sin_ref[...]
    width = q_ref.shape[0]
    for out, first, factor in ((q_ref, 0, 0.125 * LOG2E), (k_ref, width, 1.0)):
        t = dot_nt(w_ref[first : first + width, :], x)
        for h in range(0, width, HEAD_DIM):
            a, b = t[h : h + HALF], t[h + HALF : h + HEAD_DIM]
            out[h : h + HALF, :] = ((a * c - b * s) * factor).astype(BF)
            out[h + HALF : h + HEAD_DIM, :] = ((b * c + a * s) * factor).astype(BF)
    v_ref[...] = dot_nt(w_ref[2 * width :, :], x).astype(BF)


def project(x, w, cosine, sine, after=()):
    count, depth = x.shape
    width = w.shape[0] // 3
    block = min(512, count)
    table = pl.BlockSpec((HALF, block), lambda i: (0, i))
    out = pl.BlockSpec((width, block), lambda i: (0, i))
    return pl.pallas_call(
        project_kernel,
        grid=(count // block,),
        in_specs=[
            pl.BlockSpec((block, depth), lambda i: (i, 0)),
            pl.BlockSpec(w.shape, lambda i: (0, 0)),
            table,
            table,
        ]
        + [pl.BlockSpec(memory_space=pl.ANY)] * len(after),
        out_specs=[out] * 3,
        out_shape=[jax.ShapeDtypeStruct((width, count), BF)] * 3,
        compiler_params=params(),
        name="project",
    )(x, w, cosine, sine, *after)


def scale_of(stream):
    return lax.rsqrt(jnp.mean(stream * stream, axis=-1, keepdims=True) + EPS)


def norm_back_rows(grad, stream, gain):
    scale = scale_of(stream)
    tilted = grad * gain
    back = scale * tilted - stream * (scale * scale * scale) * jnp.mean(
        tilted * stream, axis=-1, keepdims=True
    )
    return back, jnp.sum(grad * stream * scale, axis=0, keepdims=True)


def add_up(ref, terms):
    for i, term in enumerate(terms):

        @pl.when(pl.program_id(0) == 0)
        def _():
            ref[i : i + 1, :] = term

        @pl.when(pl.program_id(0) > 0)
        def _():
            ref[i : i + 1, :] += term


def row_specs(rows, width, block, first=0):
    def tall(columns=width):
        return pl.BlockSpec((block, columns), lambda i: (i + first, 0))

    def whole(*shape):
        return pl.BlockSpec(shape, lambda i: (0, 0))

    return tall, whole


def enter_kernel(x_ref, s_ref, w_ref, b_ref, gain_ref, *refs):
    h_ref, n_ref = refs[-2:]
    width = x_ref.shape[1]
    h = dot(x_ref[...], w_ref[:width, :]) + dot(s_ref[...], w_ref[width:, :]) + b_ref[...]
    h_ref[...] = h
    n_ref[...] = (h * scale_of(h) * gain_ref[...]).astype(BF)


def enter(x, skip, w, bias, gain, first, count, written=()):
    rows, width = x.shape
    block = min(512, count)
    tall, whole = row_specs(rows, width, block, first // block)
    return pl.pallas_call(
        enter_kernel,
        grid=(count // block,),
        in_specs=[tall(), tall(), whole(*w.shape), whole(1, width), whole(1, width)]
        + [pl.BlockSpec(memory_space=pl.ANY)] * len(written),
        out_specs=[tall(), tall()],
        out_shape=[jax.ShapeDtypeStruct((rows, width), F32), jax.ShapeDtypeStruct((rows, width), BF)],
        input_output_aliases={5 + i: i for i in range(len(written))},
        compiler_params=params(),
        name="enter",
        cost_estimate=cost(4 * count * width * width, 10 * count * width),
    )(x, skip, w, bias[None], gain[None], *written)


def upper_kernel(h_ref, near_ref, in_ref, own_ref, far_ref, b_ref, gain_ref, h1_ref, n_ref):
    h = h_ref[...] + dot_tn(near_ref[...], own_ref[...]) + dot_tn(in_ref[...], far_ref[...])
    h = h + b_ref[...]
    h1_ref[...] = h
    n_ref[...] = (h * scale_of(h) * gain_ref[...]).astype(BF)


def upper(h0, near, arrived, own, far, bias, gain):
    rows, width = h0.shape
    block = min(512, rows)
    tall, whole = row_specs(rows, width, block)
    flat = pl.BlockSpec((near.shape[0], block), lambda i: (0, i))
    return pl.pallas_call(
        upper_kernel,
        grid=(rows // block,),
        in_specs=[
            tall(), flat, flat, whole(*own.shape), whole(*far.shape), whole(1, width), whole(1, width)
        ],
        out_specs=[tall(), tall()],
        out_shape=[jax.ShapeDtypeStruct((rows, width), F32), jax.ShapeDtypeStruct((rows, width), BF)],
        compiler_params=params(),
        name="upper",
        cost_estimate=cost(2 * rows * width * width, 12 * rows * width),
    )(h0, near, arrived, own, far, bias[None], gain[None])


def middle_kernel(
    h_ref, branch_ref, dn_ref, g_ref, valid_ref, bias_ref, gain_ref, own_ref, far_ref,
    out_ref, dh_ref, low_ref, near_ref, sent_ref, sums_ref,
):
    valid = valid_ref[...]
    h = h_ref[...]
    out_ref[...] = valid * (h + branch_ref[...] + bias_ref[...])
    g = g_ref[...].astype(F32) * valid
    back, gain_sum = norm_back_rows(dn_ref[...], h, gain_ref[...])
    dh = g + back
    dh_ref[...] = dh
    low = dh.astype(BF)
    low_ref[...] = low
    near_ref[...] = dot_nt(own_ref[...], low).astype(BF)
    sent_ref[...] = dot_nt(far_ref[...], low).astype(BF)
    add_up(
        sums_ref,
        [jnp.sum(g, 0, keepdims=True), gain_sum, jnp.sum(dh, 0, keepdims=True)],
    )


def middle(h1, branch, dn, cotangent, valid, bias, gain, own, far):
    rows, width = h1.shape
    block = min(512, rows)
    tall, whole = row_specs(rows, width, block)
    flat = pl.BlockSpec((own.shape[0], block), lambda i: (0, i))
    return pl.pallas_call(
        middle_kernel,
        grid=(rows // block,),
        in_specs=[tall(), tall(), tall(), tall(), tall(1), whole(1, width), whole(1, width)]
        + [whole(*own.shape)] * 2,
        out_specs=[tall(), tall(), tall(), flat, flat, whole(3, width)],
        out_shape=[
            jax.ShapeDtypeStruct((rows, width), F32),
            jax.ShapeDtypeStruct((rows, width), F32),
            jax.ShapeDtypeStruct((rows, width), BF),
            jax.ShapeDtypeStruct((own.shape[0], rows), BF),
            jax.ShapeDtypeStruct((own.shape[0], rows), BF),
            jax.ShapeDtypeStruct((3, width), F32),
        ],
        compiler_params=params(),
        name="middle",
        cost_estimate=cost(2 * rows * width * width, 24 * rows * width),
    )(h1, branch, dn, cotangent, valid, bias[None], gain[None], own, far)


def leave_kernel(back_ref, w_ref, sent_ref, h_ref, dh_ref, gain_ref, *refs):
    low_ref, sums_ref = refs[-2:]
    grad = dot_tn(back_ref[...], w_ref[...]) + sent_ref[...].astype(F32)
    back, gain_sum = norm_back_rows(grad, h_ref[...], gain_ref[...])
    low = (back + dh_ref[...]).astype(BF)
    low_ref[...] = low
    add_up(sums_ref, [jnp.sum(low.astype(F32), 0, keepdims=True), gain_sum])


def leave(back, w, sent, h0, dh1, gain, after):
    rows, width = h0.shape
    block = min(512, rows)
    tall, whole = row_specs(rows, width, block)
    return pl.pallas_call(
        leave_kernel,
        grid=(rows // block,),
        in_specs=[
            pl.BlockSpec((back.shape[0], block), lambda i: (0, i)),
            whole(*w.shape),
            tall(),
            tall(),
            tall(),
            whole(1, width),
        ]
        + [pl.BlockSpec(memory_space=pl.ANY)] * len(after),
        out_specs=[tall(), whole(2, width)],
        out_shape=[
            jax.ShapeDtypeStruct((rows, width), BF),
            jax.ShapeDtypeStruct((2, width), F32),
        ],
        compiler_params=params(),
        name="leave",
        cost_estimate=cost(2 * rows * width * back.shape[0], 16 * rows * width),
    )(back, w, sent, h0, dh1, gain[None], *after)


def segments(ends_ref, first, count):
    pos = lax.broadcasted_iota(jnp.int32, (1, count), 1) + first
    seg = jnp.zeros((1, count), jnp.int32)
    for i in range(ends_ref.shape[0]):
        seg = seg + (pos >= ends_ref[i]).astype(jnp.int32)
    return lax.broadcasted_iota(jnp.int32, (SEGS, 1), 0) == seg


def zeros(rows, count):
    return jnp.zeros((rows, count), F32)


def key_pieces(count):
    if count == 4096:
        main = [(k0, 384) for k0 in range(0, FIRST_MOST, 384)]
        whole = [(k0, 1024) for k0 in range(0, count, 1024)]
        return [
            (0, 2048, main),
            (2048, 1536, main),
            (3584, 256, whole),
            (FIRST_MOST, 256, [(FIRST_LEAST, count - FIRST_LEAST)]),
        ]
    step = min(512, count)
    every = [(k0, step) for k0 in range(0, count, step)]
    return [(q0, step, every) for q0 in range(0, count, step)]


def attend_kernel(cut, ends_ref, part_ref, q_ref, k_ref, v_ref, o_ref, l_ref, kaug, qaug, vaug):
    count = k_ref.shape[1]
    here = q_ref.shape[1]
    part = part_ref[0]
    same = segments(ends_ref, 0, count)
    kaug[...] = (
        jnp.concatenate([k_ref[...].astype(F32), jnp.where(same, 0.0, -1e30), zeros(48, count)], 0)
        .T.astype(BF)
    )
    mine = segments(ends_ref, part * here, here)
    qaug[...] = jnp.concatenate(
        [q_ref[...].astype(F32), jnp.where(mine, 1.0, 0.0), zeros(48, here)], 0
    ).astype(BF)
    first = lax.broadcasted_iota(jnp.int32, (SEGS, count), 0) == 0
    vaug[...] = jnp.concatenate([v_ref[...].astype(F32), jnp.where(first, 1.0, 0.0)], 0).astype(BF)

    def block(q0, width, pieces):
        queries = qaug[:, q0 : q0 + width]
        top = jnp.full((1, width), -jnp.inf, F32)
        acc = jnp.zeros((HEAD_DIM + SEGS, width), F32)
        for k0, n in pieces:
            scores = dot(kaug[k0 : k0 + n, :], queries)
            higher = jnp.maximum(top, jnp.max(scores, axis=0, keepdims=True))
            probs = jnp.exp2(scores - higher).astype(BF)
            acc = acc * jnp.exp2(top - higher) + dot(vaug[:, k0 : k0 + n], probs)
            top = higher
        total = acc[HEAD_DIM : HEAD_DIM + 1]
        o_ref[:, q0 : q0 + width] = (acc[:HEAD_DIM] / total).astype(BF)
        l_ref[0, :, q0 : q0 + width] = top + jnp.log2(total)

    pieces = key_pieces(count)
    for p in range(cut):
        low, high = p * here, (p + 1) * here

        @pl.when(part == p)
        def _():
            for q0, width, keys in pieces:
                if low <= q0 < high:
                    block(q0 - low, width, keys)


def attend(ends, part, query, keys, values, cut):
    rows, count = query.shape
    heads = rows // HEAD_DIM
    here = count // cut
    whole = pl.BlockSpec((HEAD_DIM, count), lambda h, e, p: (h, 0))
    return pl.pallas_call(
        functools.partial(attend_kernel, cut),
        grid_spec=pltpu.PrefetchScalarGridSpec(
            num_scalar_prefetch=2,
            grid=(heads,),
            in_specs=[
                pl.BlockSpec((HEAD_DIM, here), lambda h, e, p: (h, p[0])),
                whole,
                whole,
            ],
            out_specs=[
                pl.BlockSpec((HEAD_DIM, here), lambda h, e, p: (h, 0)),
                pl.BlockSpec((1, 1, here), lambda h, e, p: (h, 0, 0)),
            ],
            scratch_shapes=[
                pltpu.VMEM((count, 128), BF),
                pltpu.VMEM((128, here), BF),
                pltpu.VMEM((HEAD_DIM + SEGS, count), BF),
            ],
        ),
        out_shape=[
            jax.ShapeDtypeStruct((rows, here), BF),
            jax.ShapeDtypeStruct((heads, 1, here), F32),
        ],
        compiler_params=params(),
        name="attend",
        cost_estimate=cost(4 * rows * here * count, 8 * rows * count),
    )(ends, part, query, keys, values)


def local_segments(ends_ref, part, count):
    return segments(ends_ref, part * count, count)


def spans(first, last, step):
    return [(k0, min(step, last - k0)) for k0 in range(first, last, step)]


def regions(query_part, key_parts, half):
    edge, start = FIRST_MOST - half, FIRST_LEAST - half

    def keys(first, last, p):
        return [(p, k0, n) for k0, n in spans(first, last, 1024)]

    if query_part == 0:
        found = []
        for p in key_parts:
            found += keys(0, half, 0) if p == 0 else keys(0, edge, 1)
        return [(0, half, found)]
    low = edge - 256
    if list(key_parts) == [0]:
        return [(0, edge, keys(0, half, 0)), (edge, half - edge, [])]
    main, mixed, last = [], [], []
    for p in key_parts:
        if p == 0:
            main += keys(0, half, 0)
            mixed += keys(0, half, 0)
        else:
            main += keys(0, edge, 1)
            mixed += keys(0, half, 1)
            last += [(1, start, half - start)]
    return [(0, low, main), (low, 256, mixed), (edge, half - edge, last)]


def half_kernel(query_far, key_sides, given, last, ends_ref, part_ref, *refs):
    refs = list(refs)
    q_ref = refs.pop(0)
    kv = {side: (refs.pop(0), refs.pop(0)) for side in key_sides}
    acc_in, top_in = (refs.pop(0), refs.pop(0)) if given else (None, None)
    out_ref, top_ref = refs.pop(0), refs.pop(0)
    qaug = refs.pop(0)
    kaug = {side: refs.pop(0) for side in key_sides}
    vaug = {side: refs.pop(0) for side in key_sides}
    half = q_ref.shape[1]
    rank = part_ref[0]

    @pl.when(pl.program_id(0) == 0)
    def _():
        for side in key_sides:
            same = local_segments(ends_ref, rank if side == 0 else 1 - rank, half)
            blank = zeros(HEAD_DIM, half)
            kaug[side][...] = (
                jnp.concatenate([blank, jnp.where(same, 0.0, -1e30), zeros(48, half)], 0)
                .T.astype(BF)
            )
            first = lax.broadcasted_iota(jnp.int32, (SEGS, half), 0) == 0
            vaug[side][HEAD_DIM:, :] = jnp.where(first, 1.0, 0.0).astype(BF)
        mine = local_segments(ends_ref, 1 - rank if query_far else rank, half)
        qaug[HEAD_DIM:, :] = jnp.concatenate(
            [jnp.where(mine, 1.0, 0.0), zeros(48, half)], 0
        ).astype(BF)

    for side in key_sides:
        kaug[side][:, :HEAD_DIM] = kv[side][0][...].T
        vaug[side][:HEAD_DIM, :] = kv[side][1][...]
    qaug[:HEAD_DIM, :] = q_ref[...]

    for here in range(2):
        query_part = 1 - here if query_far else here
        part_of = {side: here if side == 0 else 1 - here for side in key_sides}
        side_of = {p: side for side, p in part_of.items()}

        @pl.when(rank == here)
        def _():
            for q0, width, pieces in regions(query_part, list(side_of), half):
                there = slice(q0, q0 + width)
                queries = qaug[:, there]
                if given:
                    top, acc = top_in[0, :, there], acc_in[0, :, there]
                else:
                    top = jnp.full((1, width), -jnp.inf, F32)
                    acc = jnp.zeros((HEAD_DIM + SEGS, width), F32)
                for p, k0, n in pieces:
                    side = side_of[p]
                    scores = dot(kaug[side][k0 : k0 + n, :], queries)
                    higher = jnp.maximum(top, jnp.max(scores, axis=0, keepdims=True))
                    probs = jnp.exp2(scores - higher).astype(BF)
                    acc = acc * jnp.exp2(top - higher) + dot(vaug[side][:, k0 : k0 + n], probs)
                    top = higher
                if last:
                    total = acc[HEAD_DIM : HEAD_DIM + 1]
                    out_ref[:, there] = (acc[:HEAD_DIM] / total).astype(BF)
                    top_ref[0, :, there] = top + jnp.log2(total)
                else:
                    out_ref[0, :, there] = acc
                    top_ref[0, :, there] = top


def attend_half(name, ends, rank, query, query_far, keys, carry=None, last=True):
    rows, half = query.shape
    heads = rows // HEAD_DIM
    sides = sorted(keys)
    head = pl.BlockSpec((HEAD_DIM, half), lambda h, e, r: (h, 0))
    tall = pl.BlockSpec((1, HEAD_DIM + SEGS, half), lambda h, e, r: (h, 0, 0))
    line = pl.BlockSpec((1, 1, half), lambda h, e, r: (h, 0, 0))
    operands = [query]
    for side in sides:
        operands += list(keys[side])
    specs = [head] * len(operands)
    if carry is not None:
        operands += list(carry)
        specs += [tall, line]
    return pl.pallas_call(
        functools.partial(half_kernel, query_far, sides, carry is not None, last),
        grid_spec=pltpu.PrefetchScalarGridSpec(
            num_scalar_prefetch=2,
            grid=(heads,),
            in_specs=specs,
            out_specs=[head if last else tall, line],
            scratch_shapes=[pltpu.VMEM((128, half), BF)]
            + [pltpu.VMEM((half, 128), BF)] * len(sides)
            + [pltpu.VMEM((HEAD_DIM + SEGS, half), BF)] * len(sides),
        ),
        out_shape=[
            jax.ShapeDtypeStruct((rows, half), BF)
            if last
            else jax.ShapeDtypeStruct((heads, HEAD_DIM + SEGS, half), F32),
            jax.ShapeDtypeStruct((heads, 1, half), F32),
        ],
        compiler_params=params(),
        name=name,
        cost_estimate=cost(16 * rows * half * half * len(sides), 8 * rows * half),
    )(ends, rank, *operands)


def split3(x):
    a = x.astype(BF).astype(F32)
    b = (x - a).astype(BF).astype(F32)
    row = lax.broadcasted_iota(jnp.int32, (SEGS, 1), 0)
    return jnp.where(row == 0, a, jnp.where(row == 1, b, jnp.where(row == 2, x - a - b, 0.0)))


def attend_back_kernel(
    ends_ref, q_ref, k_ref, v_ref, g_ref, o_ref, l_ref, cos_ref, sin_ref, d_ref,
    kaug, vaug, qaug, gaug, pair, dq,
):
    count = k_ref.shape[1]
    same = segments(ends_ref, 0, count)
    row = lax.broadcasted_iota(jnp.int32, (SEGS, count), 0)
    shift = jnp.where(row < 3, 1.0, 0.0)
    g = g_ref[...].astype(F32)
    q = q_ref[...].astype(F32)
    delta = jnp.sum(g * o_ref[...].astype(F32), axis=0, keepdims=True)
    kaug[...] = (
        jnp.concatenate(
            [k_ref[...].astype(F32), jnp.where(same, 0.0, -1e30), shift, zeros(32, count)], 0
        )
        .T.astype(BF)
    )
    vaug[...] = (
        jnp.concatenate([v_ref[...].astype(F32), shift, zeros(48, count)], 0).T.astype(BF)
    )
    qaug[...] = jnp.concatenate(
        [q, jnp.where(same, 1.0, 0.0), split3(-l_ref[0]), zeros(32, count)], 0
    ).astype(BF)
    gaug[...] = jnp.concatenate([g, split3(-delta), zeros(48, count)], 0).astype(BF)
    pair[...] = jnp.concatenate([q, g], 0).T.astype(BF)
    dq[...] = jnp.zeros_like(dq)

    def turn(grad, c, s, factor):
        a, b = grad[:HALF], grad[HALF:]
        return (
            jnp.concatenate([a * c + b * s, b * c - a * s], 0) * factor
        ).astype(BF)

    def chunk(k0, n, queries):
        where = pl.ds(k0, n)
        kb, vb, kt = kaug[where, :], vaug[where, :], k_ref[:, where]
        dk = jnp.zeros((n, HEAD_DIM), F32)
        dv = jnp.zeros((n, HEAD_DIM), F32)
        for q0, width in queries:
            there = slice(q0, q0 + width)
            probs = jnp.exp2(dot(kb, qaug[:, there]))
            tilt = (probs * dot(vb, gaug[:, there])).astype(BF)
            dv = dv + dot(probs.astype(BF), pair[there, HEAD_DIM:])
            dk = dk + dot(tilt, pair[there, :HEAD_DIM])
            dq[:, there] += dot(kt, tilt)
        c, s = cos_ref[:, where], sin_ref[:, where]
        d_ref[1, 0, :, where] = turn(dk.T, c, s, LN2)
        d_ref[2, 0, :, where] = dv.T.astype(BF)

    if count == 4096:
        main = [(q0, 1920) for q0 in range(0, FIRST_MOST, 1920)]

        def step(i, carry):
            chunk(pl.multiple_of(i * 512, 512), 512, main)
            return carry

        lax.fori_loop(0, 7, step, 0)
        chunk(3584, 256, [(q0, 1024) for q0 in range(0, count, 1024)])
        chunk(FIRST_MOST, count - FIRST_MOST, [(3584, 512)])
    else:
        size = min(512, count)

        def step(i, carry):
            chunk(pl.multiple_of(i * size, size), size, [(q, size) for q in range(0, count, size)])
            return carry

        lax.fori_loop(0, count // size, step, 0)
    d_ref[0, 0] = turn(dq[...], cos_ref[...], sin_ref[...], 0.125)


def attend_back(ends, query, keys, values, grad, mixed, logsum, cosine, sine):
    rows, count = query.shape
    heads = rows // HEAD_DIM
    whole = pl.BlockSpec((HEAD_DIM, count), lambda h, e: (h, 0))
    table = pl.BlockSpec((HALF, count), lambda h, e: (0, 0))
    out = pl.pallas_call(
        attend_back_kernel,
        grid_spec=pltpu.PrefetchScalarGridSpec(
            num_scalar_prefetch=1,
            grid=(heads,),
            in_specs=[whole] * 5
            + [pl.BlockSpec((1, 1, count), lambda h, e: (h, 0, 0)), table, table],
            out_specs=pl.BlockSpec((3, 1, HEAD_DIM, count), lambda h, e: (0, h, 0, 0)),
            scratch_shapes=[
                pltpu.VMEM((count, 128), BF),
                pltpu.VMEM((count, 128), BF),
                pltpu.VMEM((128, count), BF),
                pltpu.VMEM((128, count), BF),
                pltpu.VMEM((count, 128), BF),
                pltpu.VMEM((HEAD_DIM, count), F32),
            ],
        ),
        out_shape=jax.ShapeDtypeStruct((3, heads, HEAD_DIM, count), BF),
        compiler_params=params(),
        name="attend_back",
        cost_estimate=cost(10 * rows * count * count, 16 * rows * count),
    )(ends, query, keys, values, grad, mixed, logsum, cosine, sine)
    return out.reshape(3 * rows, count)


def turn_back(grad, c, s, factor):
    a, b = grad[:HALF], grad[HALF:]
    return (jnp.concatenate([a * c + b * s, b * c - a * s], 0) * factor).astype(BF)


def back_chunks(key_part, query_parts, half):
    edge = FIRST_MOST - half
    low = edge - 256
    found = []
    if key_part == 0:
        queries = []
        for p in query_parts:
            queries += [(p, 0, half if p == 0 else edge)]
        return [(0, half, 512, queries)]
    main = [(p, 0, half if p == 0 else edge) for p in query_parts]
    found.append((0, low, 512, main))
    found.append((low, 256, 256, [(p, 0, half) for p in query_parts]))
    if 1 in query_parts:
        found.append((edge, half - edge, 256, [(1, low, half - low)]))
    return found


def half_back_kernel(near_only, given_partial, finish, ends_ref, part_ref, *refs):
    refs = list(refs)
    sides = (0,) if near_only else (0, 1)
    given = {side: [refs.pop(0) for _ in range(8)] for side in sides}
    partial_in = refs.pop(0) if given_partial else None
    while len(refs) > (1 if near_only else 2) + 7:
        refs.pop(0)
    out_ref = None if near_only else refs.pop(0)
    near_ref = refs.pop(0)
    kaug, vaug, qaug, gaug, pair, dq, sums = refs
    rank = part_ref[0]
    half = given[0][0].shape[1]

    @pl.when(pl.program_id(0) == 0)
    def _():
        row = lax.broadcasted_iota(jnp.int32, (SEGS, half), 0)
        shift = jnp.where(row < 3, 1.0, 0.0)
        blank = zeros(HEAD_DIM, half)
        for side in sides:
            there = slice(side * half, side * half + half)
            same = local_segments(ends_ref, rank if side == 0 else 1 - rank, half)
            kaug[there, :] = (
                jnp.concatenate([blank, jnp.where(same, 0.0, -1e30), shift, zeros(32, half)], 0)
                .T.astype(BF)
            )
            vaug[there, :] = jnp.concatenate([blank, shift, zeros(48, half)], 0).T.astype(BF)
            qaug[HEAD_DIM:, there] = jnp.concatenate(
                [jnp.where(same, 1.0, 0.0), zeros(48, half)], 0
            ).astype(BF)
            gaug[HEAD_DIM:, there] = blank.astype(BF)

    for side in sides:
        q_ref, k_ref, v_ref, g_ref, o_ref, l_ref = given[side][:6]
        there = slice(side * half, side * half + half)
        g = g_ref[...]
        q = q_ref[...]
        delta = jnp.sum(g.astype(F32) * o_ref[...].astype(F32), axis=0, keepdims=True)
        kaug[there, :HEAD_DIM] = k_ref[...].T
        vaug[there, :HEAD_DIM] = v_ref[...].T
        qaug[:HEAD_DIM, there] = q
        qaug[HEAD_DIM + SEGS : HEAD_DIM + 2 * SEGS, there] = split3(-l_ref[0]).astype(BF)
        gaug[:HEAD_DIM, there] = g
        gaug[HEAD_DIM : HEAD_DIM + SEGS, there] = split3(-delta).astype(BF)
        pair[there, :] = jnp.concatenate([q, g], 0).T
    dq[...] = jnp.zeros_like(dq)
    if given_partial:
        dq[:, :half] = partial_in[0, 0]
        sums[...] = partial_in[1:, 0]
    else:
        sums[...] = jnp.zeros_like(sums)

    def chunk(side, k0, n, queries):
        where = pl.ds(side * half + k0, n)
        kb, vb, kt = kaug[where, :], vaug[where, :], given[side][1][:, pl.ds(k0, n)]
        dk = jnp.zeros((n, HEAD_DIM), F32)
        dv = jnp.zeros((n, HEAD_DIM), F32)
        for q0, width in queries:
            there = slice(q0, q0 + width)
            probs = jnp.exp2(dot(kb, qaug[:, there]))
            tilt = (probs * dot(vb, gaug[:, there])).astype(BF)
            dv = dv + dot(probs.astype(BF), pair[there, HEAD_DIM:])
            dk = dk + dot(tilt, pair[there, :HEAD_DIM])
            dq[:, there] += dot(kt, tilt)
        dk, dv = dk.T, dv.T
        if side == 0:
            sums[0, :, pl.ds(k0, n)] += dk
            sums[1, :, pl.ds(k0, n)] += dv
            return
        c, s = given[side][6][:, pl.ds(k0, n)], given[side][7][:, pl.ds(k0, n)]
        out_ref[1, 0, :, pl.ds(k0, n)] = turn_back(dk, c, s, LN2)
        out_ref[2, 0, :, pl.ds(k0, n)] = dv.astype(BF)

    for here in range(2):

        @pl.when(rank == here)
        def _():
            side_of = {here: 0, 1 - here: 1}
            for key_part, side in side_of.items():
                if near_only and side == 1:
                    continue
                if near_only:
                    query_parts = [here]
                else:
                    query_parts = [0, 1] if side == 1 else [1 - here]
                for k0, total, n, queries in back_chunks(key_part, query_parts, half):
                    spread = [(side_of[p] * half + q0, width) for p, q0, width in queries]
                    if total == n:
                        chunk(side, k0, n, spread)
                        continue

                    def step(i, carry):
                        chunk(side, pl.multiple_of(k0 + i * n, n), n, spread)
                        return carry

                    lax.fori_loop(0, total // n, step, 0)

    if not near_only:
        out_ref[0, 0] = turn_back(dq[:, half:], given[1][6][...], given[1][7][...], 0.125)
    if finish:
        c, s = given[0][6][...], given[0][7][...]
        near_ref[0, 0] = turn_back(dq[:, :half], c, s, 0.125)
        near_ref[1, 0] = turn_back(sums[0], c, s, LN2)
        near_ref[2, 0] = sums[1].astype(BF)
    else:
        near_ref[0, 0] = dq[:, :half]
        near_ref[1:, 0] = sums[...]


def half_back(name, ends, rank, sides, first, count, finish, partial=None, written=(), after=None):
    rows, half = sides[0][0].shape
    heads = rows // HEAD_DIM
    near_only = len(sides) == 1
    head = pl.BlockSpec((HEAD_DIM, half), lambda h, e, r: (h + first, 0))
    line = pl.BlockSpec((1, 1, half), lambda h, e, r: (h + first, 0, 0))
    table = pl.BlockSpec((HALF, half), lambda h, e, r: (0, 0))
    block = pl.BlockSpec((3, 1, HEAD_DIM, half), lambda h, e, r: (0, h + first, 0, 0))
    anywhere = pl.BlockSpec(memory_space=pl.ANY)
    operands, specs = [], []
    for side in sides:
        operands += list(side)
        specs += [head] * 5 + [line, table, table]
    result = jax.ShapeDtypeStruct((3, heads, HEAD_DIM, half), BF)
    if partial is not None:
        operands.append(partial)
        specs.append(block)
    aliases = {}
    for i, array in enumerate(written):
        if array is not None:
            aliases[2 + len(operands)] = i
            operands.append(array)
            specs.append(anywhere)
    if after is not None:
        operands.append(after)
        specs.append(anywhere)
    near_result = result if finish else jax.ShapeDtypeStruct(result.shape, F32)
    out_shape = [near_result] if near_only else [result, near_result]
    out_specs = [block] * len(out_shape)
    wide = half * len(sides)
    return pl.pallas_call(
        functools.partial(half_back_kernel, near_only, partial is not None, finish),
        grid_spec=pltpu.PrefetchScalarGridSpec(
            num_scalar_prefetch=2,
            grid=(count,),
            in_specs=specs,
            out_specs=out_specs,
            scratch_shapes=[
                pltpu.VMEM((wide, 128), BF),
                pltpu.VMEM((wide, 128), BF),
                pltpu.VMEM((128, wide), BF),
                pltpu.VMEM((128, wide), BF),
                pltpu.VMEM((wide, 128), BF),
                pltpu.VMEM((HEAD_DIM, wide), F32),
                pltpu.VMEM((2, HEAD_DIM, half), F32),
            ],
        ),
        out_shape=out_shape,
        input_output_aliases=aliases,
        compiler_params=params(),
        name=name,
        cost_estimate=cost(40 * count * HEAD_DIM * half * half * (1 if near_only else 3), 40 * count * HEAD_DIM * half),
    )(ends, rank, *operands)


def ffn_kernel(step, given, src_ref, dst_ref, n_ref, g_ref, up_ref, bias_ref, down_ref, *refs):
    branch_in, dn_in = refs[:2] if given else (None, None)
    branch_ref, dn_ref, dw_ref, dbias_ref, branch, dn, sems = refs[3 if given else 0 :]

    rows, depth = n_ref.shape
    steps = [(i, slice(r0, r0 + step)) for i, r0 in enumerate(range(0, rows, step))]
    opening = (pl.program_id(0) == 0) & (pl.program_id(1) == 0)
    closing = (pl.program_id(0) == pl.num_programs(0) - 1) & (
        pl.program_id(1) == pl.num_programs(1) - 1
    )

    def moves(i, part, out):
        if out:
            pairs = ((branch, branch_ref), (dn, dn_ref))
        else:
            pairs = ((branch_in, branch), (dn_in, dn))
        return [
            pltpu.make_async_copy(src.at[part, :], dst.at[part, :], sems.at[j, i])
            for j, (src, dst) in enumerate(pairs)
        ]

    @pl.when(opening)
    def _():
        if given:
            for i, part in steps:
                for move in moves(i, part, False):
                    move.start()
        else:
            branch[...] = jnp.zeros_like(branch)
            dn[...] = jnp.zeros_like(dn)

    up = up_ref[...].reshape(depth, -1)
    down, bias = down_ref[0, 0], bias_ref[0].astype(F32)
    width = up.shape[1]
    dup = jnp.zeros((width, depth), F32)
    ddown = jnp.zeros((width, depth), F32)
    dbias = jnp.zeros((1, width), F32)
    for i, part in steps:
        x, y = n_ref[part, :], g_ref[part, :]
        u = dot(x, up) + bias
        dz = dot_nt(y, down)
        normal = 0.5 * (1.0 + lax.erf(u * 0.7071067811865476))
        density = jnp.exp(-0.5 * u * u) * 0.3989422804014327
        z = (u * normal).astype(BF)
        du = (dz * (normal + u * density)).astype(BF)
        if given:

            @pl.when(opening)
            def _():
                for move in moves(i, part, False):
                    move.wait()

        branch[part, :] += dot(z, down)
        dn[part, :] += dot_nt(du, up)

        @pl.when(closing)
        def _():
            for move in moves(i, part, True):
                move.start()

        ddown = ddown + dot_tn(z, y)
        dup = dup + dot_tn(du, x)
        dbias = dbias + jnp.sum(du.astype(F32), axis=0, keepdims=True)
    dw_ref[0, 0, :width, :] = dup.astype(BF)
    dw_ref[0, 0, width:, :] = ddown.astype(BF)
    dbias_ref[0] = dbias

    @pl.when(closing)
    def _():
        for i, part in steps:
            for move in moves(i, part, True):
                move.wait()


def ffn_block(hidden):
    return min(512, hidden // 2)


def ffn(name, n2, grad, up, bias, down, extra, parts, src, dst, before=None):
    rows, depth = n2.shape
    hidden = up.shape[3]
    block = ffn_block(hidden)
    per = hidden // 2 // block
    step = min(512, rows)
    once = pl.BlockSpec(
        (rows, depth), lambda p, i, f, t: (0, 0), pipeline_mode=pl.Buffered(1)
    )
    anywhere = pl.BlockSpec(memory_space=pl.ANY)
    operands = [n2, grad, up, bias, down] + ([] if before is None else list(before))
    return pl.pallas_call(
        functools.partial(ffn_kernel, step, before is not None),
        grid_spec=pltpu.PrefetchScalarGridSpec(
            num_scalar_prefetch=2,
            grid=(src.shape[0], 2 * per),
            in_specs=[
                once,
                once,
                pl.BlockSpec((2, 1, depth // 2, block), lambda p, i, f, t: (0, f[p], 0, i)),
                pl.BlockSpec((1, 1, block), lambda p, i, f, t: (f[p], 0, i)),
                pl.BlockSpec(
                    (1, 1, block, depth), lambda p, i, f, t: (i // per, f[p], i % per, 0)
                ),
            ]
            + ([] if before is None else [anywhere] * 3),
            out_specs=[anywhere] * 2
            + [
                pl.BlockSpec(
                    (1, 1, 2 * block, depth), lambda p, i, f, t: (i // per, t[p], i % per, 0)
                ),
                pl.BlockSpec((1, 1, block), lambda p, i, f, t: (p, 0, i)),
            ],
            scratch_shapes=[pltpu.VMEM((rows, depth), F32)] * 2
            + [pltpu.SemaphoreType.DMA((2, rows // step))],
        ),
        out_shape=[jax.ShapeDtypeStruct((rows, depth), F32)] * 2
        + [
            jax.ShapeDtypeStruct((2, parts, hidden + extra, depth), BF),
            jax.ShapeDtypeStruct((src.shape[0], 1, hidden), F32),
        ],
        input_output_aliases={} if before is None else {9: 2},
        compiler_params=params(),
        name=name,
        cost_estimate=cost(12 * rows * depth * hidden * src.shape[0], 8 * depth * hidden * src.shape[0]),
    )(src, dst, *operands)


def out_back_kernel(part_ref, near_ref, in_ref, grad_ref, sums_ref, out_ref):
    for side, mixed_ref in enumerate((near_ref, in_ref)):

        @pl.when(pl.program_id(0) == side)
        def _():
            out_ref[0, 0] = dot(mixed_ref[...], grad_ref[...]).astype(BF)


def out_back(mixed, grad, sums, extra, parts):
    heads, rows = mixed[0].shape
    total, depth = sums.shape[2:]
    piece = pl.BlockSpec((extra, rows), lambda p, c, t: (c, 0))
    return pl.pallas_call(
        out_back_kernel,
        grid_spec=pltpu.PrefetchScalarGridSpec(
            num_scalar_prefetch=1,
            grid=(2, 2),
            in_specs=[
                piece,
                piece,
                pl.BlockSpec((rows, depth), lambda p, c, t: (0, 0)),
                pl.BlockSpec(memory_space=pl.ANY),
            ],
            out_specs=pl.BlockSpec(
                (1, 1, extra, depth), lambda p, c, t: (c, t[p], total // extra - 1, 0)
            ),
        ),
        out_shape=jax.ShapeDtypeStruct(sums.shape, BF),
        input_output_aliases={4: 0},
        compiler_params=params(),
        name="out_back",
        cost_estimate=cost(4 * rows * depth * heads, 4 * heads * depth),
    )(parts, *mixed, grad, sums)


def project_back_kernel(*refs):
    out_ref = refs[-2]
    pairs = refs[:-3]
    total = dot(pairs[1][...], pairs[0][...])
    for i in range(2, len(pairs), 2):
        total = total + dot(pairs[i + 1][...], pairs[i][...])
    out_ref[...] = total.astype(BF)


def project_back(pairs, passed):
    total = pairs[0][1].shape[0]
    depth = pairs[0][0].shape[1]
    block = total // 3
    specs, operands = [], []
    for x, grad, at in pairs:
        specs += [
            pl.BlockSpec(x.shape, lambda i: (0, 0)),
            pl.BlockSpec((block, x.shape[0]), functools.partial(lambda at, i: (i, at), at)),
        ]
        operands += [x, grad]
    return pl.pallas_call(
        project_back_kernel,
        grid=(3,),
        in_specs=specs + [pl.BlockSpec(memory_space=pl.ANY)],
        out_specs=[
            pl.BlockSpec((block, depth), lambda i: (i, 0)),
            pl.BlockSpec(memory_space=pl.ANY),
        ],
        out_shape=[
            jax.ShapeDtypeStruct((total, depth), BF),
            jax.ShapeDtypeStruct(passed.shape, passed.dtype),
        ],
        input_output_aliases={len(operands): 1},
        compiler_params=params(),
        name="project_back",
        cost_estimate=cost(4 * pairs[0][0].shape[0] * depth * total, 8 * depth * total),
    )(*operands, passed)


def turn_kernel(x_ref, *out_refs):
    for i, out_ref in enumerate(out_refs):

        @pl.when(pl.program_id(0) == i)
        def _():
            out_ref[...] = x_ref[...].astype(F32).T


def turn(x, parts):
    rows, depth = x.shape
    block = rows // parts
    return pl.pallas_call(
        turn_kernel,
        grid=(parts,),
        in_specs=[pl.BlockSpec((block, depth), lambda i: (i, 0))],
        out_specs=[pl.BlockSpec((depth, block), lambda i: (0, 0))] * parts,
        out_shape=[jax.ShapeDtypeStruct((depth, block), F32)] * parts,
        compiler_params=params(),
        name="turn",
        cost_estimate=cost(rows * depth, 6 * rows * depth),
    )(x)


MESH = pl.DeviceIdType.MESH


def sum_all_kernel(
    big_ref, small_ref, out_ref, small_out_ref,
    buf, done, core_in, first_in, second_in, z_in, small, small_in, small_z,
    local, send, recv, small_send, small_recv,
):
    o, c, m = lax.axis_index("dpo"), lax.axis_index("core"), lax.axis_index("mp")
    y, z = lax.rem(o, 2), lax.div(o, 2)
    zs = 4
    size = buf.shape[0] // 2
    half, quarter, eighth, last = size // 2, size // 4, size // 8, size // 32
    sibling = (o, 1 - c, m)
    across = (o, c, 1 - m)
    beside = (z * 2 + 1 - y, c, m)
    others = [lax.rem(z + d, zs) for d in range(1, zs)]

    def along(j):
        return (j * 2 + y, c, m)

    load = pltpu.make_async_copy(big_ref, buf, local.at[0])
    load.start()
    barrier = pltpu.get_barrier_semaphore()
    for device in [sibling, across, beside] + [along(j) for j in others]:
        pl.semaphore_signal(barrier, inc=1, device_id=device, device_id_type=MESH)
    pl.semaphore_wait(barrier, 6)
    small[0] = small_ref[...]

    main, tiny = (send, recv), (small_send, small_recv)
    started = []

    def copy(src, dst, sems, i, device):
        return pltpu.make_async_remote_copy(
            src_ref=src, dst_ref=dst, send_sem=sems[0].at[i], recv_sem=sems[1].at[i],
            device_id=device, device_id_type=MESH,
        )

    def go(src, dst, sems, i, device):
        one = copy(src, dst, sems, i, device)
        one.start()
        started.append(one)
        return one

    def rows(first, n, of=buf):
        return of.at[pl.ds(pl.multiple_of(first, last), n)]

    def add(first, n, got):
        def one(i, carry):
            there = pl.ds(pl.multiple_of(first + i * 128, last), 128)
            here = pl.ds(pl.multiple_of(i * 128, 128), 128)
            buf[there, :] = (buf[there, :].astype(F32) + got[here, :].astype(F32)).astype(BF)
            return carry

        lax.fori_loop(0, n // 128, one, 0)

    turn_of = ((m, y), (y, m))
    device_of = ((across, beside), (beside, across))
    far, near, far_next, near_next, own, theirs = [], [], [], [], [], []
    for s in range(2):
        a, b = turn_of[s]
        mine = s * size + c * half
        theirs.append(s * size + (1 - c) * half)
        far.append(mine + (1 - a) * quarter)
        near.append(mine + a * quarter)
        far_next.append(near[s] + (1 - b) * eighth)
        near_next.append(near[s] + b * eighth)
        own.append(near_next[s] + z * last)

    load.wait()
    arrivals = []
    for part in range(2):
        for s in range(2):
            a = turn_of[s][0]
            start = theirs[s] + ((1 - a) if part == 0 else a) * quarter
            i = 2 * part + s
            arrivals.append(go(rows(start, quarter), core_in.at[i], main, i, sibling))
    tiny_core = go(small.at[0], small_in.at[0], tiny, 0, sibling)
    firsts = []
    for s in range(2):
        arrivals[s].wait_recv()
        add(far[s], quarter, core_in.at[s])
        firsts.append(go(rows(far[s], quarter), first_in.at[s], main, 4 + s, device_of[s][0]))
    tiny_core.wait_recv()
    small[1] = small[0] + small_in[0]
    tiny_x = go(small.at[1], small_in.at[1], tiny, 1, across)
    for s in range(2):
        arrivals[2 + s].wait_recv()
        add(near[s], quarter, core_in.at[2 + s])
    tiny_x.wait_recv()
    small[2] = small[1] + small_in[1]
    tiny_y = go(small.at[2], small_in.at[2], tiny, 2, beside)
    seconds = []
    for s in range(2):
        firsts[s].wait_recv()
        add(near[s], quarter, first_in.at[s])
        seconds.append(go(rows(far_next[s], eighth), second_in.at[s], main, 6 + s, device_of[s][1]))
    tiny_y.wait_recv()
    small_z[z] = small[2] + small_in[2]
    for j in others:
        go(small_z.at[z], small_z.at[z], tiny, 3 + z, along(j))
    for s in range(2):
        seconds[s].wait_recv()
        add(near_next[s], eighth, second_in.at[s])
        for j in others:
            go(
                rows(near_next[s] + j * last, last), z_in.at[s, z], main, 8 + 4 * s + z, along(j)
            )

    def hand(first, n, i, device):
        there = rows(first, n, done)
        return go(there, there, main, i, device)

    for s in range(2):
        total = buf[pl.ds(pl.multiple_of(own[s], last), last), :].astype(F32)
        for j in others:
            copy(z_in.at[s, j], z_in.at[s, j], main, 8 + 4 * s + j, along(j)).wait_recv()
            total = total + z_in[s, j].astype(F32)
        done[pl.ds(pl.multiple_of(own[s], last), last), :] = total.astype(BF)
        for j in others:
            hand(own[s], last, 16 + 4 * s + z, along(j))
    back_second, back_first, cores = [], [], []
    for s in range(2):
        for j in others:
            there = rows(near_next[s] + j * last, last, done)
            copy(there, there, main, 16 + 4 * s + j, along(j)).wait_recv()
        back_second.append(hand(near_next[s], eighth, 24 + s, device_of[s][1]))
        back_first.append(hand(near_next[s], eighth, 26 + s, device_of[s][0]))
        cores.append(hand(near_next[s], eighth, 28 + s, sibling))
    back_more = []
    for s in range(2):
        back_second[s].wait_recv()
        back_more.append(hand(far_next[s], eighth, 30 + s, device_of[s][0]))
        cores.append(hand(far_next[s], eighth, 32 + s, sibling))
    for j in others:
        copy(small_z.at[j], small_z.at[j], tiny, 3 + j, along(j)).wait_recv()
    small_out_ref[...] = (small_z[0] + small_z[1]) + (small_z[2] + small_z[3])
    for s in range(2):
        back_first[s].wait_recv()
        cores.append(hand(far[s] + turn_of[s][1] * eighth, eighth, 34 + s, sibling))
    for s in range(2):
        back_more[s].wait_recv()
        cores.append(hand(far[s] + (1 - turn_of[s][1]) * eighth, eighth, 36 + s, sibling))
    for one in cores:
        one.wait_recv()
    store = pltpu.make_async_copy(done, out_ref, local.at[1])
    store.start()
    for one in started:
        one.wait_send()
    store.wait()


def sum_all(big, small):
    rows, width = big.shape
    quarter, eighth, last = rows // 8, rows // 16, rows // 64
    anywhere = pl.BlockSpec(memory_space=pl.ANY)
    whole = pl.BlockSpec(memory_space=pltpu.VMEM)
    dma = pltpu.SemaphoreType.DMA
    return pl.pallas_call(
        sum_all_kernel,
        in_specs=[anywhere, whole],
        out_specs=[anywhere, whole],
        out_shape=[
            jax.ShapeDtypeStruct(big.shape, BF),
            jax.ShapeDtypeStruct(small.shape, F32),
        ],
        scratch_shapes=[
            pltpu.VMEM((rows, width), BF),
            pltpu.VMEM((rows, width), BF),
            pltpu.VMEM((4, quarter, width), BF),
            pltpu.VMEM((2, quarter, width), BF),
            pltpu.VMEM((2, eighth, width), BF),
            pltpu.VMEM((2, 4, last, width), BF),
            pltpu.VMEM((3,) + small.shape, F32),
            pltpu.VMEM((3,) + small.shape, F32),
            pltpu.VMEM((4,) + small.shape, F32),
            dma((2,)),
            dma((38,)),
            dma((38,)),
            dma((7,)),
            dma((7,)),
        ],
        compiler_params=pltpu.CompilerParams(
            collective_id=0, has_side_effects=True, vmem_limit_bytes=VMEM
        ),
        name="sum_all",
        cost_estimate=cost(rows * width, 8 * rows * width),
    )(big, small)


def join_back_kernel(grad_ref, w_ref, first_ref, second_ref):
    grad = grad_ref[...]
    width = first_ref.shape[1]
    first_ref[...] = dot_nt(grad, w_ref[:width, :])
    second_ref[...] = dot_nt(grad, w_ref[width:, :])


def join_back(grad, w):
    rows, depth = grad.shape
    width = w.shape[0] // 2
    block = min(512, rows)
    out = pl.BlockSpec((block, width), lambda i: (i, 0))
    return pl.pallas_call(
        join_back_kernel,
        grid=(rows // block,),
        in_specs=[
            pl.BlockSpec((block, depth), lambda i: (i, 0)),
            pl.BlockSpec(w.shape, lambda i: (0, 0)),
        ],
        out_specs=[out, out],
        out_shape=[jax.ShapeDtypeStruct((rows, width), F32)] * 2,
        compiler_params=params(),
        name="join_back",
        cost_estimate=cost(rows * depth * width, 8 * rows * width),
    )(grad, w)


def concat_back_kernel(x_ref, s_ref, grad_ref, out_ref):
    for i, ref in enumerate((x_ref, s_ref)):

        @pl.when(pl.program_id(0) == i)
        def _():
            out_ref[...] = dot_tn(ref[...], grad_ref[...]).astype(BF)


def concat_back(x, skip, grad):
    rows, width = grad.shape
    block = min(512, width)
    per = width // block
    return pl.pallas_call(
        concat_back_kernel,
        grid=(2, per),
        in_specs=[
            pl.BlockSpec((rows, block), lambda i, j: (0, jnp.where(i == 0, j, per - 1))),
            pl.BlockSpec((rows, block), lambda i, j: (0, jnp.where(i == 0, 0, j))),
            pl.BlockSpec((rows, width), lambda i, j: (0, 0)),
        ],
        out_specs=pl.BlockSpec((block, width), lambda i, j: (i * per + j, 0)),
        out_shape=jax.ShapeDtypeStruct((2 * width, width), BF),
        compiler_params=params(),
        name="concat_back",
        cost_estimate=cost(4 * rows * width * width, 8 * rows * width),
    )(x, skip, grad)


def unpack_kernel(core_ref, own_ref, sibling_ref, up_ref, down_ref):
    mine = core_ref[0] == pl.program_id(0)
    width = down_ref.shape[0]
    block = jnp.where(mine, own_ref[...].astype(F32), sibling_ref[...].astype(F32))
    up_ref[...] = block[:width].T
    down_ref[...] = block[width:]


def unpack(core, own, sibling, hidden):
    depth = own.shape[1]
    block = ffn_block(hidden)
    per = hidden // 2 // block
    piece = pl.BlockSpec((2 * block, depth), lambda c, i, k: (i, 0))
    return pl.pallas_call(
        unpack_kernel,
        grid_spec=pltpu.PrefetchScalarGridSpec(
            num_scalar_prefetch=1,
            grid=(2, per),
            in_specs=[piece, piece],
            out_specs=[
                pl.BlockSpec((depth, block), lambda c, i, k: (0, c * per + i)),
                pl.BlockSpec((block, depth), lambda c, i, k: (c * per + i, 0)),
            ],
        ),
        out_shape=[
            jax.ShapeDtypeStruct((depth, hidden), F32),
            jax.ShapeDtypeStruct((hidden, depth), F32),
        ],
        compiler_params=params(),
        name="unpack",
        cost_estimate=cost(depth * hidden, 12 * depth * hidden),
    )(core, own, sibling)


def body(
    inputs, skip_in, cotangent, lengths, w_concat, b_concat, gain_attn, w_query, w_key, w_value,
    w_out, b_out, gain_ffn, w_up, b_up, w_down, b_down,
):
    parts = lax.axis_size("mp")
    rank = lax.axis_index("mp")
    core = lax.axis_index("core")
    dp = ("dpo", "core")
    rows, width = inputs.shape
    group = rows * parts
    paired = parts == 2 and group == 4096
    ends, pos_all, valid_all = layout(lengths[0], group)
    valid_here = lax.dynamic_slice_in_dim(valid_all, rank * rows, rows, 0)[:, None]
    each, hidden = w_out.shape[0], b_up.shape[0]
    extra = each // 2
    index = rank.reshape(1)
    other = 1 - index
    zero = jnp.zeros((1,), jnp.int32)

    def across(x):
        return lax.ppermute(x, "mp", [(0, 1), (1, 0)])

    def piece(x, i, size, axis=0):
        return lax.dynamic_slice_in_dim(x, i * size, size, axis)

    def order(near, far, axis):
        return jnp.where(
            rank == 0, jnp.concatenate([near, far], axis), jnp.concatenate([far, near], axis)
        )

    def core_half(w):
        return piece(w, core, w.shape[0] // 2)

    def gather(half):
        return lax.all_gather(half, ("core", "mp"), axis=0).reshape((2, parts) + half.shape)

    w_turned = jnp.concatenate([w_query.T, w_key.T, w_value.T], axis=0)
    grad_rows = cotangent.astype(F32) * valid_here
    grad_low = grad_rows.astype(BF)
    half_up, half_down = core_half(w_up), core_half(w_down)
    if paired:
        bias_far, out_piece = across(b_up), across(core_half(w_out))
        h0, n1 = enter(inputs, skip_in, w_concat, b_concat, gain_attn, 0, rows)
        n1, bias_far, out_piece = lax.optimization_barrier((n1, bias_far, out_piece))
        n1_far = across(n1)
        out_rest = lax.ppermute(out_piece, "core", [(0, 1), (1, 0)])
        out_far = jnp.where(
            core == 0,
            jnp.concatenate([out_piece, out_rest]),
            jnp.concatenate([out_rest, out_piece]),
        )
        tables_near = tables(piece(pos_all, rank, rows))
        q_near, k_near, v_near = project(n1, w_turned, *tables_near, after=(out_far,))
        start = attend_half(
            "near_near", ends, index, q_near, False, {0: (k_near, v_near)}, last=False
        )
        tables_far = tables(piece(pos_all, 1 - rank, rows))
        n1_far, start, half_up, half_down = lax.optimization_barrier(
            (n1_far, start, half_up, half_down)
        )
        up_all, down_all = gather(half_up), gather(half_down)
        q_far, k_far, v_far = project(n1_far, w_turned, *tables_far)
        mixed_far, log_far = attend_half(
            "far_all", ends, index, q_far, True, {0: (k_near, v_near), 1: (k_far, v_far)}
        )
        mixed_in = across(mixed_far)
        mixed_near, log_near = attend_half(
            "near_far", ends, index, q_near, False, {1: (k_far, v_far)}, carry=start
        )
        h1, n2 = upper(h0, mixed_near, mixed_in, w_out, out_far, b_out, gain_ffn)
        branch, grad_n2, sums, bias_near = ffn(
            "ffn_near", n2, grad_low, w_up.reshape(2, 1, width // 2, hidden),
            b_up.reshape(1, 1, hidden), w_down.reshape(2, 1, hidden // 2, width),
            extra, parts, zero, index,
        )
        both = jnp.stack([bias_far, bias_far]).reshape(2, 1, hidden)
        branch, grad_n2, sums, grad_bias = ffn(
            "ffn_far", n2, grad_low, up_all, both, down_all, extra, parts, other, other,
            before=(branch, grad_n2, sums),
        )
        grad_bias = order(bias_near, grad_bias, 0)
        output, grad_h1, grad_h1_low, grad_near, grad_sent, early = middle(
            h1, branch, grad_n2, cotangent, valid_here, b_down, gain_ffn, w_out, out_far
        )
        grad_far = across(grad_sent)
        sums = out_back(
            (mixed_near, mixed_in), grad_h1_low, sums, extra, jnp.concatenate([index, other])
        )
    else:
        joined = jnp.concatenate([inputs, skip_in], axis=1)
        h0 = dot(joined, w_concat) + b_concat
        scale_one = lax.rsqrt(jnp.mean(h0 * h0, axis=-1, keepdims=True) + EPS)
        n1 = (h0 * scale_one * gain_attn).astype(BF)
        n1_all = lax.all_gather(n1, "mp", axis=0, tiled=True)
        bias_all = lax.all_gather(b_up, "mp", axis=0).reshape(parts, 1, -1)
        w_out_all = lax.all_gather(w_out, "mp", axis=0, tiled=True)
        up_all, down_all = gather(half_up), gather(half_down)
        cosine, sine = tables(pos_all)
        query, keys, values = project(n1_all, w_turned, cosine, sine)
        mixed, logsum = attend(ends, zero, query, keys, values, 1)
        mixed_rows = lax.all_to_all(mixed, "mp", 1, 0, tiled=True)
        h1 = h0 + dot_tn(mixed_rows, w_out_all) + b_out
        scale_two = lax.rsqrt(jnp.mean(h1 * h1, axis=-1, keepdims=True) + EPS)
        n2 = (h1 * scale_two * gain_ffn).astype(BF)
        every = jnp.arange(parts, dtype=jnp.int32)
        branch, grad_n2, sums, grad_bias = ffn(
            "ffn", n2, grad_low, up_all, bias_all, down_all, extra, parts, every, every
        )
        output = valid_here * (h1 + branch + b_down)
        grad_h1, grad_gain_ffn = norm_back(grad_n2, h1, scale_two, gain_ffn)
        grad_h1 = grad_h1 + grad_rows
        grad_h1_low = grad_h1.astype(BF)
        grad_mixed = lax.all_to_all(
            dot_nt(w_out_all, grad_h1_low).astype(BF), "mp", 0, 1, tiled=True
        )
        grad_out = dot(mixed_rows, grad_h1_low).astype(BF)
        grad_out = grad_out.reshape(parts, 2, extra, width).transpose(1, 0, 2, 3)
        sums = lax.dynamic_update_slice(sums, grad_out, (0, 0, hidden, 0))
        early = jnp.stack([jnp.sum(grad_rows, 0), grad_gain_ffn, jnp.sum(grad_h1, 0)])
    def unpack_all(own):
        sibling = lax.ppermute(own, "core", [(0, 1), (1, 0)])
        up, down = unpack(core.reshape(1), own, sibling, hidden)
        first, second = own[hidden:].astype(F32), sibling[hidden:].astype(F32)
        out = jnp.where(
            core == 0, jnp.concatenate([first, second]), jnp.concatenate([second, first])
        )
        return up, down, out

    part = lax.psum_scatter(
        sums.reshape((2 * parts,) + sums.shape[2:]), ("core", "mp"), scatter_dimension=0, tiled=True
    )[0]
    summed = lax.psum(part, "dpo")
    if paired:
        near = (q_near, k_near, v_near, grad_near, mixed_near, log_near) + tables_near
        far = (q_far, k_far, v_far, grad_far, mixed_far, log_far) + tables_far
        heads = each // HEAD_DIM
        back = functools.partial(half_back, ends=ends, rank=index)
        both = (near, far)
        middle_head = heads // 2
        opening = back("back_near0", sides=(near,), first=0, count=middle_head, finish=False)[0]
        written, at = (), 0
        quarter = middle_head // 4
        for i, count in enumerate((2 * quarter, quarter, middle_head - 3 * quarter)):
            written = back(
                f"back_first{i}", sides=both, first=at, count=count, finish=True,
                partial=opening, written=written, after=part if i == 2 else None,
            )
            at += count
        back_far, back_near = written
        partial = None
        for i in range(2):
            back_far, partial = back(
                f"back_second{i}", sides=both, first=at, count=middle_head // 2, finish=False,
                written=(back_far, partial),
            )
            at += middle_head // 2
        back_far = back_far.reshape(3 * each, rows)
        grad_far_rows = dot_tn(back_far, w_turned).astype(BF)
        sent = across(grad_far_rows)
        back_near = back(
            "back_near1", sides=(near,), first=middle_head, count=heads - middle_head, finish=True,
            partial=partial, written=(back_near,), after=grad_far_rows,
        )[0].reshape(3 * each, rows)
        pairs = [(n1, back_near, 0), (n1_far, back_far, 0)]
        grad_qkv, summed = project_back(pairs, summed)
        grad_h0_low, late = leave(
            back_near, w_turned, sent, h0, grad_h1, gain_attn, (grad_qkv,)
        )
    else:
        back = attend_back(ends, query, keys, values, grad_mixed, mixed, logsum, cosine, sine)
        grad_n1 = dot_tn(back, w_turned).astype(BF)
        grad_n1 = lax.psum_scatter(grad_n1, "mp", scatter_dimension=0, tiled=True).astype(F32)
        grad_qkv, summed = project_back([(n1_all, back, 0)], summed)
        grad_h0, grad_gain_attn = norm_back(grad_n1, h0, scale_one, gain_attn)
        grad_h0_low = (grad_h0 + grad_h1).astype(BF)
        late = jnp.stack([jnp.sum(grad_h0_low.astype(F32), axis=0), grad_gain_attn])
    grad_up, grad_down, grad_out = unpack_all(summed)
    grad_w_concat = concat_back(inputs, skip_in, grad_h0_low)
    small = jnp.concatenate([early, late, grad_bias.reshape(-1, width)])
    small = jnp.pad(small, ((0, -small.shape[0] % 8), (0, 0)))
    if paired and lax.axis_size("dpo") == 8:
        tail, small = sum_all(grad_w_concat, small)
        grad_qkv = lax.psum(grad_qkv, dp)
    else:
        tail, small = lax.psum((grad_w_concat, small), dp + ("mp",))
        grad_qkv = lax.psum(grad_qkv, dp)
    grad_inputs, grad_skip = join_back(grad_h0_low, w_concat)
    grad_query, grad_key, grad_value = turn(grad_qkv, 3)
    return (
        output,
        grad_inputs,
        grad_skip,
        tail.astype(F32),
        small[3],
        small[4],
        grad_query,
        grad_key,
        grad_value,
        grad_out,
        small[2],
        small[1],
        grad_up,
        piece(small[5 : 5 + parts * hidden // width].reshape(-1), rank, hidden),
        grad_down,
        small[0],
    )


def solution(mesh):
    dp, mp = mesh.shape["dp"], mesh.shape["mp"]
    mesh = Mesh(mesh.devices.reshape(dp // 2, 2, mp), ("dpo", "core", "mp"))
    rows = P(("dpo", "core", "mp"), None)
    columns = P(None, "mp")
    upright = P("mp", None)
    return jax.shard_map(
        body,
        mesh=mesh,
        in_specs=(
            rows, rows, rows, P(("dpo", "core"), None), P(), P(), P(), columns, columns, columns,
            upright, P(), P(), columns, P("mp"), upright, P(),
        ),
        out_specs=(
            rows, rows, rows, P(), P(), P(), columns, columns, columns,
            upright, P(), P(), columns, P("mp"), upright, P(),
        ),
        check_vma=False,
    )
```

```python
import functools

import jax
import jax.numpy as jnp
from jax import lax
from jax.experimental import pallas as pl
from jax.experimental.pallas import tpu as pltpu
from jax.sharding import Mesh
from jax.sharding import PartitionSpec as P

HEAD_DIM = 64
HALF = HEAD_DIM // 2
EPS = 1e-06
FIRST_LEAST = 3712
FIRST_MOST = 3840
SEGS = 16
LOG2E = 1.4426950408889634
LN2 = 0.6931471805599453
VMEM = 60 * 2**20

BF = jnp.bfloat16
F32 = jnp.float32


def dot(left, right, dims=((1,), (0,))):
    return lax.dot_general(left, right, (dims, ((), ())), preferred_element_type=F32)


def dot_tn(left, right):
    return dot(left, right, ((0,), (0,)))


def dot_nt(left, right):
    return dot(left, right, ((1,), (1,)))


def layout(lengths_row, count):
    ends = jnp.cumsum(lengths_row)
    starts = ends - lengths_row
    places = jnp.arange(count, dtype=jnp.int32)
    seg = jnp.sum((places[:, None] >= ends[None, :]).astype(jnp.int32), axis=1)
    owner = seg[:, None] == jnp.arange(lengths_row.shape[0], dtype=jnp.int32)[None, :]
    start_of = jnp.sum(jnp.where(owner, starts[None, :], 0), axis=1)
    pos = (places - start_of).astype(F32)
    valid = (places < ends[-1]).astype(F32)
    return (ends.astype(jnp.int32), pos, valid)


def tables(pos):
    freq = jnp.exp(-jnp.log(10000.0) * jnp.arange(HALF, dtype=F32) * 2.0 / HEAD_DIM)
    angle = freq[:, None] * pos[None, :]
    return (jnp.cos(angle), jnp.sin(angle))


def norm_back(grad, stream, scale, gain):
    tilted = grad * gain
    grad_gain = jnp.sum(grad * stream * scale, axis=0)
    grad_stream = scale * tilted - stream * scale**3 * jnp.mean(
        tilted * stream, axis=-1, keepdims=True
    )
    return (grad_stream, grad_gain)


def params():
    return pltpu.CompilerParams(vmem_limit_bytes=VMEM)


def cost(flops, moved):
    return pl.CostEstimate(flops=flops // 64, bytes_accessed=moved // 64, transcendentals=0)


def project_kernel(x_ref, w_ref, cos_ref, sin_ref, *refs):
    q_ref, k_ref, v_ref = refs[-3:]
    x = x_ref[...]
    c, s = cos_ref[...], sin_ref[...]
    width = q_ref.shape[0]
    for out, first, factor in ((q_ref, 0, 0.125 * LOG2E), (k_ref, width, 1.0)):
        t = dot_nt(w_ref[first : first + width, :], x)
        for h in range(0, width, HEAD_DIM):
            a, b = t[h : h + HALF], t[h + HALF : h + HEAD_DIM]
            out[h : h + HALF, :] = ((a * c - b * s) * factor).astype(BF)
            out[h + HALF : h + HEAD_DIM, :] = ((b * c + a * s) * factor).astype(BF)
    v_ref[...] = dot_nt(w_ref[2 * width :, :], x).astype(BF)


def project(x, w, cosine, sine, after=()):
    count, depth = x.shape
    width = w.shape[0] // 3
    block = min(512, count)
    table = pl.BlockSpec((HALF, block), lambda i: (0, i))
    out = pl.BlockSpec((width, block), lambda i: (0, i))
    return pl.pallas_call(
        project_kernel,
        grid=(count // block,),
        in_specs=[
            pl.BlockSpec((block, depth), lambda i: (i, 0)),
            pl.BlockSpec(w.shape, lambda i: (0, 0)),
            table,
            table,
        ]
        + [pl.BlockSpec(memory_space=pl.ANY)] * len(after),
        out_specs=[out] * 3,
        out_shape=[jax.ShapeDtypeStruct((width, count), BF)] * 3,
        compiler_params=params(),
        name="project",
    )(x, w, cosine, sine, *after)


def scale_of(stream):
    return lax.rsqrt(jnp.mean(stream * stream, axis=-1, keepdims=True) + EPS)


def norm_back_rows(grad, stream, gain):
    scale = scale_of(stream)
    tilted = grad * gain
    back = scale * tilted - stream * (scale * scale * scale) * jnp.mean(
        tilted * stream, axis=-1, keepdims=True
    )
    return back, jnp.sum(grad * stream * scale, axis=0, keepdims=True)


def add_up(ref, terms):
    for i, term in enumerate(terms):

        @pl.when(pl.program_id(0) == 0)
        def _():
            ref[i : i + 1, :] = term

        @pl.when(pl.program_id(0) > 0)
        def _():
            ref[i : i + 1, :] += term


def row_specs(rows, width, block, first=0):
    def tall(columns=width):
        return pl.BlockSpec((block, columns), lambda i: (i + first, 0))

    def whole(*shape):
        return pl.BlockSpec(shape, lambda i: (0, 0))

    return tall, whole


def enter_kernel(x_ref, s_ref, w_ref, b_ref, gain_ref, *refs):
    h_ref, n_ref = refs[-2:]
    width = x_ref.shape[1]
    h = dot(x_ref[...], w_ref[:width, :]) + dot(s_ref[...], w_ref[width:, :]) + b_ref[...]
    h_ref[...] = h
    n_ref[...] = (h * scale_of(h) * gain_ref[...]).astype(BF)


def enter(x, skip, w, bias, gain, first, count, written=()):
    rows, width = x.shape
    block = min(512, count)
    tall, whole = row_specs(rows, width, block, first // block)
    return pl.pallas_call(
        enter_kernel,
        grid=(count // block,),
        in_specs=[tall(), tall(), whole(*w.shape), whole(1, width), whole(1, width)]
        + [pl.BlockSpec(memory_space=pl.ANY)] * len(written),
        out_specs=[tall(), tall()],
        out_shape=[jax.ShapeDtypeStruct((rows, width), F32), jax.ShapeDtypeStruct((rows, width), BF)],
        input_output_aliases={5 + i: i for i in range(len(written))},
        compiler_params=params(),
        name="enter",
        cost_estimate=cost(4 * count * width * width, 10 * count * width),
    )(x, skip, w, bias[None], gain[None], *written)


def upper_kernel(h_ref, near_ref, in_ref, own_ref, far_ref, b_ref, gain_ref, h1_ref, n_ref):
    h = h_ref[...] + dot_tn(near_ref[...], own_ref[...]) + dot_tn(in_ref[...], far_ref[...])
    h = h + b_ref[...]
    h1_ref[...] = h
    n_ref[...] = (h * scale_of(h) * gain_ref[...]).astype(BF)


def upper(h0, near, arrived, own, far, bias, gain):
    rows, width = h0.shape
    block = min(512, rows)
    tall, whole = row_specs(rows, width, block)
    flat = pl.BlockSpec((near.shape[0], block), lambda i: (0, i))
    return pl.pallas_call(
        upper_kernel,
        grid=(rows // block,),
        in_specs=[
            tall(), flat, flat, whole(*own.shape), whole(*far.shape), whole(1, width), whole(1, width)
        ],
        out_specs=[tall(), tall()],
        out_shape=[jax.ShapeDtypeStruct((rows, width), F32), jax.ShapeDtypeStruct((rows, width), BF)],
        compiler_params=params(),
        name="upper",
        cost_estimate=cost(2 * rows * width * width, 12 * rows * width),
    )(h0, near, arrived, own, far, bias[None], gain[None])


def middle_kernel(
    h_ref, dn_ref, g_ref, valid_ref, gain_ref, own_ref, far_ref,
    dh_ref, low_ref, near_ref, sent_ref, sums_ref,
):
    valid = valid_ref[...]
    h = h_ref[...]
    g = g_ref[...].astype(F32) * valid
    back, gain_sum = norm_back_rows(dn_ref[...], h, gain_ref[...])
    dh = g + back
    dh_ref[...] = dh
    low = dh.astype(BF)
    low_ref[...] = low
    near_ref[...] = dot_nt(own_ref[...], low).astype(BF)
    sent_ref[...] = dot_nt(far_ref[...], low).astype(BF)
    add_up(
        sums_ref,
        [jnp.sum(g, 0, keepdims=True), gain_sum, jnp.sum(dh, 0, keepdims=True)],
    )


def middle(h1, dn, cotangent, valid, gain, own, far):
    rows, width = h1.shape
    block = min(512, rows)
    tall, whole = row_specs(rows, width, block)
    flat = pl.BlockSpec((own.shape[0], block), lambda i: (0, i))
    return pl.pallas_call(
        middle_kernel,
        grid=(rows // block,),
        in_specs=[tall(), tall(), tall(), tall(1), whole(1, width)] + [whole(*own.shape)] * 2,
        out_specs=[tall(), tall(), flat, flat, whole(3, width)],
        out_shape=[
            jax.ShapeDtypeStruct((rows, width), F32),
            jax.ShapeDtypeStruct((rows, width), BF),
            jax.ShapeDtypeStruct((own.shape[0], rows), BF),
            jax.ShapeDtypeStruct((own.shape[0], rows), BF),
            jax.ShapeDtypeStruct((3, width), F32),
        ],
        compiler_params=params(),
        name="middle",
        cost_estimate=cost(2 * rows * width * width, 24 * rows * width),
    )(h1, dn, cotangent, valid, gain[None], own, far)


def result_kernel(h_ref, branch_ref, valid_ref, bias_ref, after_ref, out_ref):
    out_ref[...] = valid_ref[...] * (h_ref[...] + branch_ref[...] + bias_ref[...])


def result(h1, branch, valid, bias, after):
    rows, width = h1.shape
    block = min(512, rows)
    tall, whole = row_specs(rows, width, block)
    return pl.pallas_call(
        result_kernel,
        grid=(rows // block,),
        in_specs=[
            tall(), tall(), tall(1), whole(1, width), pl.BlockSpec(memory_space=pl.ANY)
        ],
        out_specs=tall(),
        out_shape=jax.ShapeDtypeStruct((rows, width), F32),
        compiler_params=params(),
        name="result",
        cost_estimate=cost(rows * width, 12 * rows * width),
    )(h1, branch, valid, bias[None], after)


def leave_kernel(back_ref, w_ref, sent_ref, h_ref, dh_ref, gain_ref, *refs):
    low_ref, sums_ref = refs[-2:]
    grad = dot_tn(back_ref[...], w_ref[...]) + sent_ref[...].astype(F32)
    back, gain_sum = norm_back_rows(grad, h_ref[...], gain_ref[...])
    low = (back + dh_ref[...]).astype(BF)
    low_ref[...] = low
    add_up(sums_ref, [jnp.sum(low.astype(F32), 0, keepdims=True), gain_sum])


def leave(back, w, sent, h0, dh1, gain, after):
    rows, width = h0.shape
    block = min(512, rows)
    tall, whole = row_specs(rows, width, block)
    return pl.pallas_call(
        leave_kernel,
        grid=(rows // block,),
        in_specs=[
            pl.BlockSpec((back.shape[0], block), lambda i: (0, i)),
            whole(*w.shape),
            tall(),
            tall(),
            tall(),
            whole(1, width),
        ]
        + [pl.BlockSpec(memory_space=pl.ANY)] * len(after),
        out_specs=[tall(), whole(2, width)],
        out_shape=[
            jax.ShapeDtypeStruct((rows, width), BF),
            jax.ShapeDtypeStruct((2, width), F32),
        ],
        compiler_params=params(),
        name="leave",
        cost_estimate=cost(2 * rows * width * back.shape[0], 16 * rows * width),
    )(back, w, sent, h0, dh1, gain[None], *after)


def segments(ends_ref, first, count):
    pos = lax.broadcasted_iota(jnp.int32, (1, count), 1) + first
    seg = jnp.zeros((1, count), jnp.int32)
    for i in range(ends_ref.shape[0]):
        seg = seg + (pos >= ends_ref[i]).astype(jnp.int32)
    return lax.broadcasted_iota(jnp.int32, (SEGS, 1), 0) == seg


def zeros(rows, count):
    return jnp.zeros((rows, count), F32)


def key_pieces(count):
    if count == 4096:
        main = [(k0, 384) for k0 in range(0, FIRST_MOST, 384)]
        whole = [(k0, 1024) for k0 in range(0, count, 1024)]
        return [
            (0, 2048, main),
            (2048, 1536, main),
            (3584, 256, whole),
            (FIRST_MOST, 256, [(FIRST_LEAST, count - FIRST_LEAST)]),
        ]
    step = min(512, count)
    every = [(k0, step) for k0 in range(0, count, step)]
    return [(q0, step, every) for q0 in range(0, count, step)]


def attend_kernel(cut, ends_ref, part_ref, q_ref, k_ref, v_ref, o_ref, l_ref, kaug, qaug, vaug):
    count = k_ref.shape[1]
    here = q_ref.shape[1]
    part = part_ref[0]
    same = segments(ends_ref, 0, count)
    kaug[...] = (
        jnp.concatenate([k_ref[...].astype(F32), jnp.where(same, 0.0, -1e30), zeros(48, count)], 0)
        .T.astype(BF)
    )
    mine = segments(ends_ref, part * here, here)
    qaug[...] = jnp.concatenate(
        [q_ref[...].astype(F32), jnp.where(mine, 1.0, 0.0), zeros(48, here)], 0
    ).astype(BF)
    first = lax.broadcasted_iota(jnp.int32, (SEGS, count), 0) == 0
    vaug[...] = jnp.concatenate([v_ref[...].astype(F32), jnp.where(first, 1.0, 0.0)], 0).astype(BF)

    def block(q0, width, pieces):
        queries = qaug[:, q0 : q0 + width]
        top = jnp.full((1, width), -jnp.inf, F32)
        acc = jnp.zeros((HEAD_DIM + SEGS, width), F32)
        for k0, n in pieces:
            scores = dot(kaug[k0 : k0 + n, :], queries)
            higher = jnp.maximum(top, jnp.max(scores, axis=0, keepdims=True))
            probs = jnp.exp2(scores - higher).astype(BF)
            acc = acc * jnp.exp2(top - higher) + dot(vaug[:, k0 : k0 + n], probs)
            top = higher
        total = acc[HEAD_DIM : HEAD_DIM + 1]
        o_ref[:, q0 : q0 + width] = (acc[:HEAD_DIM] / total).astype(BF)
        l_ref[0, :, q0 : q0 + width] = top + jnp.log2(total)

    pieces = key_pieces(count)
    for p in range(cut):
        low, high = p * here, (p + 1) * here

        @pl.when(part == p)
        def _():
            for q0, width, keys in pieces:
                if low <= q0 < high:
                    block(q0 - low, width, keys)


def attend(ends, part, query, keys, values, cut):
    rows, count = query.shape
    heads = rows // HEAD_DIM
    here = count // cut
    whole = pl.BlockSpec((HEAD_DIM, count), lambda h, e, p: (h, 0))
    return pl.pallas_call(
        functools.partial(attend_kernel, cut),
        grid_spec=pltpu.PrefetchScalarGridSpec(
            num_scalar_prefetch=2,
            grid=(heads,),
            in_specs=[
                pl.BlockSpec((HEAD_DIM, here), lambda h, e, p: (h, p[0])),
                whole,
                whole,
            ],
            out_specs=[
                pl.BlockSpec((HEAD_DIM, here), lambda h, e, p: (h, 0)),
                pl.BlockSpec((1, 1, here), lambda h, e, p: (h, 0, 0)),
            ],
            scratch_shapes=[
                pltpu.VMEM((count, 128), BF),
                pltpu.VMEM((128, here), BF),
                pltpu.VMEM((HEAD_DIM + SEGS, count), BF),
            ],
        ),
        out_shape=[
            jax.ShapeDtypeStruct((rows, here), BF),
            jax.ShapeDtypeStruct((heads, 1, here), F32),
        ],
        compiler_params=params(),
        name="attend",
        cost_estimate=cost(4 * rows * here * count, 8 * rows * count),
    )(ends, part, query, keys, values)


def local_segments(ends_ref, part, count):
    return segments(ends_ref, part * count, count)


def spans(first, last, step):
    return [(k0, min(step, last - k0)) for k0 in range(first, last, step)]


def regions(query_part, key_parts, half):
    edge, start = FIRST_MOST - half, FIRST_LEAST - half

    def keys(first, last, p):
        return [(p, k0, n) for k0, n in spans(first, last, 1024)]

    if query_part == 0:
        found = []
        for p in key_parts:
            found += keys(0, half, 0) if p == 0 else keys(0, edge, 1)
        return [(0, half, found)]
    low = edge - 256
    if list(key_parts) == [0]:
        return [(0, edge, keys(0, half, 0)), (edge, half - edge, [])]
    main, mixed, last = [], [], []
    for p in key_parts:
        if p == 0:
            main += keys(0, half, 0)
            mixed += keys(0, half, 0)
        else:
            main += keys(0, edge, 1)
            mixed += keys(0, half, 1)
            last += [(1, start, half - start)]
    return [(0, low, main), (low, 256, mixed), (edge, half - edge, last)]


def half_kernel(query_far, key_sides, given, last, ends_ref, part_ref, *refs):
    refs = list(refs)
    q_ref = refs.pop(0)
    kv = {side: (refs.pop(0), refs.pop(0)) for side in key_sides}
    acc_in, top_in = (refs.pop(0), refs.pop(0)) if given else (None, None)
    out_ref, top_ref = refs.pop(0), refs.pop(0)
    qaug = refs.pop(0)
    kaug = {side: refs.pop(0) for side in key_sides}
    vaug = {side: refs.pop(0) for side in key_sides}
    half = q_ref.shape[1]
    rank = part_ref[0]

    @pl.when(pl.program_id(0) == 0)
    def _():
        for side in key_sides:
            same = local_segments(ends_ref, rank if side == 0 else 1 - rank, half)
            blank = zeros(HEAD_DIM, half)
            kaug[side][...] = (
                jnp.concatenate([blank, jnp.where(same, 0.0, -1e30), zeros(48, half)], 0)
                .T.astype(BF)
            )
            first = lax.broadcasted_iota(jnp.int32, (SEGS, half), 0) == 0
            vaug[side][HEAD_DIM:, :] = jnp.where(first, 1.0, 0.0).astype(BF)
        mine = local_segments(ends_ref, 1 - rank if query_far else rank, half)
        qaug[HEAD_DIM:, :] = jnp.concatenate(
            [jnp.where(mine, 1.0, 0.0), zeros(48, half)], 0
        ).astype(BF)

    for side in key_sides:
        kaug[side][:, :HEAD_DIM] = kv[side][0][...].T
        vaug[side][:HEAD_DIM, :] = kv[side][1][...]
    qaug[:HEAD_DIM, :] = q_ref[...]

    for here in range(2):
        query_part = 1 - here if query_far else here
        part_of = {side: here if side == 0 else 1 - here for side in key_sides}
        side_of = {p: side for side, p in part_of.items()}

        @pl.when(rank == here)
        def _():
            for q0, width, pieces in regions(query_part, list(side_of), half):
                there = slice(q0, q0 + width)
                queries = qaug[:, there]
                if given:
                    top, acc = top_in[0, :, there], acc_in[0, :, there]
                else:
                    top = jnp.full((1, width), -jnp.inf, F32)
                    acc = jnp.zeros((HEAD_DIM + SEGS, width), F32)
                for p, k0, n in pieces:
                    side = side_of[p]
                    scores = dot(kaug[side][k0 : k0 + n, :], queries)
                    higher = jnp.maximum(top, jnp.max(scores, axis=0, keepdims=True))
                    probs = jnp.exp2(scores - higher).astype(BF)
                    acc = acc * jnp.exp2(top - higher) + dot(vaug[side][:, k0 : k0 + n], probs)
                    top = higher
                if last:
                    total = acc[HEAD_DIM : HEAD_DIM + 1]
                    out_ref[:, there] = (acc[:HEAD_DIM] / total).astype(BF)
                    top_ref[0, :, there] = top + jnp.log2(total)
                else:
                    out_ref[0, :, there] = acc
                    top_ref[0, :, there] = top


def attend_half(name, ends, rank, query, query_far, keys, carry=None, last=True):
    rows, half = query.shape
    heads = rows // HEAD_DIM
    sides = sorted(keys)
    head = pl.BlockSpec((HEAD_DIM, half), lambda h, e, r: (h, 0))
    tall = pl.BlockSpec((1, HEAD_DIM + SEGS, half), lambda h, e, r: (h, 0, 0))
    line = pl.BlockSpec((1, 1, half), lambda h, e, r: (h, 0, 0))
    operands = [query]
    for side in sides:
        operands += list(keys[side])
    specs = [head] * len(operands)
    if carry is not None:
        operands += list(carry)
        specs += [tall, line]
    return pl.pallas_call(
        functools.partial(half_kernel, query_far, sides, carry is not None, last),
        grid_spec=pltpu.PrefetchScalarGridSpec(
            num_scalar_prefetch=2,
            grid=(heads,),
            in_specs=specs,
            out_specs=[head if last else tall, line],
            scratch_shapes=[pltpu.VMEM((128, half), BF)]
            + [pltpu.VMEM((half, 128), BF)] * len(sides)
            + [pltpu.VMEM((HEAD_DIM + SEGS, half), BF)] * len(sides),
        ),
        out_shape=[
            jax.ShapeDtypeStruct((rows, half), BF)
            if last
            else jax.ShapeDtypeStruct((heads, HEAD_DIM + SEGS, half), F32),
            jax.ShapeDtypeStruct((heads, 1, half), F32),
        ],
        compiler_params=params(),
        name=name,
        cost_estimate=cost(16 * rows * half * half * len(sides), 8 * rows * half),
    )(ends, rank, *operands)


def split3(x):
    a = x.astype(BF).astype(F32)
    b = (x - a).astype(BF).astype(F32)
    row = lax.broadcasted_iota(jnp.int32, (SEGS, 1), 0)
    return jnp.where(row == 0, a, jnp.where(row == 1, b, jnp.where(row == 2, x - a - b, 0.0)))


def attend_back_kernel(
    ends_ref, q_ref, k_ref, v_ref, g_ref, o_ref, l_ref, cos_ref, sin_ref, d_ref,
    kaug, vaug, qaug, gaug, pair, dq,
):
    count = k_ref.shape[1]
    same = segments(ends_ref, 0, count)
    row = lax.broadcasted_iota(jnp.int32, (SEGS, count), 0)
    shift = jnp.where(row < 3, 1.0, 0.0)
    g = g_ref[...].astype(F32)
    q = q_ref[...].astype(F32)
    delta = jnp.sum(g * o_ref[...].astype(F32), axis=0, keepdims=True)
    kaug[...] = (
        jnp.concatenate(
            [k_ref[...].astype(F32), jnp.where(same, 0.0, -1e30), shift, zeros(32, count)], 0
        )
        .T.astype(BF)
    )
    vaug[...] = (
        jnp.concatenate([v_ref[...].astype(F32), shift, zeros(48, count)], 0).T.astype(BF)
    )
    qaug[...] = jnp.concatenate(
        [q, jnp.where(same, 1.0, 0.0), split3(-l_ref[0]), zeros(32, count)], 0
    ).astype(BF)
    gaug[...] = jnp.concatenate([g, split3(-delta), zeros(48, count)], 0).astype(BF)
    pair[...] = jnp.concatenate([q, g], 0).T.astype(BF)
    dq[...] = jnp.zeros_like(dq)

    def turn(grad, c, s, factor):
        a, b = grad[:HALF], grad[HALF:]
        return (
            jnp.concatenate([a * c + b * s, b * c - a * s], 0) * factor
        ).astype(BF)

    def chunk(k0, n, queries):
        where = pl.ds(k0, n)
        kb, vb, kt = kaug[where, :], vaug[where, :], k_ref[:, where]
        dk = jnp.zeros((n, HEAD_DIM), F32)
        dv = jnp.zeros((n, HEAD_DIM), F32)
        for q0, width in queries:
            there = slice(q0, q0 + width)
            probs = jnp.exp2(dot(kb, qaug[:, there]))
            tilt = (probs * dot(vb, gaug[:, there])).astype(BF)
            dv = dv + dot(probs.astype(BF), pair[there, HEAD_DIM:])
            dk = dk + dot(tilt, pair[there, :HEAD_DIM])
            dq[:, there] += dot(kt, tilt)
        c, s = cos_ref[:, where], sin_ref[:, where]
        d_ref[1, 0, :, where] = turn(dk.T, c, s, LN2)
        d_ref[2, 0, :, where] = dv.T.astype(BF)

    if count == 4096:
        main = [(q0, 1920) for q0 in range(0, FIRST_MOST, 1920)]

        def step(i, carry):
            chunk(pl.multiple_of(i * 512, 512), 512, main)
            return carry

        lax.fori_loop(0, 7, step, 0)
        chunk(3584, 256, [(q0, 1024) for q0 in range(0, count, 1024)])
        chunk(FIRST_MOST, count - FIRST_MOST, [(3584, 512)])
    else:
        size = min(512, count)

        def step(i, carry):
            chunk(pl.multiple_of(i * size, size), size, [(q, size) for q in range(0, count, size)])
            return carry

        lax.fori_loop(0, count // size, step, 0)
    d_ref[0, 0] = turn(dq[...], cos_ref[...], sin_ref[...], 0.125)


def attend_back(ends, query, keys, values, grad, mixed, logsum, cosine, sine):
    rows, count = query.shape
    heads = rows // HEAD_DIM
    whole = pl.BlockSpec((HEAD_DIM, count), lambda h, e: (h, 0))
    table = pl.BlockSpec((HALF, count), lambda h, e: (0, 0))
    out = pl.pallas_call(
        attend_back_kernel,
        grid_spec=pltpu.PrefetchScalarGridSpec(
            num_scalar_prefetch=1,
            grid=(heads,),
            in_specs=[whole] * 5
            + [pl.BlockSpec((1, 1, count), lambda h, e: (h, 0, 0)), table, table],
            out_specs=pl.BlockSpec((3, 1, HEAD_DIM, count), lambda h, e: (0, h, 0, 0)),
            scratch_shapes=[
                pltpu.VMEM((count, 128), BF),
                pltpu.VMEM((count, 128), BF),
                pltpu.VMEM((128, count), BF),
                pltpu.VMEM((128, count), BF),
                pltpu.VMEM((count, 128), BF),
                pltpu.VMEM((HEAD_DIM, count), F32),
            ],
        ),
        out_shape=jax.ShapeDtypeStruct((3, heads, HEAD_DIM, count), BF),
        compiler_params=params(),
        name="attend_back",
        cost_estimate=cost(10 * rows * count * count, 16 * rows * count),
    )(ends, query, keys, values, grad, mixed, logsum, cosine, sine)
    return out.reshape(3 * rows, count)


def turn_back(grad, c, s, factor):
    a, b = grad[:HALF], grad[HALF:]
    return (jnp.concatenate([a * c + b * s, b * c - a * s], 0) * factor).astype(BF)


def back_chunks(key_part, query_parts, half):
    edge = FIRST_MOST - half
    low = edge - 256
    found = []
    if key_part == 0:
        queries = []
        for p in query_parts:
            queries += [(p, 0, half if p == 0 else edge)]
        return [(0, half, 512, queries)]
    main = [(p, 0, half if p == 0 else edge) for p in query_parts]
    found.append((0, low, 512, main))
    found.append((low, 256, 256, [(p, 0, half) for p in query_parts]))
    if 1 in query_parts:
        found.append((edge, half - edge, 256, [(1, low, half - low)]))
    return found


def half_back_kernel(near_only, given_partial, finish, ends_ref, part_ref, *refs):
    refs = list(refs)
    sides = (0,) if near_only else (0, 1)
    given = {side: [refs.pop(0) for _ in range(8)] for side in sides}
    partial_in = refs.pop(0) if given_partial else None
    while len(refs) > (1 if near_only else 2) + 7:
        refs.pop(0)
    out_ref = None if near_only else refs.pop(0)
    near_ref = refs.pop(0)
    kaug, vaug, qaug, gaug, pair, dq, sums = refs
    rank = part_ref[0]
    half = given[0][0].shape[1]

    @pl.when(pl.program_id(0) == 0)
    def _():
        row = lax.broadcasted_iota(jnp.int32, (SEGS, half), 0)
        shift = jnp.where(row < 3, 1.0, 0.0)
        blank = zeros(HEAD_DIM, half)
        for side in sides:
            there = slice(side * half, side * half + half)
            same = local_segments(ends_ref, rank if side == 0 else 1 - rank, half)
            kaug[there, :] = (
                jnp.concatenate([blank, jnp.where(same, 0.0, -1e30), shift, zeros(32, half)], 0)
                .T.astype(BF)
            )
            vaug[there, :] = jnp.concatenate([blank, shift, zeros(48, half)], 0).T.astype(BF)
            qaug[HEAD_DIM:, there] = jnp.concatenate(
                [jnp.where(same, 1.0, 0.0), zeros(48, half)], 0
            ).astype(BF)
            gaug[HEAD_DIM:, there] = blank.astype(BF)

    for side in sides:
        q_ref, k_ref, v_ref, g_ref, o_ref, l_ref = given[side][:6]
        there = slice(side * half, side * half + half)
        g = g_ref[...]
        q = q_ref[...]
        delta = jnp.sum(g.astype(F32) * o_ref[...].astype(F32), axis=0, keepdims=True)
        kaug[there, :HEAD_DIM] = k_ref[...].T
        vaug[there, :HEAD_DIM] = v_ref[...].T
        qaug[:HEAD_DIM, there] = q
        qaug[HEAD_DIM + SEGS : HEAD_DIM + 2 * SEGS, there] = split3(-l_ref[0]).astype(BF)
        gaug[:HEAD_DIM, there] = g
        gaug[HEAD_DIM : HEAD_DIM + SEGS, there] = split3(-delta).astype(BF)
        pair[there, :] = jnp.concatenate([q, g], 0).T
    dq[...] = jnp.zeros_like(dq)
    if given_partial:
        dq[:, :half] = partial_in[0, 0]
        sums[...] = partial_in[1:, 0]
    else:
        sums[...] = jnp.zeros_like(sums)

    def chunk(side, k0, n, queries):
        where = pl.ds(side * half + k0, n)
        kb, vb, kt = kaug[where, :], vaug[where, :], given[side][1][:, pl.ds(k0, n)]
        dk = jnp.zeros((n, HEAD_DIM), F32)
        dv = jnp.zeros((n, HEAD_DIM), F32)
        for q0, width in queries:
            there = slice(q0, q0 + width)
            probs = jnp.exp2(dot(kb, qaug[:, there]))
            tilt = (probs * dot(vb, gaug[:, there])).astype(BF)
            dv = dv + dot(probs.astype(BF), pair[there, HEAD_DIM:])
            dk = dk + dot(tilt, pair[there, :HEAD_DIM])
            dq[:, there] += dot(kt, tilt)
        dk, dv = dk.T, dv.T
        if side == 0:
            sums[0, :, pl.ds(k0, n)] += dk
            sums[1, :, pl.ds(k0, n)] += dv
            return
        c, s = given[side][6][:, pl.ds(k0, n)], given[side][7][:, pl.ds(k0, n)]
        out_ref[1, 0, :, pl.ds(k0, n)] = turn_back(dk, c, s, LN2)
        out_ref[2, 0, :, pl.ds(k0, n)] = dv.astype(BF)

    for here in range(2):

        @pl.when(rank == here)
        def _():
            side_of = {here: 0, 1 - here: 1}
            for key_part, side in side_of.items():
                if near_only and side == 1:
                    continue
                if near_only:
                    query_parts = [here]
                else:
                    query_parts = [0, 1] if side == 1 else [1 - here]
                for k0, total, n, queries in back_chunks(key_part, query_parts, half):
                    spread = [(side_of[p] * half + q0, width) for p, q0, width in queries]
                    if total == n:
                        chunk(side, k0, n, spread)
                        continue

                    def step(i, carry):
                        chunk(side, pl.multiple_of(k0 + i * n, n), n, spread)
                        return carry

                    lax.fori_loop(0, total // n, step, 0)

    if not near_only:
        out_ref[0, 0] = turn_back(dq[:, half:], given[1][6][...], given[1][7][...], 0.125)
    if finish:
        c, s = given[0][6][...], given[0][7][...]
        near_ref[0, 0] = turn_back(dq[:, :half], c, s, 0.125)
        near_ref[1, 0] = turn_back(sums[0], c, s, LN2)
        near_ref[2, 0] = sums[1].astype(BF)
    else:
        near_ref[0, 0] = dq[:, :half]
        near_ref[1:, 0] = sums[...]


def half_back(name, ends, rank, sides, first, count, finish, partial=None, written=(), after=None):
    rows, half = sides[0][0].shape
    heads = rows // HEAD_DIM
    near_only = len(sides) == 1
    head = pl.BlockSpec((HEAD_DIM, half), lambda h, e, r: (h + first, 0))
    line = pl.BlockSpec((1, 1, half), lambda h, e, r: (h + first, 0, 0))
    table = pl.BlockSpec((HALF, half), lambda h, e, r: (0, 0))
    block = pl.BlockSpec((3, 1, HEAD_DIM, half), lambda h, e, r: (0, h + first, 0, 0))
    anywhere = pl.BlockSpec(memory_space=pl.ANY)
    operands, specs = [], []
    for side in sides:
        operands += list(side)
        specs += [head] * 5 + [line, table, table]
    result = jax.ShapeDtypeStruct((3, heads, HEAD_DIM, half), BF)
    if partial is not None:
        operands.append(partial)
        specs.append(block)
    aliases = {}
    for i, array in enumerate(written):
        if array is not None:
            aliases[2 + len(operands)] = i
            operands.append(array)
            specs.append(anywhere)
    if after is not None:
        operands.append(after)
        specs.append(anywhere)
    near_result = result if finish else jax.ShapeDtypeStruct(result.shape, F32)
    out_shape = [near_result] if near_only else [result, near_result]
    out_specs = [block] * len(out_shape)
    wide = half * len(sides)
    return pl.pallas_call(
        functools.partial(half_back_kernel, near_only, partial is not None, finish),
        grid_spec=pltpu.PrefetchScalarGridSpec(
            num_scalar_prefetch=2,
            grid=(count,),
            in_specs=specs,
            out_specs=out_specs,
            scratch_shapes=[
                pltpu.VMEM((wide, 128), BF),
                pltpu.VMEM((wide, 128), BF),
                pltpu.VMEM((128, wide), BF),
                pltpu.VMEM((128, wide), BF),
                pltpu.VMEM((wide, 128), BF),
                pltpu.VMEM((HEAD_DIM, wide), F32),
                pltpu.VMEM((2, HEAD_DIM, half), F32),
            ],
        ),
        out_shape=out_shape,
        input_output_aliases=aliases,
        compiler_params=params(),
        name=name,
        cost_estimate=cost(40 * count * HEAD_DIM * half * half * (1 if near_only else 3), 40 * count * HEAD_DIM * half),
    )(ends, rank, *operands)


def ffn_kernel(step, given, src_ref, dst_ref, n_ref, g_ref, up_ref, bias_ref, down_ref, *refs):
    branch_in, dn_in = refs[:2] if given else (None, None)
    branch_ref, dn_ref, dw_ref, dbias_ref, branch, dn, sems = refs[3 if given else 0 :]

    rows, depth = n_ref.shape
    steps = [(i, slice(r0, r0 + step)) for i, r0 in enumerate(range(0, rows, step))]
    opening = (pl.program_id(0) == 0) & (pl.program_id(1) == 0)
    closing = (pl.program_id(0) == pl.num_programs(0) - 1) & (
        pl.program_id(1) == pl.num_programs(1) - 1
    )

    def moves(i, part, out):
        if out:
            pairs = ((branch, branch_ref), (dn, dn_ref))
        else:
            pairs = ((branch_in, branch), (dn_in, dn))
        return [
            pltpu.make_async_copy(src.at[part, :], dst.at[part, :], sems.at[j, i])
            for j, (src, dst) in enumerate(pairs)
        ]

    @pl.when(opening)
    def _():
        if given:
            for i, part in steps:
                for move in moves(i, part, False):
                    move.start()
        else:
            branch[...] = jnp.zeros_like(branch)
            dn[...] = jnp.zeros_like(dn)

    up = up_ref[...].reshape(depth, -1)
    down, bias = down_ref[0, 0], bias_ref[0].astype(F32)
    width = up.shape[1]
    dup = jnp.zeros((width, depth), F32)
    ddown = jnp.zeros((width, depth), F32)
    dbias = jnp.zeros((1, width), F32)
    for i, part in steps:
        x, y = n_ref[part, :], g_ref[part, :]
        u = dot(x, up) + bias
        dz = dot_nt(y, down)
        normal = 0.5 * (1.0 + lax.erf(u * 0.7071067811865476))
        density = jnp.exp(-0.5 * u * u) * 0.3989422804014327
        z = (u * normal).astype(BF)
        du = (dz * (normal + u * density)).astype(BF)
        if given:

            @pl.when(opening)
            def _():
                for move in moves(i, part, False):
                    move.wait()

        branch[part, :] += dot(z, down)
        dn[part, :] += dot_nt(du, up)

        @pl.when(closing)
        def _():
            for move in moves(i, part, True):
                move.start()

        ddown = ddown + dot_tn(z, y)
        dup = dup + dot_tn(du, x)
        dbias = dbias + jnp.sum(du.astype(F32), axis=0, keepdims=True)
    dw_ref[0, 0, :width, :] = dup.astype(BF)
    dw_ref[0, 0, width:, :] = ddown.astype(BF)
    dbias_ref[0] = dbias

    @pl.when(closing)
    def _():
        for i, part in steps:
            for move in moves(i, part, True):
                move.wait()


def ffn_block(hidden):
    return min(512, hidden // 2)


def ffn(name, n2, grad, up, bias, down, extra, parts, src, dst, before=None):
    rows, depth = n2.shape
    hidden = up.shape[3]
    block = ffn_block(hidden)
    per = hidden // 2 // block
    step = min(512, rows)
    once = pl.BlockSpec(
        (rows, depth), lambda p, i, f, t: (0, 0), pipeline_mode=pl.Buffered(1)
    )
    anywhere = pl.BlockSpec(memory_space=pl.ANY)
    operands = [n2, grad, up, bias, down] + ([] if before is None else list(before))
    return pl.pallas_call(
        functools.partial(ffn_kernel, step, before is not None),
        grid_spec=pltpu.PrefetchScalarGridSpec(
            num_scalar_prefetch=2,
            grid=(src.shape[0], 2 * per),
            in_specs=[
                once,
                once,
                pl.BlockSpec((2, 1, depth // 2, block), lambda p, i, f, t: (0, f[p], 0, i)),
                pl.BlockSpec((1, 1, block), lambda p, i, f, t: (f[p], 0, i)),
                pl.BlockSpec(
                    (1, 1, block, depth), lambda p, i, f, t: (i // per, f[p], i % per, 0)
                ),
            ]
            + ([] if before is None else [anywhere] * 3),
            out_specs=[anywhere] * 2
            + [
                pl.BlockSpec(
                    (1, 1, 2 * block, depth), lambda p, i, f, t: (i // per, t[p], i % per, 0)
                ),
                pl.BlockSpec((1, 1, block), lambda p, i, f, t: (p, 0, i)),
            ],
            scratch_shapes=[pltpu.VMEM((rows, depth), F32)] * 2
            + [pltpu.SemaphoreType.DMA((2, rows // step))],
        ),
        out_shape=[jax.ShapeDtypeStruct((rows, depth), F32)] * 2
        + [
            jax.ShapeDtypeStruct((2, parts, hidden + extra, depth), BF),
            jax.ShapeDtypeStruct((src.shape[0], 1, hidden), F32),
        ],
        input_output_aliases={} if before is None else {9: 2},
        compiler_params=params(),
        name=name,
        cost_estimate=cost(12 * rows * depth * hidden * src.shape[0], 8 * depth * hidden * src.shape[0]),
    )(src, dst, *operands)


def out_back_kernel(part_ref, near_ref, in_ref, grad_ref, sums_ref, out_ref):
    for side, mixed_ref in enumerate((near_ref, in_ref)):

        @pl.when(pl.program_id(0) == side)
        def _():
            out_ref[0, 0] = dot(mixed_ref[...], grad_ref[...]).astype(BF)


def out_back(mixed, grad, sums, extra, parts):
    heads, rows = mixed[0].shape
    total, depth = sums.shape[2:]
    piece = pl.BlockSpec((extra, rows), lambda p, c, t: (c, 0))
    return pl.pallas_call(
        out_back_kernel,
        grid_spec=pltpu.PrefetchScalarGridSpec(
            num_scalar_prefetch=1,
            grid=(2, 2),
            in_specs=[
                piece,
                piece,
                pl.BlockSpec((rows, depth), lambda p, c, t: (0, 0)),
                pl.BlockSpec(memory_space=pl.ANY),
            ],
            out_specs=pl.BlockSpec(
                (1, 1, extra, depth), lambda p, c, t: (c, t[p], total // extra - 1, 0)
            ),
        ),
        out_shape=jax.ShapeDtypeStruct(sums.shape, BF),
        input_output_aliases={4: 0},
        compiler_params=params(),
        name="out_back",
        cost_estimate=cost(4 * rows * depth * heads, 4 * heads * depth),
    )(parts, *mixed, grad, sums)


def project_back_kernel(*refs):
    out_ref = refs[-2]
    pairs = refs[:-3]
    total = dot(pairs[1][...], pairs[0][...])
    for i in range(2, len(pairs), 2):
        total = total + dot(pairs[i + 1][...], pairs[i][...])
    out_ref[...] = total.astype(BF)


def project_back(pairs, passed):
    total = pairs[0][1].shape[0]
    depth = pairs[0][0].shape[1]
    block = total // 3
    specs, operands = [], []
    for x, grad, at in pairs:
        specs += [
            pl.BlockSpec(x.shape, lambda i: (0, 0)),
            pl.BlockSpec((block, x.shape[0]), functools.partial(lambda at, i: (i, at), at)),
        ]
        operands += [x, grad]
    return pl.pallas_call(
        project_back_kernel,
        grid=(3,),
        in_specs=specs + [pl.BlockSpec(memory_space=pl.ANY)],
        out_specs=[
            pl.BlockSpec((block, depth), lambda i: (i, 0)),
            pl.BlockSpec(memory_space=pl.ANY),
        ],
        out_shape=[
            jax.ShapeDtypeStruct((total, depth), BF),
            jax.ShapeDtypeStruct(passed.shape, passed.dtype),
        ],
        input_output_aliases={len(operands): 1},
        compiler_params=params(),
        name="project_back",
        cost_estimate=cost(4 * pairs[0][0].shape[0] * depth * total, 8 * depth * total),
    )(*operands, passed)


def turn_kernel(x_ref, *out_refs):
    for i, out_ref in enumerate(out_refs):

        @pl.when(pl.program_id(0) == i)
        def _():
            out_ref[...] = x_ref[...].astype(F32).T


def turn(x, parts):
    rows, depth = x.shape
    block = rows // parts
    return pl.pallas_call(
        turn_kernel,
        grid=(parts,),
        in_specs=[pl.BlockSpec((block, depth), lambda i: (i, 0))],
        out_specs=[pl.BlockSpec((depth, block), lambda i: (0, 0))] * parts,
        out_shape=[jax.ShapeDtypeStruct((depth, block), F32)] * parts,
        compiler_params=params(),
        name="turn",
        cost_estimate=cost(rows * depth, 6 * rows * depth),
    )(x)


MESH = pl.DeviceIdType.MESH


def sum_all_kernel(
    big_ref, small_ref, out_ref, small_out_ref,
    buf, done, core_in, first_in, second_in, z_in, small, small_in, small_z,
    local, send, recv, small_send, small_recv,
):
    o, c, m = lax.axis_index("dpo"), lax.axis_index("core"), lax.axis_index("mp")
    y, z = lax.rem(o, 2), lax.div(o, 2)
    zs = 4
    size = buf.shape[0] // 2
    half, quarter, eighth, last = size // 2, size // 4, size // 8, size // 32
    sibling = (o, 1 - c, m)
    across = (o, c, 1 - m)
    beside = (z * 2 + 1 - y, c, m)
    others = [lax.rem(z + d, zs) for d in range(1, zs)]

    def along(j):
        return (j * 2 + y, c, m)

    load = pltpu.make_async_copy(big_ref, buf, local.at[0])
    load.start()
    barrier = pltpu.get_barrier_semaphore()
    for device in [sibling, across, beside] + [along(j) for j in others]:
        pl.semaphore_signal(barrier, inc=1, device_id=device, device_id_type=MESH)
    pl.semaphore_wait(barrier, 6)
    small[0] = small_ref[...]

    main, tiny = (send, recv), (small_send, small_recv)
    started = []

    def copy(src, dst, sems, i, device):
        return pltpu.make_async_remote_copy(
            src_ref=src, dst_ref=dst, send_sem=sems[0].at[i], recv_sem=sems[1].at[i],
            device_id=device, device_id_type=MESH,
        )

    def go(src, dst, sems, i, device):
        one = copy(src, dst, sems, i, device)
        one.start()
        started.append(one)
        return one

    def rows(first, n, of=buf):
        return of.at[pl.ds(pl.multiple_of(first, last), n)]

    def add(first, n, got):
        def one(i, carry):
            there = pl.ds(pl.multiple_of(first + i * 128, last), 128)
            here = pl.ds(pl.multiple_of(i * 128, 128), 128)
            buf[there, :] = (buf[there, :].astype(F32) + got[here, :].astype(F32)).astype(BF)
            return carry

        lax.fori_loop(0, n // 128, one, 0)

    turn_of = ((m, y), (y, m))
    device_of = ((across, beside), (beside, across))
    far, near, far_next, near_next, own, theirs = [], [], [], [], [], []
    for s in range(2):
        a, b = turn_of[s]
        mine = s * size + c * half
        theirs.append(s * size + (1 - c) * half)
        far.append(mine + (1 - a) * quarter)
        near.append(mine + a * quarter)
        far_next.append(near[s] + (1 - b) * eighth)
        near_next.append(near[s] + b * eighth)
        own.append(near_next[s] + z * last)

    load.wait()
    arrivals = []
    for part in range(2):
        for s in range(2):
            a = turn_of[s][0]
            start = theirs[s] + ((1 - a) if part == 0 else a) * quarter
            i = 2 * part + s
            arrivals.append(go(rows(start, quarter), core_in.at[i], main, i, sibling))
    tiny_core = go(small.at[0], small_in.at[0], tiny, 0, sibling)
    firsts = []
    for s in range(2):
        arrivals[s].wait_recv()
        add(far[s], quarter, core_in.at[s])
        firsts.append(go(rows(far[s], quarter), first_in.at[s], main, 4 + s, device_of[s][0]))
    tiny_core.wait_recv()
    small[1] = small[0] + small_in[0]
    tiny_x = go(small.at[1], small_in.at[1], tiny, 1, across)
    for s in range(2):
        arrivals[2 + s].wait_recv()
        add(near[s], quarter, core_in.at[2 + s])
    tiny_x.wait_recv()
    small[2] = small[1] + small_in[1]
    tiny_y = go(small.at[2], small_in.at[2], tiny, 2, beside)
    seconds = []
    for s in range(2):
        firsts[s].wait_recv()
        add(near[s], quarter, first_in.at[s])
        seconds.append(go(rows(far_next[s], eighth), second_in.at[s], main, 6 + s, device_of[s][1]))
    tiny_y.wait_recv()
    small_z[z] = small[2] + small_in[2]
    for j in others:
        go(small_z.at[z], small_z.at[z], tiny, 3 + z, along(j))
    for s in range(2):
        seconds[s].wait_recv()
        add(near_next[s], eighth, second_in.at[s])
        for j in others:
            go(
                rows(near_next[s] + j * last, last), z_in.at[s, z], main, 8 + 4 * s + z, along(j)
            )

    def hand(first, n, i, device):
        there = rows(first, n, done)
        return go(there, there, main, i, device)

    for s in range(2):
        total = buf[pl.ds(pl.multiple_of(own[s], last), last), :].astype(F32)
        for j in others:
            copy(z_in.at[s, j], z_in.at[s, j], main, 8 + 4 * s + j, along(j)).wait_recv()
            total = total + z_in[s, j].astype(F32)
        done[pl.ds(pl.multiple_of(own[s], last), last), :] = total.astype(BF)
        for j in others:
            hand(own[s], last, 16 + 4 * s + z, along(j))
    back_second, back_first, cores = [], [], []
    for s in range(2):
        for j in others:
            there = rows(near_next[s] + j * last, last, done)
            copy(there, there, main, 16 + 4 * s + j, along(j)).wait_recv()
        back_second.append(hand(near_next[s], eighth, 24 + s, device_of[s][1]))
        back_first.append(hand(near_next[s], eighth, 26 + s, device_of[s][0]))
        cores.append(hand(near_next[s], eighth, 28 + s, sibling))
    back_more = []
    for s in range(2):
        back_second[s].wait_recv()
        back_more.append(hand(far_next[s], eighth, 30 + s, device_of[s][0]))
        cores.append(hand(far_next[s], eighth, 32 + s, sibling))
    for j in others:
        copy(small_z.at[j], small_z.at[j], tiny, 3 + j, along(j)).wait_recv()
    small_out_ref[...] = (small_z[0] + small_z[1]) + (small_z[2] + small_z[3])
    for s in range(2):
        back_first[s].wait_recv()
        cores.append(hand(far[s] + turn_of[s][1] * eighth, eighth, 34 + s, sibling))
    for s in range(2):
        back_more[s].wait_recv()
        cores.append(hand(far[s] + (1 - turn_of[s][1]) * eighth, eighth, 36 + s, sibling))
    for one in cores:
        one.wait_recv()
    store = pltpu.make_async_copy(done, out_ref, local.at[1])
    store.start()
    for one in started:
        one.wait_send()
    store.wait()


def sum_all(big, small):
    rows, width = big.shape
    quarter, eighth, last = rows // 8, rows // 16, rows // 64
    anywhere = pl.BlockSpec(memory_space=pl.ANY)
    whole = pl.BlockSpec(memory_space=pltpu.VMEM)
    dma = pltpu.SemaphoreType.DMA
    return pl.pallas_call(
        sum_all_kernel,
        in_specs=[anywhere, whole],
        out_specs=[anywhere, whole],
        out_shape=[
            jax.ShapeDtypeStruct(big.shape, BF),
            jax.ShapeDtypeStruct(small.shape, F32),
        ],
        scratch_shapes=[
            pltpu.VMEM((rows, width), BF),
            pltpu.VMEM((rows, width), BF),
            pltpu.VMEM((4, quarter, width), BF),
            pltpu.VMEM((2, quarter, width), BF),
            pltpu.VMEM((2, eighth, width), BF),
            pltpu.VMEM((2, 4, last, width), BF),
            pltpu.VMEM((3,) + small.shape, F32),
            pltpu.VMEM((3,) + small.shape, F32),
            pltpu.VMEM((4,) + small.shape, F32),
            dma((2,)),
            dma((38,)),
            dma((38,)),
            dma((7,)),
            dma((7,)),
        ],
        compiler_params=pltpu.CompilerParams(
            collective_id=0, has_side_effects=True, vmem_limit_bytes=VMEM
        ),
        name="sum_all",
        cost_estimate=cost(rows * width, 8 * rows * width),
    )(big, small)


def join_back_kernel(grad_ref, w_ref, first_ref, second_ref):
    grad = grad_ref[...]
    width = first_ref.shape[1]
    first_ref[...] = dot_nt(grad, w_ref[:width, :])
    second_ref[...] = dot_nt(grad, w_ref[width:, :])


def join_back(grad, w):
    rows, depth = grad.shape
    width = w.shape[0] // 2
    block = min(512, rows)
    out = pl.BlockSpec((block, width), lambda i: (i, 0))
    return pl.pallas_call(
        join_back_kernel,
        grid=(rows // block,),
        in_specs=[
            pl.BlockSpec((block, depth), lambda i: (i, 0)),
            pl.BlockSpec(w.shape, lambda i: (0, 0)),
        ],
        out_specs=[out, out],
        out_shape=[jax.ShapeDtypeStruct((rows, width), F32)] * 2,
        compiler_params=params(),
        name="join_back",
        cost_estimate=cost(rows * depth * width, 8 * rows * width),
    )(grad, w)


def concat_back_kernel(x_ref, s_ref, grad_ref, out_ref):
    for i, ref in enumerate((x_ref, s_ref)):

        @pl.when(pl.program_id(0) == i)
        def _():
            out_ref[...] = dot_tn(ref[...], grad_ref[...]).astype(BF)


def concat_back(x, skip, grad):
    rows, width = grad.shape
    block = min(512, width)
    per = width // block
    return pl.pallas_call(
        concat_back_kernel,
        grid=(2, per),
        in_specs=[
            pl.BlockSpec((rows, block), lambda i, j: (0, jnp.where(i == 0, j, per - 1))),
            pl.BlockSpec((rows, block), lambda i, j: (0, jnp.where(i == 0, 0, j))),
            pl.BlockSpec((rows, width), lambda i, j: (0, 0)),
        ],
        out_specs=pl.BlockSpec((block, width), lambda i, j: (i * per + j, 0)),
        out_shape=jax.ShapeDtypeStruct((2 * width, width), BF),
        compiler_params=params(),
        name="concat_back",
        cost_estimate=cost(4 * rows * width * width, 8 * rows * width),
    )(x, skip, grad)


def unpack_kernel(core_ref, own_ref, sibling_ref, up_ref, down_ref):
    mine = core_ref[0] == pl.program_id(0)
    width = down_ref.shape[0]
    block = jnp.where(mine, own_ref[...].astype(F32), sibling_ref[...].astype(F32))
    up_ref[...] = block[:width].T
    down_ref[...] = block[width:]


def unpack(core, own, sibling, hidden):
    depth = own.shape[1]
    block = ffn_block(hidden)
    per = hidden // 2 // block
    piece = pl.BlockSpec((2 * block, depth), lambda c, i, k: (i, 0))
    return pl.pallas_call(
        unpack_kernel,
        grid_spec=pltpu.PrefetchScalarGridSpec(
            num_scalar_prefetch=1,
            grid=(2, per),
            in_specs=[piece, piece],
            out_specs=[
                pl.BlockSpec((depth, block), lambda c, i, k: (0, c * per + i)),
                pl.BlockSpec((block, depth), lambda c, i, k: (c * per + i, 0)),
            ],
        ),
        out_shape=[
            jax.ShapeDtypeStruct((depth, hidden), F32),
            jax.ShapeDtypeStruct((hidden, depth), F32),
        ],
        compiler_params=params(),
        name="unpack",
        cost_estimate=cost(depth * hidden, 12 * depth * hidden),
    )(core, own, sibling)


def body(
    inputs, skip_in, cotangent, lengths, w_concat, b_concat, gain_attn, w_query, w_key, w_value,
    w_out, b_out, gain_ffn, w_up, b_up, w_down, b_down,
):
    parts = lax.axis_size("mp")
    rank = lax.axis_index("mp")
    core = lax.axis_index("core")
    dp = ("dpo", "core")
    rows, width = inputs.shape
    group = rows * parts
    paired = parts == 2 and group == 4096
    ends, pos_all, valid_all = layout(lengths[0], group)
    valid_here = lax.dynamic_slice_in_dim(valid_all, rank * rows, rows, 0)[:, None]
    each, hidden = w_out.shape[0], b_up.shape[0]
    extra = each // 2
    index = rank.reshape(1)
    other = 1 - index
    zero = jnp.zeros((1,), jnp.int32)

    def across(x):
        return lax.ppermute(x, "mp", [(0, 1), (1, 0)])

    def piece(x, i, size, axis=0):
        return lax.dynamic_slice_in_dim(x, i * size, size, axis)

    def order(near, far, axis):
        return jnp.where(
            rank == 0, jnp.concatenate([near, far], axis), jnp.concatenate([far, near], axis)
        )

    def core_half(w):
        return piece(w, core, w.shape[0] // 2)

    def gather(half):
        return lax.all_gather(half, ("core", "mp"), axis=0).reshape((2, parts) + half.shape)

    w_turned = jnp.concatenate([w_query.T, w_key.T, w_value.T], axis=0)
    grad_rows = cotangent.astype(F32) * valid_here
    grad_low = grad_rows.astype(BF)
    half_up, half_down = core_half(w_up), core_half(w_down)
    if paired:
        bias_far, out_piece = across(b_up), across(core_half(w_out))
        h0, n1 = enter(inputs, skip_in, w_concat, b_concat, gain_attn, 0, rows)
        n1, bias_far, out_piece = lax.optimization_barrier((n1, bias_far, out_piece))
        n1_far = across(n1)
        out_rest = lax.ppermute(out_piece, "core", [(0, 1), (1, 0)])
        out_far = jnp.where(
            core == 0,
            jnp.concatenate([out_piece, out_rest]),
            jnp.concatenate([out_rest, out_piece]),
        )
        tables_near = tables(piece(pos_all, rank, rows))
        bias_both = jnp.stack([bias_far, bias_far]).reshape(2, 1, hidden)
        q_near, k_near, v_near = project(
            n1, w_turned, *tables_near, after=(out_far, grad_low, bias_both, valid_here)
        )
        start = attend_half(
            "near_near", ends, index, q_near, False, {0: (k_near, v_near)}, last=False
        )
        tables_far = tables(piece(pos_all, 1 - rank, rows))
        n1_far, start, half_up = lax.optimization_barrier((n1_far, start, half_up))
        up_all = gather(half_up)
        q_far, k_far, v_far = project(n1_far, w_turned, *tables_far)
        mixed_far, log_far = attend_half(
            "far_all", ends, index, q_far, True, {0: (k_near, v_near), 1: (k_far, v_far)}
        )
        mixed_in = across(mixed_far)
        mixed_near, log_near = attend_half(
            "near_far", ends, index, q_near, False, {1: (k_far, v_far)}, carry=start
        )
        mixed_in, mixed_near, half_down = lax.optimization_barrier(
            (mixed_in, mixed_near, half_down)
        )
        down_all = gather(half_down)
        h1, n2 = upper(h0, mixed_near, mixed_in, w_out, out_far, b_out, gain_ffn)
        branch, grad_n2, sums, bias_near = ffn(
            "ffn_near", n2, grad_low, w_up.reshape(2, 1, width // 2, hidden),
            b_up.reshape(1, 1, hidden), w_down.reshape(2, 1, hidden // 2, width),
            extra, parts, zero, index,
        )
        branch, grad_n2, sums, grad_bias = ffn(
            "ffn_far", n2, grad_low, up_all, bias_both, down_all, extra, parts, other, other,
            before=(branch, grad_n2, sums),
        )
        grad_bias = order(bias_near, grad_bias, 0)
        grad_h1, grad_h1_low, grad_near, grad_sent, early = middle(
            h1, grad_n2, cotangent, valid_here, gain_ffn, w_out, out_far
        )
        grad_far = across(grad_sent)
        sums = out_back(
            (mixed_near, mixed_in), grad_h1_low, sums, extra, jnp.concatenate([index, other])
        )
    else:
        joined = jnp.concatenate([inputs, skip_in], axis=1)
        h0 = dot(joined, w_concat) + b_concat
        scale_one = lax.rsqrt(jnp.mean(h0 * h0, axis=-1, keepdims=True) + EPS)
        n1 = (h0 * scale_one * gain_attn).astype(BF)
        n1_all = lax.all_gather(n1, "mp", axis=0, tiled=True)
        bias_all = lax.all_gather(b_up, "mp", axis=0).reshape(parts, 1, -1)
        w_out_all = lax.all_gather(w_out, "mp", axis=0, tiled=True)
        up_all, down_all = gather(half_up), gather(half_down)
        cosine, sine = tables(pos_all)
        query, keys, values = project(n1_all, w_turned, cosine, sine)
        mixed, logsum = attend(ends, zero, query, keys, values, 1)
        mixed_rows = lax.all_to_all(mixed, "mp", 1, 0, tiled=True)
        h1 = h0 + dot_tn(mixed_rows, w_out_all) + b_out
        scale_two = lax.rsqrt(jnp.mean(h1 * h1, axis=-1, keepdims=True) + EPS)
        n2 = (h1 * scale_two * gain_ffn).astype(BF)
        every = jnp.arange(parts, dtype=jnp.int32)
        branch, grad_n2, sums, grad_bias = ffn(
            "ffn", n2, grad_low, up_all, bias_all, down_all, extra, parts, every, every
        )
        output = valid_here * (h1 + branch + b_down)
        grad_h1, grad_gain_ffn = norm_back(grad_n2, h1, scale_two, gain_ffn)
        grad_h1 = grad_h1 + grad_rows
        grad_h1_low = grad_h1.astype(BF)
        grad_mixed = lax.all_to_all(
            dot_nt(w_out_all, grad_h1_low).astype(BF), "mp", 0, 1, tiled=True
        )
        grad_out = dot(mixed_rows, grad_h1_low).astype(BF)
        grad_out = grad_out.reshape(parts, 2, extra, width).transpose(1, 0, 2, 3)
        sums = lax.dynamic_update_slice(sums, grad_out, (0, 0, hidden, 0))
        early = jnp.stack([jnp.sum(grad_rows, 0), grad_gain_ffn, jnp.sum(grad_h1, 0)])
    def unpack_all(own):
        sibling = lax.ppermute(own, "core", [(0, 1), (1, 0)])
        up, down = unpack(core.reshape(1), own, sibling, hidden)
        first, second = own[hidden:].astype(F32), sibling[hidden:].astype(F32)
        out = jnp.where(
            core == 0, jnp.concatenate([first, second]), jnp.concatenate([second, first])
        )
        return up, down, out

    part = lax.psum_scatter(
        sums.reshape((2 * parts,) + sums.shape[2:]), ("core", "mp"), scatter_dimension=0, tiled=True
    )[0]
    summed = lax.psum(part, "dpo")
    if paired:
        near = (q_near, k_near, v_near, grad_near, mixed_near, log_near) + tables_near
        far = (q_far, k_far, v_far, grad_far, mixed_far, log_far) + tables_far
        heads = each // HEAD_DIM
        back = functools.partial(half_back, ends=ends, rank=index)
        both = (near, far)
        middle_head = heads // 2
        opening = back("back_near0", sides=(near,), first=0, count=middle_head, finish=False)[0]
        written, at = (), 0
        quarter = middle_head // 4
        for i, count in enumerate((middle_head - quarter, quarter)):
            written = back(
                f"back_first{i}", sides=both, first=at, count=count, finish=True,
                partial=opening, written=written, after=part if i else None,
            )
            at += count
        back_far, back_near = written
        back_far, partial = back(
            "back_second", sides=both, first=at, count=heads - at, finish=False,
            written=(back_far, None),
        )
        back_far = back_far.reshape(3 * each, rows)
        grad_far_rows = dot_tn(back_far, w_turned).astype(BF)
        sent = across(grad_far_rows)
        back_near = back(
            "back_near1", sides=(near,), first=middle_head, count=heads - middle_head, finish=True,
            partial=partial, written=(back_near,), after=grad_far_rows,
        )[0].reshape(3 * each, rows)
        pairs = [(n1, back_near, 0), (n1_far, back_far, 0)]
        grad_qkv, summed = project_back(pairs, summed)
        output = result(h1, branch, valid_here, b_down, grad_qkv)
        grad_h0_low, late = leave(
            back_near, w_turned, sent, h0, grad_h1, gain_attn, (output,)
        )
    else:
        back = attend_back(ends, query, keys, values, grad_mixed, mixed, logsum, cosine, sine)
        grad_n1 = dot_tn(back, w_turned).astype(BF)
        grad_n1 = lax.psum_scatter(grad_n1, "mp", scatter_dimension=0, tiled=True).astype(F32)
        grad_qkv, summed = project_back([(n1_all, back, 0)], summed)
        grad_h0, grad_gain_attn = norm_back(grad_n1, h0, scale_one, gain_attn)
        grad_h0_low = (grad_h0 + grad_h1).astype(BF)
        late = jnp.stack([jnp.sum(grad_h0_low.astype(F32), axis=0), grad_gain_attn])
    grad_up, grad_down, grad_out = unpack_all(summed)
    grad_w_concat = concat_back(inputs, skip_in, grad_h0_low)
    small = jnp.concatenate([early, late, grad_bias.reshape(-1, width)])
    small = jnp.pad(small, ((0, -small.shape[0] % 8), (0, 0)))
    if paired and lax.axis_size("dpo") == 8:
        tail, small = sum_all(grad_w_concat, small)
        grad_qkv = lax.psum(grad_qkv, dp)
    else:
        tail, small = lax.psum((grad_w_concat, small), dp + ("mp",))
        grad_qkv = lax.psum(grad_qkv, dp)
    grad_inputs, grad_skip = join_back(grad_h0_low, w_concat)
    grad_query, grad_key, grad_value = turn(grad_qkv, 3)
    return (
        output,
        grad_inputs,
        grad_skip,
        tail.astype(F32),
        small[3],
        small[4],
        grad_query,
        grad_key,
        grad_value,
        grad_out,
        small[2],
        small[1],
        grad_up,
        piece(small[5 : 5 + parts * hidden // width].reshape(-1), rank, hidden),
        grad_down,
        small[0],
    )


def solution(mesh):
    dp, mp = mesh.shape["dp"], mesh.shape["mp"]
    mesh = Mesh(mesh.devices.reshape(dp // 2, 2, mp), ("dpo", "core", "mp"))
    rows = P(("dpo", "core", "mp"), None)
    columns = P(None, "mp")
    upright = P("mp", None)
    return jax.shard_map(
        body,
        mesh=mesh,
        in_specs=(
            rows, rows, rows, P(("dpo", "core"), None), P(), P(), P(), columns, columns, columns,
            upright, P(), P(), columns, P("mp"), upright, P(),
        ),
        out_specs=(
            rows, rows, rows, P(), P(), P(), columns, columns, columns,
            upright, P(), P(), columns, P("mp"), upright, P(),
        ),
        check_vma=False,
    )
```

```python
import functools

import jax
import jax.numpy as jnp
from jax import lax
from jax.experimental import pallas as pl
from jax.experimental.pallas import tpu as pltpu
from jax.sharding import Mesh
from jax.sharding import PartitionSpec as P

HEAD_DIM = 64
HALF = HEAD_DIM // 2
EPS = 1e-06
FIRST_LEAST = 3712
FIRST_MOST = 3840
SEGS = 16
LOG2E = 1.4426950408889634
LN2 = 0.6931471805599453
VMEM = 60 * 2**20

BF = jnp.bfloat16
F32 = jnp.float32


def dot(left, right, dims=((1,), (0,))):
    return lax.dot_general(left, right, (dims, ((), ())), preferred_element_type=F32)


def dot_tn(left, right):
    return dot(left, right, ((0,), (0,)))


def dot_nt(left, right):
    return dot(left, right, ((1,), (1,)))


def layout(lengths_row, count):
    ends = jnp.cumsum(lengths_row)
    starts = ends - lengths_row
    places = jnp.arange(count, dtype=jnp.int32)
    seg = jnp.sum((places[:, None] >= ends[None, :]).astype(jnp.int32), axis=1)
    owner = seg[:, None] == jnp.arange(lengths_row.shape[0], dtype=jnp.int32)[None, :]
    start_of = jnp.sum(jnp.where(owner, starts[None, :], 0), axis=1)
    pos = (places - start_of).astype(F32)
    valid = (places < ends[-1]).astype(F32)
    return (ends.astype(jnp.int32), pos, valid)


def tables(pos):
    freq = jnp.exp(-jnp.log(10000.0) * jnp.arange(HALF, dtype=F32) * 2.0 / HEAD_DIM)
    angle = freq[:, None] * pos[None, :]
    return (jnp.cos(angle), jnp.sin(angle))


def norm_back(grad, stream, scale, gain):
    tilted = grad * gain
    grad_gain = jnp.sum(grad * stream * scale, axis=0)
    grad_stream = scale * tilted - stream * scale**3 * jnp.mean(
        tilted * stream, axis=-1, keepdims=True
    )
    return (grad_stream, grad_gain)


def params():
    return pltpu.CompilerParams(vmem_limit_bytes=VMEM)


def cost(flops, moved):
    return pl.CostEstimate(flops=flops // 64, bytes_accessed=moved // 64, transcendentals=0)


def project_kernel(x_ref, w_ref, cos_ref, sin_ref, *refs):
    q_ref, k_ref, v_ref = refs[-3:]
    x = x_ref[...]
    c, s = cos_ref[...], sin_ref[...]
    width = q_ref.shape[0]
    for out, first, factor in ((q_ref, 0, 0.125 * LOG2E), (k_ref, width, 1.0)):
        t = dot_nt(w_ref[first : first + width, :], x)
        for h in range(0, width, HEAD_DIM):
            a, b = t[h : h + HALF], t[h + HALF : h + HEAD_DIM]
            out[h : h + HALF, :] = ((a * c - b * s) * factor).astype(BF)
            out[h + HALF : h + HEAD_DIM, :] = ((b * c + a * s) * factor).astype(BF)
    v_ref[...] = dot_nt(w_ref[2 * width :, :], x).astype(BF)


def project(x, w, cosine, sine, after=()):
    count, depth = x.shape
    width = w.shape[0] // 3
    block = min(512, count)
    table = pl.BlockSpec((HALF, block), lambda i: (0, i))
    out = pl.BlockSpec((width, block), lambda i: (0, i))
    return pl.pallas_call(
        project_kernel,
        grid=(count // block,),
        in_specs=[
            pl.BlockSpec((block, depth), lambda i: (i, 0)),
            pl.BlockSpec(w.shape, lambda i: (0, 0)),
            table,
            table,
        ]
        + [pl.BlockSpec(memory_space=pl.ANY)] * len(after),
        out_specs=[out] * 3,
        out_shape=[jax.ShapeDtypeStruct((width, count), BF)] * 3,
        compiler_params=params(),
        name="project",
    )(x, w, cosine, sine, *after)


def scale_of(stream):
    return lax.rsqrt(jnp.mean(stream * stream, axis=-1, keepdims=True) + EPS)


def norm_back_rows(grad, stream, gain):
    scale = scale_of(stream)
    tilted = grad * gain
    back = scale * tilted - stream * (scale * scale * scale) * jnp.mean(
        tilted * stream, axis=-1, keepdims=True
    )
    return back, jnp.sum(grad * stream * scale, axis=0, keepdims=True)


def add_up(ref, terms):
    for i, term in enumerate(terms):

        @pl.when(pl.program_id(0) == 0)
        def _():
            ref[i : i + 1, :] = term

        @pl.when(pl.program_id(0) > 0)
        def _():
            ref[i : i + 1, :] += term


def row_specs(rows, width, block, first=0):
    def tall(columns=width):
        return pl.BlockSpec((block, columns), lambda i: (i + first, 0))

    def whole(*shape):
        return pl.BlockSpec(shape, lambda i: (0, 0))

    return tall, whole


def enter_kernel(x_ref, s_ref, w_ref, b_ref, gain_ref, *refs):
    h_ref, n_ref = refs[-2:]
    width = x_ref.shape[1]
    h = dot(x_ref[...], w_ref[:width, :]) + dot(s_ref[...], w_ref[width:, :]) + b_ref[...]
    h_ref[...] = h
    n_ref[...] = (h * scale_of(h) * gain_ref[...]).astype(BF)


def enter(x, skip, w, bias, gain, first, count, written=()):
    rows, width = x.shape
    block = min(512, count)
    tall, whole = row_specs(rows, width, block, first // block)
    return pl.pallas_call(
        enter_kernel,
        grid=(count // block,),
        in_specs=[tall(), tall(), whole(*w.shape), whole(1, width), whole(1, width)]
        + [pl.BlockSpec(memory_space=pl.ANY)] * len(written),
        out_specs=[tall(), tall()],
        out_shape=[jax.ShapeDtypeStruct((rows, width), F32), jax.ShapeDtypeStruct((rows, width), BF)],
        input_output_aliases={5 + i: i for i in range(len(written))},
        compiler_params=params(),
        name="enter",
        cost_estimate=cost(4 * count * width * width, 10 * count * width),
    )(x, skip, w, bias[None], gain[None], *written)


def upper_kernel(h_ref, near_ref, in_ref, own_ref, far_ref, b_ref, gain_ref, h1_ref, n_ref):
    h = h_ref[...] + dot_tn(near_ref[...], own_ref[...]) + dot_tn(in_ref[...], far_ref[...])
    h = h + b_ref[...]
    h1_ref[...] = h
    n_ref[...] = (h * scale_of(h) * gain_ref[...]).astype(BF)


def upper(h0, near, arrived, own, far, bias, gain):
    rows, width = h0.shape
    block = min(512, rows)
    tall, whole = row_specs(rows, width, block)
    flat = pl.BlockSpec((near.shape[0], block), lambda i: (0, i))
    return pl.pallas_call(
        upper_kernel,
        grid=(rows // block,),
        in_specs=[
            tall(), flat, flat, whole(*own.shape), whole(*far.shape), whole(1, width), whole(1, width)
        ],
        out_specs=[tall(), tall()],
        out_shape=[jax.ShapeDtypeStruct((rows, width), F32), jax.ShapeDtypeStruct((rows, width), BF)],
        compiler_params=params(),
        name="upper",
        cost_estimate=cost(2 * rows * width * width, 12 * rows * width),
    )(h0, near, arrived, own, far, bias[None], gain[None])


def middle_kernel(
    h_ref, dn_ref, g_ref, valid_ref, gain_ref, own_ref, far_ref,
    dh_ref, low_ref, near_ref, sent_ref, sums_ref,
):
    valid = valid_ref[...]
    h = h_ref[...]
    g = g_ref[...].astype(F32) * valid
    back, gain_sum = norm_back_rows(dn_ref[...], h, gain_ref[...])
    dh = g + back
    dh_ref[...] = dh
    low = dh.astype(BF)
    low_ref[...] = low
    near_ref[...] = dot_nt(own_ref[...], low).astype(BF)
    sent_ref[...] = dot_nt(far_ref[...], low).astype(BF)
    add_up(
        sums_ref,
        [jnp.sum(g, 0, keepdims=True), gain_sum, jnp.sum(dh, 0, keepdims=True)],
    )


def middle(h1, dn, cotangent, valid, gain, own, far):
    rows, width = h1.shape
    block = min(512, rows)
    tall, whole = row_specs(rows, width, block)
    flat = pl.BlockSpec((own.shape[0], block), lambda i: (0, i))
    return pl.pallas_call(
        middle_kernel,
        grid=(rows // block,),
        in_specs=[tall(), tall(), tall(), tall(1), whole(1, width)] + [whole(*own.shape)] * 2,
        out_specs=[tall(), tall(), flat, flat, whole(3, width)],
        out_shape=[
            jax.ShapeDtypeStruct((rows, width), F32),
            jax.ShapeDtypeStruct((rows, width), BF),
            jax.ShapeDtypeStruct((own.shape[0], rows), BF),
            jax.ShapeDtypeStruct((own.shape[0], rows), BF),
            jax.ShapeDtypeStruct((3, width), F32),
        ],
        compiler_params=params(),
        name="middle",
        cost_estimate=cost(2 * rows * width * width, 24 * rows * width),
    )(h1, dn, cotangent, valid, gain[None], own, far)


def result_kernel(h_ref, branch_ref, valid_ref, bias_ref, after_ref, out_ref):
    out_ref[...] = valid_ref[...] * (h_ref[...] + branch_ref[...] + bias_ref[...])


def result(h1, branch, valid, bias, after):
    rows, width = h1.shape
    block = min(512, rows)
    tall, whole = row_specs(rows, width, block)
    return pl.pallas_call(
        result_kernel,
        grid=(rows // block,),
        in_specs=[
            tall(), tall(), tall(1), whole(1, width), pl.BlockSpec(memory_space=pl.ANY)
        ],
        out_specs=tall(),
        out_shape=jax.ShapeDtypeStruct((rows, width), F32),
        compiler_params=params(),
        name="result",
        cost_estimate=cost(rows * width, 12 * rows * width),
    )(h1, branch, valid, bias[None], after)


def leave_kernel(back_ref, w_ref, sent_ref, h_ref, dh_ref, gain_ref, *refs):
    low_ref, sums_ref = refs[-2:]
    grad = dot_tn(back_ref[...], w_ref[...]) + sent_ref[...].astype(F32)
    back, gain_sum = norm_back_rows(grad, h_ref[...], gain_ref[...])
    low = (back + dh_ref[...]).astype(BF)
    low_ref[...] = low
    add_up(sums_ref, [jnp.sum(low.astype(F32), 0, keepdims=True), gain_sum])


def leave(back, w, sent, h0, dh1, gain, after):
    rows, width = h0.shape
    block = min(512, rows)
    tall, whole = row_specs(rows, width, block)
    return pl.pallas_call(
        leave_kernel,
        grid=(rows // block,),
        in_specs=[
            pl.BlockSpec((back.shape[0], block), lambda i: (0, i)),
            whole(*w.shape),
            tall(),
            tall(),
            tall(),
            whole(1, width),
        ]
        + [pl.BlockSpec(memory_space=pl.ANY)] * len(after),
        out_specs=[tall(), whole(2, width)],
        out_shape=[
            jax.ShapeDtypeStruct((rows, width), BF),
            jax.ShapeDtypeStruct((2, width), F32),
        ],
        compiler_params=params(),
        name="leave",
        cost_estimate=cost(2 * rows * width * back.shape[0], 16 * rows * width),
    )(back, w, sent, h0, dh1, gain[None], *after)


def segments(ends_ref, first, count):
    pos = lax.broadcasted_iota(jnp.int32, (1, count), 1) + first
    seg = jnp.zeros((1, count), jnp.int32)
    for i in range(ends_ref.shape[0]):
        seg = seg + (pos >= ends_ref[i]).astype(jnp.int32)
    return lax.broadcasted_iota(jnp.int32, (SEGS, 1), 0) == seg


def zeros(rows, count):
    return jnp.zeros((rows, count), F32)


def key_pieces(count):
    if count == 4096:
        main = [(k0, 384) for k0 in range(0, FIRST_MOST, 384)]
        whole = [(k0, 1024) for k0 in range(0, count, 1024)]
        return [
            (0, 2048, main),
            (2048, 1536, main),
            (3584, 256, whole),
            (FIRST_MOST, 256, [(FIRST_LEAST, count - FIRST_LEAST)]),
        ]
    step = min(512, count)
    every = [(k0, step) for k0 in range(0, count, step)]
    return [(q0, step, every) for q0 in range(0, count, step)]


def attend_kernel(cut, ends_ref, part_ref, q_ref, k_ref, v_ref, o_ref, l_ref, kaug, qaug, vaug):
    count = k_ref.shape[1]
    here = q_ref.shape[1]
    part = part_ref[0]
    same = segments(ends_ref, 0, count)
    kaug[...] = (
        jnp.concatenate([k_ref[...].astype(F32), jnp.where(same, 0.0, -1e30), zeros(48, count)], 0)
        .T.astype(BF)
    )
    mine = segments(ends_ref, part * here, here)
    qaug[...] = jnp.concatenate(
        [q_ref[...].astype(F32), jnp.where(mine, 1.0, 0.0), zeros(48, here)], 0
    ).astype(BF)
    first = lax.broadcasted_iota(jnp.int32, (SEGS, count), 0) == 0
    vaug[...] = jnp.concatenate([v_ref[...].astype(F32), jnp.where(first, 1.0, 0.0)], 0).astype(BF)

    def block(q0, width, pieces):
        queries = qaug[:, q0 : q0 + width]
        top = jnp.full((1, width), -jnp.inf, F32)
        acc = jnp.zeros((HEAD_DIM + SEGS, width), F32)
        for k0, n in pieces:
            scores = dot(kaug[k0 : k0 + n, :], queries)
            higher = jnp.maximum(top, jnp.max(scores, axis=0, keepdims=True))
            probs = jnp.exp2(scores - higher).astype(BF)
            acc = acc * jnp.exp2(top - higher) + dot(vaug[:, k0 : k0 + n], probs)
            top = higher
        total = acc[HEAD_DIM : HEAD_DIM + 1]
        o_ref[:, q0 : q0 + width] = (acc[:HEAD_DIM] / total).astype(BF)
        l_ref[0, :, q0 : q0 + width] = top + jnp.log2(total)

    pieces = key_pieces(count)
    for p in range(cut):
        low, high = p * here, (p + 1) * here

        @pl.when(part == p)
        def _():
            for q0, width, keys in pieces:
                if low <= q0 < high:
                    block(q0 - low, width, keys)


def attend(ends, part, query, keys, values, cut):
    rows, count = query.shape
    heads = rows // HEAD_DIM
    here = count // cut
    whole = pl.BlockSpec((HEAD_DIM, count), lambda h, e, p: (h, 0))
    return pl.pallas_call(
        functools.partial(attend_kernel, cut),
        grid_spec=pltpu.PrefetchScalarGridSpec(
            num_scalar_prefetch=2,
            grid=(heads,),
            in_specs=[
                pl.BlockSpec((HEAD_DIM, here), lambda h, e, p: (h, p[0])),
                whole,
                whole,
            ],
            out_specs=[
                pl.BlockSpec((HEAD_DIM, here), lambda h, e, p: (h, 0)),
                pl.BlockSpec((1, 1, here), lambda h, e, p: (h, 0, 0)),
            ],
            scratch_shapes=[
                pltpu.VMEM((count, 128), BF),
                pltpu.VMEM((128, here), BF),
                pltpu.VMEM((HEAD_DIM + SEGS, count), BF),
            ],
        ),
        out_shape=[
            jax.ShapeDtypeStruct((rows, here), BF),
            jax.ShapeDtypeStruct((heads, 1, here), F32),
        ],
        compiler_params=params(),
        name="attend",
        cost_estimate=cost(4 * rows * here * count, 8 * rows * count),
    )(ends, part, query, keys, values)


def local_segments(ends_ref, part, count):
    return segments(ends_ref, part * count, count)


def spans(first, last, step):
    return [(k0, min(step, last - k0)) for k0 in range(first, last, step)]


def regions(query_part, key_parts, half):
    edge, start = FIRST_MOST - half, FIRST_LEAST - half

    def keys(first, last, p):
        return [(p, k0, n) for k0, n in spans(first, last, 1024)]

    if query_part == 0:
        found = []
        for p in key_parts:
            found += keys(0, half, 0) if p == 0 else keys(0, edge, 1)
        return [(0, half, found)]
    low = edge - 256
    if list(key_parts) == [0]:
        return [(0, edge, keys(0, half, 0)), (edge, half - edge, [])]
    main, mixed, last = [], [], []
    for p in key_parts:
        if p == 0:
            main += keys(0, half, 0)
            mixed += keys(0, half, 0)
        else:
            main += keys(0, edge, 1)
            mixed += keys(0, half, 1)
            last += [(1, start, half - start)]
    return [(0, low, main), (low, 256, mixed), (edge, half - edge, last)]


def half_kernel(query_far, key_sides, given, last, ends_ref, part_ref, *refs):
    refs = list(refs)
    q_ref = refs.pop(0)
    kv = {side: (refs.pop(0), refs.pop(0)) for side in key_sides}
    acc_in, top_in = (refs.pop(0), refs.pop(0)) if given else (None, None)
    out_ref, top_ref = refs.pop(0), refs.pop(0)
    qaug = refs.pop(0)
    kaug = {side: refs.pop(0) for side in key_sides}
    vaug = {side: refs.pop(0) for side in key_sides}
    half = q_ref.shape[1]
    rank = part_ref[0]

    @pl.when(pl.program_id(0) == 0)
    def _():
        for side in key_sides:
            same = local_segments(ends_ref, rank if side == 0 else 1 - rank, half)
            blank = zeros(HEAD_DIM, half)
            kaug[side][...] = (
                jnp.concatenate([blank, jnp.where(same, 0.0, -1e30), zeros(48, half)], 0)
                .T.astype(BF)
            )
            first = lax.broadcasted_iota(jnp.int32, (SEGS, half), 0) == 0
            vaug[side][HEAD_DIM:, :] = jnp.where(first, 1.0, 0.0).astype(BF)
        mine = local_segments(ends_ref, 1 - rank if query_far else rank, half)
        qaug[HEAD_DIM:, :] = jnp.concatenate(
            [jnp.where(mine, 1.0, 0.0), zeros(48, half)], 0
        ).astype(BF)

    for side in key_sides:
        kaug[side][:, :HEAD_DIM] = kv[side][0][...].T
        vaug[side][:HEAD_DIM, :] = kv[side][1][...]
    qaug[:HEAD_DIM, :] = q_ref[...]

    for here in range(2):
        query_part = 1 - here if query_far else here
        part_of = {side: here if side == 0 else 1 - here for side in key_sides}
        side_of = {p: side for side, p in part_of.items()}

        @pl.when(rank == here)
        def _():
            for q0, width, pieces in regions(query_part, list(side_of), half):
                there = slice(q0, q0 + width)
                queries = qaug[:, there]
                if given:
                    top, acc = top_in[0, :, there], acc_in[0, :, there]
                else:
                    top = jnp.full((1, width), -jnp.inf, F32)
                    acc = jnp.zeros((HEAD_DIM + SEGS, width), F32)
                for p, k0, n in pieces:
                    side = side_of[p]
                    scores = dot(kaug[side][k0 : k0 + n, :], queries)
                    higher = jnp.maximum(top, jnp.max(scores, axis=0, keepdims=True))
                    probs = jnp.exp2(scores - higher).astype(BF)
                    acc = acc * jnp.exp2(top - higher) + dot(vaug[side][:, k0 : k0 + n], probs)
                    top = higher
                if last:
                    total = acc[HEAD_DIM : HEAD_DIM + 1]
                    out_ref[:, there] = (acc[:HEAD_DIM] / total).astype(BF)
                    top_ref[0, :, there] = top + jnp.log2(total)
                else:
                    out_ref[0, :, there] = acc
                    top_ref[0, :, there] = top


def attend_half(name, ends, rank, query, query_far, keys, carry=None, last=True):
    rows, half = query.shape
    heads = rows // HEAD_DIM
    sides = sorted(keys)
    head = pl.BlockSpec((HEAD_DIM, half), lambda h, e, r: (h, 0))
    tall = pl.BlockSpec((1, HEAD_DIM + SEGS, half), lambda h, e, r: (h, 0, 0))
    line = pl.BlockSpec((1, 1, half), lambda h, e, r: (h, 0, 0))
    operands = [query]
    for side in sides:
        operands += list(keys[side])
    specs = [head] * len(operands)
    if carry is not None:
        operands += list(carry)
        specs += [tall, line]
    return pl.pallas_call(
        functools.partial(half_kernel, query_far, sides, carry is not None, last),
        grid_spec=pltpu.PrefetchScalarGridSpec(
            num_scalar_prefetch=2,
            grid=(heads,),
            in_specs=specs,
            out_specs=[head if last else tall, line],
            scratch_shapes=[pltpu.VMEM((128, half), BF)]
            + [pltpu.VMEM((half, 128), BF)] * len(sides)
            + [pltpu.VMEM((HEAD_DIM + SEGS, half), BF)] * len(sides),
        ),
        out_shape=[
            jax.ShapeDtypeStruct((rows, half), BF)
            if last
            else jax.ShapeDtypeStruct((heads, HEAD_DIM + SEGS, half), F32),
            jax.ShapeDtypeStruct((heads, 1, half), F32),
        ],
        compiler_params=params(),
        name=name,
        cost_estimate=cost(16 * rows * half * half * len(sides), 8 * rows * half),
    )(ends, rank, *operands)


def split3(x):
    a = x.astype(BF).astype(F32)
    b = (x - a).astype(BF).astype(F32)
    row = lax.broadcasted_iota(jnp.int32, (SEGS, 1), 0)
    return jnp.where(row == 0, a, jnp.where(row == 1, b, jnp.where(row == 2, x - a - b, 0.0)))


def attend_back_kernel(
    ends_ref, q_ref, k_ref, v_ref, g_ref, o_ref, l_ref, cos_ref, sin_ref, d_ref,
    kaug, vaug, qaug, gaug, pair, dq,
):
    count = k_ref.shape[1]
    same = segments(ends_ref, 0, count)
    row = lax.broadcasted_iota(jnp.int32, (SEGS, count), 0)
    shift = jnp.where(row < 3, 1.0, 0.0)
    g = g_ref[...].astype(F32)
    q = q_ref[...].astype(F32)
    delta = jnp.sum(g * o_ref[...].astype(F32), axis=0, keepdims=True)
    kaug[...] = (
        jnp.concatenate(
            [k_ref[...].astype(F32), jnp.where(same, 0.0, -1e30), shift, zeros(32, count)], 0
        )
        .T.astype(BF)
    )
    vaug[...] = (
        jnp.concatenate([v_ref[...].astype(F32), shift, zeros(48, count)], 0).T.astype(BF)
    )
    qaug[...] = jnp.concatenate(
        [q, jnp.where(same, 1.0, 0.0), split3(-l_ref[0]), zeros(32, count)], 0
    ).astype(BF)
    gaug[...] = jnp.concatenate([g, split3(-delta), zeros(48, count)], 0).astype(BF)
    pair[...] = jnp.concatenate([q, g], 0).T.astype(BF)
    dq[...] = jnp.zeros_like(dq)

    def turn(grad, c, s, factor):
        a, b = grad[:HALF], grad[HALF:]
        return (
            jnp.concatenate([a * c + b * s, b * c - a * s], 0) * factor
        ).astype(BF)

    def chunk(k0, n, queries):
        where = pl.ds(k0, n)
        kb, vb, kt = kaug[where, :], vaug[where, :], k_ref[:, where]
        dk = jnp.zeros((n, HEAD_DIM), F32)
        dv = jnp.zeros((n, HEAD_DIM), F32)
        for q0, width in queries:
            there = slice(q0, q0 + width)
            probs = jnp.exp2(dot(kb, qaug[:, there]))
            tilt = (probs * dot(vb, gaug[:, there])).astype(BF)
            dv = dv + dot(probs.astype(BF), pair[there, HEAD_DIM:])
            dk = dk + dot(tilt, pair[there, :HEAD_DIM])
            dq[:, there] += dot(kt, tilt)
        c, s = cos_ref[:, where], sin_ref[:, where]
        d_ref[1, 0, :, where] = turn(dk.T, c, s, LN2)
        d_ref[2, 0, :, where] = dv.T.astype(BF)

    if count == 4096:
        main = [(q0, 1920) for q0 in range(0, FIRST_MOST, 1920)]

        def step(i, carry):
            chunk(pl.multiple_of(i * 512, 512), 512, main)
            return carry

        lax.fori_loop(0, 7, step, 0)
        chunk(3584, 256, [(q0, 1024) for q0 in range(0, count, 1024)])
        chunk(FIRST_MOST, count - FIRST_MOST, [(3584, 512)])
    else:
        size = min(512, count)

        def step(i, carry):
            chunk(pl.multiple_of(i * size, size), size, [(q, size) for q in range(0, count, size)])
            return carry

        lax.fori_loop(0, count // size, step, 0)
    d_ref[0, 0] = turn(dq[...], cos_ref[...], sin_ref[...], 0.125)


def attend_back(ends, query, keys, values, grad, mixed, logsum, cosine, sine):
    rows, count = query.shape
    heads = rows // HEAD_DIM
    whole = pl.BlockSpec((HEAD_DIM, count), lambda h, e: (h, 0))
    table = pl.BlockSpec((HALF, count), lambda h, e: (0, 0))
    out = pl.pallas_call(
        attend_back_kernel,
        grid_spec=pltpu.PrefetchScalarGridSpec(
            num_scalar_prefetch=1,
            grid=(heads,),
            in_specs=[whole] * 5
            + [pl.BlockSpec((1, 1, count), lambda h, e: (h, 0, 0)), table, table],
            out_specs=pl.BlockSpec((3, 1, HEAD_DIM, count), lambda h, e: (0, h, 0, 0)),
            scratch_shapes=[
                pltpu.VMEM((count, 128), BF),
                pltpu.VMEM((count, 128), BF),
                pltpu.VMEM((128, count), BF),
                pltpu.VMEM((128, count), BF),
                pltpu.VMEM((count, 128), BF),
                pltpu.VMEM((HEAD_DIM, count), F32),
            ],
        ),
        out_shape=jax.ShapeDtypeStruct((3, heads, HEAD_DIM, count), BF),
        compiler_params=params(),
        name="attend_back",
        cost_estimate=cost(10 * rows * count * count, 16 * rows * count),
    )(ends, query, keys, values, grad, mixed, logsum, cosine, sine)
    return out.reshape(3 * rows, count)


def turn_back(grad, c, s, factor):
    a, b = grad[:HALF], grad[HALF:]
    return (jnp.concatenate([a * c + b * s, b * c - a * s], 0) * factor).astype(BF)


def back_chunks(key_part, query_parts, half):
    edge = FIRST_MOST - half
    low = edge - 256
    found = []
    if key_part == 0:
        queries = []
        for p in query_parts:
            queries += [(p, 0, half if p == 0 else edge)]
        return [(0, half, 512, queries)]
    main = [(p, 0, half if p == 0 else edge) for p in query_parts]
    found.append((0, low, 512, main))
    found.append((low, 256, 256, [(p, 0, half) for p in query_parts]))
    if 1 in query_parts:
        found.append((edge, half - edge, 256, [(1, low, half - low)]))
    return found


def half_back_kernel(near_only, given_partial, finish, ends_ref, part_ref, *refs):
    refs = list(refs)
    sides = (0,) if near_only else (0, 1)
    given = {side: [refs.pop(0) for _ in range(8)] for side in sides}
    partial_in = refs.pop(0) if given_partial else None
    while len(refs) > (1 if near_only else 2) + 7:
        refs.pop(0)
    out_ref = None if near_only else refs.pop(0)
    near_ref = refs.pop(0)
    kaug, vaug, qaug, gaug, pair, dq, sums = refs
    rank = part_ref[0]
    half = given[0][0].shape[1]

    @pl.when(pl.program_id(0) == 0)
    def _():
        row = lax.broadcasted_iota(jnp.int32, (SEGS, half), 0)
        shift = jnp.where(row < 3, 1.0, 0.0)
        blank = zeros(HEAD_DIM, half)
        for side in sides:
            there = slice(side * half, side * half + half)
            same = local_segments(ends_ref, rank if side == 0 else 1 - rank, half)
            kaug[there, :] = (
                jnp.concatenate([blank, jnp.where(same, 0.0, -1e30), shift, zeros(32, half)], 0)
                .T.astype(BF)
            )
            vaug[there, :] = jnp.concatenate([blank, shift, zeros(48, half)], 0).T.astype(BF)
            qaug[HEAD_DIM:, there] = jnp.concatenate(
                [jnp.where(same, 1.0, 0.0), zeros(48, half)], 0
            ).astype(BF)
            gaug[HEAD_DIM:, there] = blank.astype(BF)

    for side in sides:
        q_ref, k_ref, v_ref, g_ref, o_ref, l_ref = given[side][:6]
        there = slice(side * half, side * half + half)
        g = g_ref[...]
        q = q_ref[...]
        delta = jnp.sum(g.astype(F32) * o_ref[...].astype(F32), axis=0, keepdims=True)
        kaug[there, :HEAD_DIM] = k_ref[...].T
        vaug[there, :HEAD_DIM] = v_ref[...].T
        qaug[:HEAD_DIM, there] = q
        qaug[HEAD_DIM + SEGS : HEAD_DIM + 2 * SEGS, there] = split3(-l_ref[0]).astype(BF)
        gaug[:HEAD_DIM, there] = g
        gaug[HEAD_DIM : HEAD_DIM + SEGS, there] = split3(-delta).astype(BF)
        pair[there, :] = jnp.concatenate([q, g], 0).T
    dq[...] = jnp.zeros_like(dq)
    if given_partial:
        dq[:, :half] = partial_in[0, 0]
        sums[...] = partial_in[1:, 0]
    else:
        sums[...] = jnp.zeros_like(sums)

    def chunk(side, k0, n, queries):
        where = pl.ds(side * half + k0, n)
        kb, vb, kt = kaug[where, :], vaug[where, :], given[side][1][:, pl.ds(k0, n)]
        dk = jnp.zeros((n, HEAD_DIM), F32)
        dv = jnp.zeros((n, HEAD_DIM), F32)
        for q0, width in queries:
            there = slice(q0, q0 + width)
            probs = jnp.exp2(dot(kb, qaug[:, there]))
            tilt = (probs * dot(vb, gaug[:, there])).astype(BF)
            dv = dv + dot(probs.astype(BF), pair[there, HEAD_DIM:])
            dk = dk + dot(tilt, pair[there, :HEAD_DIM])
            dq[:, there] += dot(kt, tilt)
        dk, dv = dk.T, dv.T
        if side == 0:
            sums[0, :, pl.ds(k0, n)] += dk
            sums[1, :, pl.ds(k0, n)] += dv
            return
        c, s = given[side][6][:, pl.ds(k0, n)], given[side][7][:, pl.ds(k0, n)]
        out_ref[1, 0, :, pl.ds(k0, n)] = turn_back(dk, c, s, LN2)
        out_ref[2, 0, :, pl.ds(k0, n)] = dv.astype(BF)

    for here in range(2):

        @pl.when(rank == here)
        def _():
            side_of = {here: 0, 1 - here: 1}
            for key_part, side in side_of.items():
                if near_only and side == 1:
                    continue
                if near_only:
                    query_parts = [here]
                else:
                    query_parts = [0, 1] if side == 1 else [1 - here]
                for k0, total, n, queries in back_chunks(key_part, query_parts, half):
                    spread = [(side_of[p] * half + q0, width) for p, q0, width in queries]
                    if total == n:
                        chunk(side, k0, n, spread)
                        continue

                    def step(i, carry):
                        chunk(side, pl.multiple_of(k0 + i * n, n), n, spread)
                        return carry

                    lax.fori_loop(0, total // n, step, 0)

    if not near_only:
        out_ref[0, 0] = turn_back(dq[:, half:], given[1][6][...], given[1][7][...], 0.125)
    if finish:
        c, s = given[0][6][...], given[0][7][...]
        near_ref[0, 0] = turn_back(dq[:, :half], c, s, 0.125)
        near_ref[1, 0] = turn_back(sums[0], c, s, LN2)
        near_ref[2, 0] = sums[1].astype(BF)
    else:
        near_ref[0, 0] = dq[:, :half]
        near_ref[1:, 0] = sums[...]


def half_back(name, ends, rank, sides, first, count, finish, partial=None, written=(), after=None):
    rows, half = sides[0][0].shape
    heads = rows // HEAD_DIM
    near_only = len(sides) == 1
    head = pl.BlockSpec((HEAD_DIM, half), lambda h, e, r: (h + first, 0))
    line = pl.BlockSpec((1, 1, half), lambda h, e, r: (h + first, 0, 0))
    table = pl.BlockSpec((HALF, half), lambda h, e, r: (0, 0))
    block = pl.BlockSpec((3, 1, HEAD_DIM, half), lambda h, e, r: (0, h + first, 0, 0))
    anywhere = pl.BlockSpec(memory_space=pl.ANY)
    operands, specs = [], []
    for side in sides:
        operands += list(side)
        specs += [head] * 5 + [line, table, table]
    result = jax.ShapeDtypeStruct((3, heads, HEAD_DIM, half), BF)
    if partial is not None:
        operands.append(partial)
        specs.append(block)
    aliases = {}
    for i, array in enumerate(written):
        if array is not None:
            aliases[2 + len(operands)] = i
            operands.append(array)
            specs.append(anywhere)
    if after is not None:
        operands.append(after)
        specs.append(anywhere)
    near_result = result if finish else jax.ShapeDtypeStruct(result.shape, F32)
    out_shape = [near_result] if near_only else [result, near_result]
    out_specs = [block] * len(out_shape)
    wide = half * len(sides)
    return pl.pallas_call(
        functools.partial(half_back_kernel, near_only, partial is not None, finish),
        grid_spec=pltpu.PrefetchScalarGridSpec(
            num_scalar_prefetch=2,
            grid=(count,),
            in_specs=specs,
            out_specs=out_specs,
            scratch_shapes=[
                pltpu.VMEM((wide, 128), BF),
                pltpu.VMEM((wide, 128), BF),
                pltpu.VMEM((128, wide), BF),
                pltpu.VMEM((128, wide), BF),
                pltpu.VMEM((wide, 128), BF),
                pltpu.VMEM((HEAD_DIM, wide), F32),
                pltpu.VMEM((2, HEAD_DIM, half), F32),
            ],
        ),
        out_shape=out_shape,
        input_output_aliases=aliases,
        compiler_params=params(),
        name=name,
        cost_estimate=cost(40 * count * HEAD_DIM * half * half * (1 if near_only else 3), 40 * count * HEAD_DIM * half),
    )(ends, rank, *operands)


def ffn_kernel(step, given, src_ref, dst_ref, n_ref, g_ref, up_ref, bias_ref, down_ref, *refs):
    branch_in, dn_in = refs[:2] if given else (None, None)
    branch_ref, dn_ref, dw_ref, dbias_ref, branch, dn, sems = refs[3 if given else 0 :]

    rows, depth = n_ref.shape
    steps = [(i, slice(r0, r0 + step)) for i, r0 in enumerate(range(0, rows, step))]
    opening = (pl.program_id(0) == 0) & (pl.program_id(1) == 0)
    closing = (pl.program_id(0) == pl.num_programs(0) - 1) & (
        pl.program_id(1) == pl.num_programs(1) - 1
    )

    def moves(i, part, out):
        if out:
            pairs = ((branch, branch_ref), (dn, dn_ref))
        else:
            pairs = ((branch_in, branch), (dn_in, dn))
        return [
            pltpu.make_async_copy(src.at[part, :], dst.at[part, :], sems.at[j, i])
            for j, (src, dst) in enumerate(pairs)
        ]

    @pl.when(opening)
    def _():
        if given:
            for i, part in steps:
                for move in moves(i, part, False):
                    move.start()
        else:
            branch[...] = jnp.zeros_like(branch)
            dn[...] = jnp.zeros_like(dn)

    up = up_ref[...].reshape(depth, -1)
    down, bias = down_ref[0, 0], bias_ref[0].astype(F32)
    width = up.shape[1]
    dup = jnp.zeros((width, depth), F32)
    ddown = jnp.zeros((width, depth), F32)
    dbias = jnp.zeros((1, width), F32)
    for i, part in steps:
        x, y = n_ref[part, :], g_ref[part, :]
        u = dot(x, up) + bias
        dz = dot_nt(y, down)
        normal = 0.5 * (1.0 + lax.erf(u * 0.7071067811865476))
        density = jnp.exp(-0.5 * u * u) * 0.3989422804014327
        z = (u * normal).astype(BF)
        du = (dz * (normal + u * density)).astype(BF)
        if given:

            @pl.when(opening)
            def _():
                for move in moves(i, part, False):
                    move.wait()

        branch[part, :] += dot(z, down)
        dn[part, :] += dot_nt(du, up)

        @pl.when(closing)
        def _():
            for move in moves(i, part, True):
                move.start()

        ddown = ddown + dot_tn(z, y)
        dup = dup + dot_tn(du, x)
        dbias = dbias + jnp.sum(du.astype(F32), axis=0, keepdims=True)
    dw_ref[0, 0, :width, :] = dup.astype(BF)
    dw_ref[0, 0, width:, :] = ddown.astype(BF)
    dbias_ref[0] = dbias

    @pl.when(closing)
    def _():
        for i, part in steps:
            for move in moves(i, part, True):
                move.wait()


def ffn_block(hidden):
    return min(512, hidden // 2)


def ffn(name, n2, grad, up, bias, down, extra, parts, src, dst, before=None):
    rows, depth = n2.shape
    hidden = up.shape[3]
    block = ffn_block(hidden)
    per = hidden // 2 // block
    step = min(512, rows)
    once = pl.BlockSpec(
        (rows, depth), lambda p, i, f, t: (0, 0), pipeline_mode=pl.Buffered(1)
    )
    anywhere = pl.BlockSpec(memory_space=pl.ANY)
    operands = [n2, grad, up, bias, down] + ([] if before is None else list(before))
    return pl.pallas_call(
        functools.partial(ffn_kernel, step, before is not None),
        grid_spec=pltpu.PrefetchScalarGridSpec(
            num_scalar_prefetch=2,
            grid=(src.shape[0], 2 * per),
            in_specs=[
                once,
                once,
                pl.BlockSpec((2, 1, depth // 2, block), lambda p, i, f, t: (0, f[p], 0, i)),
                pl.BlockSpec((1, 1, block), lambda p, i, f, t: (f[p], 0, i)),
                pl.BlockSpec(
                    (1, 1, block, depth), lambda p, i, f, t: (i // per, f[p], i % per, 0)
                ),
            ]
            + ([] if before is None else [anywhere] * 3),
            out_specs=[anywhere] * 2
            + [
                pl.BlockSpec(
                    (1, 1, 2 * block, depth), lambda p, i, f, t: (i // per, t[p], i % per, 0)
                ),
                pl.BlockSpec((1, 1, block), lambda p, i, f, t: (p, 0, i)),
            ],
            scratch_shapes=[pltpu.VMEM((rows, depth), F32)] * 2
            + [pltpu.SemaphoreType.DMA((2, rows // step))],
        ),
        out_shape=[jax.ShapeDtypeStruct((rows, depth), F32)] * 2
        + [
            jax.ShapeDtypeStruct((2, parts, hidden + extra, depth), BF),
            jax.ShapeDtypeStruct((src.shape[0], 1, hidden), F32),
        ],
        input_output_aliases={} if before is None else {9: 2},
        compiler_params=params(),
        name=name,
        cost_estimate=cost(12 * rows * depth * hidden * src.shape[0], 8 * depth * hidden * src.shape[0]),
    )(src, dst, *operands)


def out_back_kernel(part_ref, near_ref, in_ref, grad_ref, sums_ref, out_ref):
    for side, mixed_ref in enumerate((near_ref, in_ref)):

        @pl.when(pl.program_id(0) == side)
        def _():
            out_ref[0, 0] = dot(mixed_ref[...], grad_ref[...]).astype(BF)


def out_back(mixed, grad, sums, extra, parts):
    heads, rows = mixed[0].shape
    total, depth = sums.shape[2:]
    piece = pl.BlockSpec((extra, rows), lambda p, c, t: (c, 0))
    return pl.pallas_call(
        out_back_kernel,
        grid_spec=pltpu.PrefetchScalarGridSpec(
            num_scalar_prefetch=1,
            grid=(2, 2),
            in_specs=[
                piece,
                piece,
                pl.BlockSpec((rows, depth), lambda p, c, t: (0, 0)),
                pl.BlockSpec(memory_space=pl.ANY),
            ],
            out_specs=pl.BlockSpec(
                (1, 1, extra, depth), lambda p, c, t: (c, t[p], total // extra - 1, 0)
            ),
        ),
        out_shape=jax.ShapeDtypeStruct(sums.shape, BF),
        input_output_aliases={4: 0},
        compiler_params=params(),
        name="out_back",
        cost_estimate=cost(4 * rows * depth * heads, 4 * heads * depth),
    )(parts, *mixed, grad, sums)


def project_back_kernel(*refs):
    out_ref = refs[-2]
    pairs = refs[:-3]
    total = dot(pairs[1][...], pairs[0][...])
    for i in range(2, len(pairs), 2):
        total = total + dot(pairs[i + 1][...], pairs[i][...])
    out_ref[...] = total.astype(BF)


def project_back(pairs, passed):
    total = pairs[0][1].shape[0]
    depth = pairs[0][0].shape[1]
    block = total // 3
    specs, operands = [], []
    for x, grad, at in pairs:
        specs += [
            pl.BlockSpec(x.shape, lambda i: (0, 0)),
            pl.BlockSpec((block, x.shape[0]), functools.partial(lambda at, i: (i, at), at)),
        ]
        operands += [x, grad]
    return pl.pallas_call(
        project_back_kernel,
        grid=(3,),
        in_specs=specs + [pl.BlockSpec(memory_space=pl.ANY)],
        out_specs=[
            pl.BlockSpec((block, depth), lambda i: (i, 0)),
            pl.BlockSpec(memory_space=pl.ANY),
        ],
        out_shape=[
            jax.ShapeDtypeStruct((total, depth), BF),
            jax.ShapeDtypeStruct(passed.shape, passed.dtype),
        ],
        input_output_aliases={len(operands): 1},
        compiler_params=params(),
        name="project_back",
        cost_estimate=cost(4 * pairs[0][0].shape[0] * depth * total, 8 * depth * total),
    )(*operands, passed)


def turn_kernel(x_ref, *out_refs):
    for i, out_ref in enumerate(out_refs):

        @pl.when(pl.program_id(0) == i)
        def _():
            out_ref[...] = x_ref[...].astype(F32).T


def turn(x, parts):
    rows, depth = x.shape
    block = rows // parts
    return pl.pallas_call(
        turn_kernel,
        grid=(parts,),
        in_specs=[pl.BlockSpec((block, depth), lambda i: (i, 0))],
        out_specs=[pl.BlockSpec((depth, block), lambda i: (0, 0))] * parts,
        out_shape=[jax.ShapeDtypeStruct((depth, block), F32)] * parts,
        compiler_params=params(),
        name="turn",
        cost_estimate=cost(rows * depth, 6 * rows * depth),
    )(x)


MESH = pl.DeviceIdType.MESH


def sum_all_kernel(
    big_ref, small_ref, out_ref, small_out_ref,
    buf, done, core_in, first_in, second_in, z_in, small, small_in, small_z,
    local, send, recv, small_send, small_recv,
):
    o, c, m = lax.axis_index("dpo"), lax.axis_index("core"), lax.axis_index("mp")
    y, z = lax.rem(o, 2), lax.div(o, 2)
    zs = 4
    size = buf.shape[0] // 2
    half, quarter, eighth, last = size // 2, size // 4, size // 8, size // 32
    sibling = (o, 1 - c, m)
    across = (o, c, 1 - m)
    beside = (z * 2 + 1 - y, c, m)
    others = [lax.rem(z + d, zs) for d in range(1, zs)]

    def along(j):
        return (j * 2 + y, c, m)

    load = pltpu.make_async_copy(big_ref, buf, local.at[0])
    load.start()
    barrier = pltpu.get_barrier_semaphore()
    for device in [sibling, across, beside] + [along(j) for j in others]:
        pl.semaphore_signal(barrier, inc=1, device_id=device, device_id_type=MESH)
    pl.semaphore_wait(barrier, 6)
    small[0] = small_ref[...]

    main, tiny = (send, recv), (small_send, small_recv)
    started = []

    def copy(src, dst, sems, i, device):
        return pltpu.make_async_remote_copy(
            src_ref=src, dst_ref=dst, send_sem=sems[0].at[i], recv_sem=sems[1].at[i],
            device_id=device, device_id_type=MESH,
        )

    def go(src, dst, sems, i, device):
        one = copy(src, dst, sems, i, device)
        one.start()
        started.append(one)
        return one

    def rows(first, n, of=buf):
        return of.at[pl.ds(pl.multiple_of(first, last), n)]

    def add(first, n, got):
        def one(i, carry):
            there = pl.ds(pl.multiple_of(first + i * 128, last), 128)
            here = pl.ds(pl.multiple_of(i * 128, 128), 128)
            buf[there, :] = (buf[there, :].astype(F32) + got[here, :].astype(F32)).astype(BF)
            return carry

        lax.fori_loop(0, n // 128, one, 0)

    turn_of = ((m, y), (y, m))
    device_of = ((across, beside), (beside, across))
    far, near, far_next, near_next, own, theirs = [], [], [], [], [], []
    for s in range(2):
        a, b = turn_of[s]
        mine = s * size + c * half
        theirs.append(s * size + (1 - c) * half)
        far.append(mine + (1 - a) * quarter)
        near.append(mine + a * quarter)
        far_next.append(near[s] + (1 - b) * eighth)
        near_next.append(near[s] + b * eighth)
        own.append(near_next[s] + z * last)

    load.wait()
    arrivals = []
    for part in range(2):
        for s in range(2):
            a = turn_of[s][0]
            start = theirs[s] + ((1 - a) if part == 0 else a) * quarter
            i = 2 * part + s
            arrivals.append(go(rows(start, quarter), core_in.at[i], main, i, sibling))
    tiny_core = go(small.at[0], small_in.at[0], tiny, 0, sibling)
    firsts = []
    for s in range(2):
        arrivals[s].wait_recv()
        add(far[s], quarter, core_in.at[s])
        firsts.append(go(rows(far[s], quarter), first_in.at[s], main, 4 + s, device_of[s][0]))
    tiny_core.wait_recv()
    small[1] = small[0] + small_in[0]
    tiny_x = go(small.at[1], small_in.at[1], tiny, 1, across)
    for s in range(2):
        arrivals[2 + s].wait_recv()
        add(near[s], quarter, core_in.at[2 + s])
    tiny_x.wait_recv()
    small[2] = small[1] + small_in[1]
    tiny_y = go(small.at[2], small_in.at[2], tiny, 2, beside)
    seconds = []
    for s in range(2):
        firsts[s].wait_recv()
        add(near[s], quarter, first_in.at[s])
        seconds.append(go(rows(far_next[s], eighth), second_in.at[s], main, 6 + s, device_of[s][1]))
    tiny_y.wait_recv()
    small_z[z] = small[2] + small_in[2]
    for j in others:
        go(small_z.at[z], small_z.at[z], tiny, 3 + z, along(j))
    for s in range(2):
        seconds[s].wait_recv()
        add(near_next[s], eighth, second_in.at[s])
        for j in others:
            go(
                rows(near_next[s] + j * last, last), z_in.at[s, z], main, 8 + 4 * s + z, along(j)
            )

    def hand(first, n, i, device):
        there = rows(first, n, done)
        return go(there, there, main, i, device)

    for s in range(2):
        total = buf[pl.ds(pl.multiple_of(own[s], last), last), :].astype(F32)
        for j in others:
            copy(z_in.at[s, j], z_in.at[s, j], main, 8 + 4 * s + j, along(j)).wait_recv()
            total = total + z_in[s, j].astype(F32)
        done[pl.ds(pl.multiple_of(own[s], last), last), :] = total.astype(BF)
        for j in others:
            hand(own[s], last, 16 + 4 * s + z, along(j))
    back_second, back_first, cores = [], [], []
    for s in range(2):
        for j in others:
            there = rows(near_next[s] + j * last, last, done)
            copy(there, there, main, 16 + 4 * s + j, along(j)).wait_recv()
        back_second.append(hand(near_next[s], eighth, 24 + s, device_of[s][1]))
        back_first.append(hand(near_next[s], eighth, 26 + s, device_of[s][0]))
        cores.append(hand(near_next[s], eighth, 28 + s, sibling))
    back_more = []
    for s in range(2):
        back_second[s].wait_recv()
        back_more.append(hand(far_next[s], eighth, 30 + s, device_of[s][0]))
        cores.append(hand(far_next[s], eighth, 32 + s, sibling))
    for j in others:
        copy(small_z.at[j], small_z.at[j], tiny, 3 + j, along(j)).wait_recv()
    small_out_ref[...] = (small_z[0] + small_z[1]) + (small_z[2] + small_z[3])
    for s in range(2):
        back_first[s].wait_recv()
        cores.append(hand(far[s] + turn_of[s][1] * eighth, eighth, 34 + s, sibling))
    for s in range(2):
        back_more[s].wait_recv()
        cores.append(hand(far[s] + (1 - turn_of[s][1]) * eighth, eighth, 36 + s, sibling))
    for one in cores:
        one.wait_recv()
    store = pltpu.make_async_copy(done, out_ref, local.at[1])
    store.start()
    for one in started:
        one.wait_send()
    store.wait()


def sum_all(big, small):
    rows, width = big.shape
    quarter, eighth, last = rows // 8, rows // 16, rows // 64
    anywhere = pl.BlockSpec(memory_space=pl.ANY)
    whole = pl.BlockSpec(memory_space=pltpu.VMEM)
    dma = pltpu.SemaphoreType.DMA
    return pl.pallas_call(
        sum_all_kernel,
        in_specs=[anywhere, whole],
        out_specs=[anywhere, whole],
        out_shape=[
            jax.ShapeDtypeStruct(big.shape, BF),
            jax.ShapeDtypeStruct(small.shape, F32),
        ],
        scratch_shapes=[
            pltpu.VMEM((rows, width), BF),
            pltpu.VMEM((rows, width), BF),
            pltpu.VMEM((4, quarter, width), BF),
            pltpu.VMEM((2, quarter, width), BF),
            pltpu.VMEM((2, eighth, width), BF),
            pltpu.VMEM((2, 4, last, width), BF),
            pltpu.VMEM((3,) + small.shape, F32),
            pltpu.VMEM((3,) + small.shape, F32),
            pltpu.VMEM((4,) + small.shape, F32),
            dma((2,)),
            dma((38,)),
            dma((38,)),
            dma((7,)),
            dma((7,)),
        ],
        compiler_params=pltpu.CompilerParams(
            collective_id=0, has_side_effects=True, vmem_limit_bytes=VMEM
        ),
        name="sum_all",
        cost_estimate=cost(rows * width, 8 * rows * width),
    )(big, small)


def join_back_kernel(grad_ref, w_ref, sum_ref, first_ref, second_ref, wide_ref):
    wide_ref[...] = sum_ref[...].astype(F32)
    grad = grad_ref[...]
    width = first_ref.shape[1]
    first_ref[...] = dot_nt(grad, w_ref[:width, :])
    second_ref[...] = dot_nt(grad, w_ref[width:, :])


def join_back(grad, w, total):
    rows, depth = grad.shape
    width = w.shape[0] // 2
    block = min(512, rows)
    out = pl.BlockSpec((block, width), lambda i: (i, 0))
    piece = pl.BlockSpec((w.shape[0] * block // rows, depth), lambda i: (i, 0))
    return pl.pallas_call(
        join_back_kernel,
        grid=(rows // block,),
        in_specs=[
            pl.BlockSpec((block, depth), lambda i: (i, 0)),
            pl.BlockSpec(w.shape, lambda i: (0, 0)),
            piece,
        ],
        out_specs=[out, out, piece],
        out_shape=[jax.ShapeDtypeStruct((rows, width), F32)] * 2
        + [jax.ShapeDtypeStruct(w.shape, F32)],
        compiler_params=params(),
        name="join_back",
        cost_estimate=cost(rows * depth * width, 8 * rows * width),
    )(grad, w, total)


def concat_back_kernel(x_ref, s_ref, grad_ref, out_ref):
    for i, ref in enumerate((x_ref, s_ref)):

        @pl.when(pl.program_id(0) == i)
        def _():
            out_ref[...] = dot_tn(ref[...], grad_ref[...]).astype(BF)


def concat_back(x, skip, grad):
    rows, width = grad.shape
    block = min(512, width)
    per = width // block
    return pl.pallas_call(
        concat_back_kernel,
        grid=(2, per),
        in_specs=[
            pl.BlockSpec((rows, block), lambda i, j: (0, jnp.where(i == 0, j, per - 1))),
            pl.BlockSpec((rows, block), lambda i, j: (0, jnp.where(i == 0, 0, j))),
            pl.BlockSpec((rows, width), lambda i, j: (0, 0)),
        ],
        out_specs=pl.BlockSpec((block, width), lambda i, j: (i * per + j, 0)),
        out_shape=jax.ShapeDtypeStruct((2 * width, width), BF),
        compiler_params=params(),
        name="concat_back",
        cost_estimate=cost(4 * rows * width * width, 8 * rows * width),
    )(x, skip, grad)


def unpack_kernel(core_ref, own_ref, sibling_ref, up_ref, down_ref):
    mine = core_ref[0] == pl.program_id(0)
    width = down_ref.shape[0]
    block = jnp.where(mine, own_ref[...].astype(F32), sibling_ref[...].astype(F32))
    up_ref[...] = block[:width].T
    down_ref[...] = block[width:]


def unpack(core, own, sibling, hidden):
    depth = own.shape[1]
    block = ffn_block(hidden)
    per = hidden // 2 // block
    piece = pl.BlockSpec((2 * block, depth), lambda c, i, k: (i, 0))
    return pl.pallas_call(
        unpack_kernel,
        grid_spec=pltpu.PrefetchScalarGridSpec(
            num_scalar_prefetch=1,
            grid=(2, per),
            in_specs=[piece, piece],
            out_specs=[
                pl.BlockSpec((depth, block), lambda c, i, k: (0, c * per + i)),
                pl.BlockSpec((block, depth), lambda c, i, k: (c * per + i, 0)),
            ],
        ),
        out_shape=[
            jax.ShapeDtypeStruct((depth, hidden), F32),
            jax.ShapeDtypeStruct((hidden, depth), F32),
        ],
        compiler_params=params(),
        name="unpack",
        cost_estimate=cost(depth * hidden, 12 * depth * hidden),
    )(core, own, sibling)


def body(
    inputs, skip_in, cotangent, lengths, w_concat, b_concat, gain_attn, w_query, w_key, w_value,
    w_out, b_out, gain_ffn, w_up, b_up, w_down, b_down,
):
    parts = lax.axis_size("mp")
    rank = lax.axis_index("mp")
    core = lax.axis_index("core")
    dp = ("dpo", "core")
    rows, width = inputs.shape
    group = rows * parts
    paired = parts == 2 and group == 4096
    ends, pos_all, valid_all = layout(lengths[0], group)
    valid_here = lax.dynamic_slice_in_dim(valid_all, rank * rows, rows, 0)[:, None]
    each, hidden = w_out.shape[0], b_up.shape[0]
    extra = each // 2
    index = rank.reshape(1)
    other = 1 - index
    zero = jnp.zeros((1,), jnp.int32)

    def across(x):
        return lax.ppermute(x, "mp", [(0, 1), (1, 0)])

    def piece(x, i, size, axis=0):
        return lax.dynamic_slice_in_dim(x, i * size, size, axis)

    def order(near, far, axis):
        return jnp.where(
            rank == 0, jnp.concatenate([near, far], axis), jnp.concatenate([far, near], axis)
        )

    def core_half(w):
        return piece(w, core, w.shape[0] // 2)

    def gather(half):
        return lax.all_gather(half, ("core", "mp"), axis=0).reshape((2, parts) + half.shape)

    w_turned = jnp.concatenate([w_query.T, w_key.T, w_value.T], axis=0)
    grad_rows = cotangent.astype(F32) * valid_here
    grad_low = grad_rows.astype(BF)
    half_up, half_down = core_half(w_up), core_half(w_down)
    if paired:
        bias_far, out_piece = across(b_up), across(core_half(w_out))
        h0, n1 = enter(inputs, skip_in, w_concat, b_concat, gain_attn, 0, rows)
        n1, bias_far, out_piece = lax.optimization_barrier((n1, bias_far, out_piece))
        n1_far = across(n1)
        out_rest = lax.ppermute(out_piece, "core", [(0, 1), (1, 0)])
        out_far = jnp.where(
            core == 0,
            jnp.concatenate([out_piece, out_rest]),
            jnp.concatenate([out_rest, out_piece]),
        )
        tables_near = tables(piece(pos_all, rank, rows))
        bias_both = jnp.stack([bias_far, bias_far]).reshape(2, 1, hidden)
        q_near, k_near, v_near = project(
            n1, w_turned, *tables_near, after=(out_far, grad_low, bias_both, valid_here, half_down)
        )
        start = attend_half(
            "near_near", ends, index, q_near, False, {0: (k_near, v_near)}, last=False
        )
        tables_far = tables(piece(pos_all, 1 - rank, rows))
        n1_far, start, half_up = lax.optimization_barrier((n1_far, start, half_up))
        up_all = gather(half_up)
        q_far, k_far, v_far = project(n1_far, w_turned, *tables_far)
        mixed_far, log_far = attend_half(
            "far_all", ends, index, q_far, True, {0: (k_near, v_near), 1: (k_far, v_far)}
        )
        mixed_in = across(mixed_far)
        mixed_near, log_near = attend_half(
            "near_far", ends, index, q_near, False, {1: (k_far, v_far)}, carry=start
        )
        mixed_in, mixed_near, half_down = lax.optimization_barrier(
            (mixed_in, mixed_near, half_down)
        )
        down_all = gather(half_down)
        h1, n2 = upper(h0, mixed_near, mixed_in, w_out, out_far, b_out, gain_ffn)
        branch, grad_n2, sums, bias_near = ffn(
            "ffn_near", n2, grad_low, w_up.reshape(2, 1, width // 2, hidden),
            b_up.reshape(1, 1, hidden), w_down.reshape(2, 1, hidden // 2, width),
            extra, parts, zero, index,
        )
        branch, grad_n2, sums, grad_bias = ffn(
            "ffn_far", n2, grad_low, up_all, bias_both, down_all, extra, parts, other, other,
            before=(branch, grad_n2, sums),
        )
        grad_bias = order(bias_near, grad_bias, 0)
        grad_h1, grad_h1_low, grad_near, grad_sent, early = middle(
            h1, grad_n2, cotangent, valid_here, gain_ffn, w_out, out_far
        )
        grad_far = across(grad_sent)
        sums = out_back(
            (mixed_near, mixed_in), grad_h1_low, sums, extra, jnp.concatenate([index, other])
        )
    else:
        joined = jnp.concatenate([inputs, skip_in], axis=1)
        h0 = dot(joined, w_concat) + b_concat
        scale_one = lax.rsqrt(jnp.mean(h0 * h0, axis=-1, keepdims=True) + EPS)
        n1 = (h0 * scale_one * gain_attn).astype(BF)
        n1_all = lax.all_gather(n1, "mp", axis=0, tiled=True)
        bias_all = lax.all_gather(b_up, "mp", axis=0).reshape(parts, 1, -1)
        w_out_all = lax.all_gather(w_out, "mp", axis=0, tiled=True)
        up_all, down_all = gather(half_up), gather(half_down)
        cosine, sine = tables(pos_all)
        query, keys, values = project(n1_all, w_turned, cosine, sine)
        mixed, logsum = attend(ends, zero, query, keys, values, 1)
        mixed_rows = lax.all_to_all(mixed, "mp", 1, 0, tiled=True)
        h1 = h0 + dot_tn(mixed_rows, w_out_all) + b_out
        scale_two = lax.rsqrt(jnp.mean(h1 * h1, axis=-1, keepdims=True) + EPS)
        n2 = (h1 * scale_two * gain_ffn).astype(BF)
        every = jnp.arange(parts, dtype=jnp.int32)
        branch, grad_n2, sums, grad_bias = ffn(
            "ffn", n2, grad_low, up_all, bias_all, down_all, extra, parts, every, every
        )
        output = valid_here * (h1 + branch + b_down)
        grad_h1, grad_gain_ffn = norm_back(grad_n2, h1, scale_two, gain_ffn)
        grad_h1 = grad_h1 + grad_rows
        grad_h1_low = grad_h1.astype(BF)
        grad_mixed = lax.all_to_all(
            dot_nt(w_out_all, grad_h1_low).astype(BF), "mp", 0, 1, tiled=True
        )
        grad_out = dot(mixed_rows, grad_h1_low).astype(BF)
        grad_out = grad_out.reshape(parts, 2, extra, width).transpose(1, 0, 2, 3)
        sums = lax.dynamic_update_slice(sums, grad_out, (0, 0, hidden, 0))
        early = jnp.stack([jnp.sum(grad_rows, 0), grad_gain_ffn, jnp.sum(grad_h1, 0)])
    def unpack_all(own):
        sibling = lax.ppermute(own, "core", [(0, 1), (1, 0)])
        up, down = unpack(core.reshape(1), own, sibling, hidden)
        first, second = own[hidden:].astype(F32), sibling[hidden:].astype(F32)
        out = jnp.where(
            core == 0, jnp.concatenate([first, second]), jnp.concatenate([second, first])
        )
        return up, down, out

    part = lax.psum_scatter(
        sums.reshape((2 * parts,) + sums.shape[2:]), ("core", "mp"), scatter_dimension=0, tiled=True
    )[0]
    summed = lax.psum(part, "dpo")
    if paired:
        near = (q_near, k_near, v_near, grad_near, mixed_near, log_near) + tables_near
        far = (q_far, k_far, v_far, grad_far, mixed_far, log_far) + tables_far
        heads = each // HEAD_DIM
        back = functools.partial(half_back, ends=ends, rank=index)
        both = (near, far)
        middle_head = heads // 2
        opening = back("back_near0", sides=(near,), first=0, count=middle_head, finish=False)[0]
        written, at = (), 0
        quarter = middle_head // 4
        for i, count in enumerate((middle_head - quarter, quarter)):
            written = back(
                f"back_first{i}", sides=both, first=at, count=count, finish=True,
                partial=opening, written=written, after=part if i else None,
            )
            at += count
        back_far, back_near = written
        back_far, partial = back(
            "back_second", sides=both, first=at, count=heads - at, finish=False,
            written=(back_far, None),
        )
        back_far = back_far.reshape(3 * each, rows)
        grad_far_rows = dot_tn(back_far, w_turned).astype(BF)
        sent = across(grad_far_rows)
        back_near = back(
            "back_near1", sides=(near,), first=middle_head, count=heads - middle_head, finish=True,
            partial=partial, written=(back_near,), after=grad_far_rows,
        )[0].reshape(3 * each, rows)
        pairs = [(n1, back_near, 0), (n1_far, back_far, 0)]
        grad_qkv, summed = project_back(pairs, summed)
        output = result(h1, branch, valid_here, b_down, grad_qkv)
        grad_h0_low, late = leave(
            back_near, w_turned, sent, h0, grad_h1, gain_attn, (output,)
        )
    else:
        back = attend_back(ends, query, keys, values, grad_mixed, mixed, logsum, cosine, sine)
        grad_n1 = dot_tn(back, w_turned).astype(BF)
        grad_n1 = lax.psum_scatter(grad_n1, "mp", scatter_dimension=0, tiled=True).astype(F32)
        grad_qkv, summed = project_back([(n1_all, back, 0)], summed)
        grad_h0, grad_gain_attn = norm_back(grad_n1, h0, scale_one, gain_attn)
        grad_h0_low = (grad_h0 + grad_h1).astype(BF)
        late = jnp.stack([jnp.sum(grad_h0_low.astype(F32), axis=0), grad_gain_attn])
    grad_up, grad_down, grad_out = unpack_all(summed)
    grad_w_concat = concat_back(inputs, skip_in, grad_h0_low)
    small = jnp.concatenate([early, late, grad_bias.reshape(-1, width)])
    small = jnp.pad(small, ((0, -small.shape[0] % 8), (0, 0)))
    if paired and lax.axis_size("dpo") == 8:
        tail, small = sum_all(grad_w_concat, small)
        grad_qkv = lax.psum(grad_qkv, dp)
    else:
        tail, small = lax.psum((grad_w_concat, small), dp + ("mp",))
        grad_qkv = lax.psum(grad_qkv, dp)
    grad_inputs, grad_skip, tail = join_back(grad_h0_low, w_concat, tail)
    grad_query, grad_key, grad_value = turn(grad_qkv, 3)
    return (
        output,
        grad_inputs,
        grad_skip,
        tail,
        small[3],
        small[4],
        grad_query,
        grad_key,
        grad_value,
        grad_out,
        small[2],
        small[1],
        grad_up,
        piece(small[5 : 5 + parts * hidden // width].reshape(-1), rank, hidden),
        grad_down,
        small[0],
    )


def solution(mesh):
    dp, mp = mesh.shape["dp"], mesh.shape["mp"]
    mesh = Mesh(mesh.devices.reshape(dp // 2, 2, mp), ("dpo", "core", "mp"))
    rows = P(("dpo", "core", "mp"), None)
    columns = P(None, "mp")
    upright = P("mp", None)
    return jax.shard_map(
        body,
        mesh=mesh,
        in_specs=(
            rows, rows, rows, P(("dpo", "core"), None), P(), P(), P(), columns, columns, columns,
            upright, P(), P(), columns, P("mp"), upright, P(),
        ),
        out_specs=(
            rows, rows, rows, P(), P(), P(), columns, columns, columns,
            upright, P(), P(), columns, P("mp"), upright, P(),
        ),
        check_vma=False,
    )
```
